128 devices in a mesh: dp: 32 (over y, z, x_hi), tensor: 4 (over x_lo, core).
Axes of the slice: x: 4 (x_hi: 2, x_lo: 2; x = x_hi * 2 + x_lo), y: 4, z: 4, core: 2. Of those that a mesh axis runs over, the one named last changes fastest.
Arguments:
- tokens: bfloat16 [65536, 512], P(('dp', 'tensor')), may hold values from -6 to 6
- cotangent: bfloat16 [65536, 512], P(('dp', 'tensor')), may hold values from -6 to 6
- doc_lengths: int32 [32, 9], P('dp'), may hold values from 0 to 2048, as said below
- group_slot: int32 [128, 512], P(('dp', 'tensor')), may hold values from 0 to 511, each once within a row
- norm1_gain: float32 [512], replicated, may hold values from 0.5 to 1.5
- qkv_weight: bfloat16 [512, 1536], P(None, 'tensor'), may hold values from -0.25 to 0.25
- out_weight: bfloat16 [512, 512], P('tensor'), may hold values from -4 to 4
- norm2_gain: float32 [512], replicated, may hold values from 0.5 to 1.5
- router_weight: bfloat16 [512, 8], replicated, may hold values from -0.1875 to 0.1875
- expert_in: bfloat16 [8, 512, 2048], P('tensor'), may hold values from -1.5 to 1.5
- expert_out: bfloat16 [8, 2048, 512], P('tensor'), may hold values from -2 to 2
Outputs:
- block_out: bfloat16 [65536, 512], P(('dp', 'tensor'))
- grad_tokens: bfloat16 [65536, 512], P(('dp', 'tensor'))
- grad_norm1: float32 [512], replicated
- grad_qkv: float32 [512, 1536], P(None, 'tensor')
- grad_out: float32 [512, 512], P('tensor')
- grad_norm2: float32 [512], replicated
- grad_router: float32 [512, 8], replicated
- grad_expert_in: float32 [8, 512, 2048], P('tensor')
- grad_expert_out: float32 [8, 2048, 512], P('tensor')
The draws below stay inside these ranges and needn't reach their ends.
Inputs may be any that keep to these rules, and one draw needn't show every extreme that they name: `doc_lengths`: each row's entries sum to 2048; a zero is an unused slot; documents fill the row in slot order.
All inputs are finite; a program needn't handle non-finite values.
Results may differ from the reference program's by a relative error of at most 0.035.
Values may be sent and summed in bfloat16 or wider, within the bound.
A program may use at most 128 MiB of HBM per device.

```python
import jax
import jax.numpy as jnp
from jax import lax

D = 512
HEADS = 8
FF = 2048
EXPERTS = 8
GROUP = 32
TOK_DEV = 512
LENGTH = 2048
TOKENS = 65536
N_DP = 32
N_TENSOR = 4


def draw_doc_lengths(key, part):
    key = jax.random.fold_in(key, 11)
    subkeys = jax.random.split(key, 5)
    longest = max(TOK_DEV // 8, 2)
    chosen_row = jax.random.randint(subkeys[4], (), 0, N_DP)
    row_index = jnp.arange(N_DP, dtype=jnp.int32)[:, None]
    lead_count = jax.random.randint(subkeys[0], (N_DP, 1), 0, 4)
    trail_count = jax.random.randint(subkeys[1], (N_DP, 1), 0, 4)
    lead_count = jnp.where(row_index == chosen_row, 0, lead_count)
    trail_count = jnp.where(row_index == chosen_row, 0, trail_count)
    slot_index = jnp.arange(4, dtype=jnp.int32)[None, :]
    leading = jnp.where(slot_index < lead_count, jax.random.randint(subkeys[2], (N_DP, 4), 1, longest), 0)
    trailing = jnp.where(slot_index < trail_count, jax.random.randint(subkeys[3], (N_DP, 4), 1, longest), 0)
    middle = LENGTH - jnp.sum(leading, axis=1, keepdims=True) - jnp.sum(trailing, axis=1, keepdims=True)
    return jnp.concatenate([leading, middle, trailing], axis=1).astype(jnp.int32)


def block_scale(rng, extent, shards, smallest, top_value):
    def one(axis_at, parts):
        steps = jax.random.uniform(jax.random.fold_in(jax.random.fold_in(rng, 6), axis_at), (parts,), jnp.float32, smallest / len(shards), top_value / len(shards))
        return jnp.repeat(jnp.exp(steps), extent[axis_at] // parts).reshape((-1,) + (1,) * (len(extent) - axis_at - 1))

    gain = one(*shards[0])
    for cut in shards[1:]:
        gain = gain * one(*cut)
    return gain


def noise(own_key, dims, width, limit, cuts=(), kind=jnp.bfloat16):
    array = jax.random.normal(own_key, dims, jnp.float32) * width
    if len(cuts) > 0:
        array = block_scale(own_key, dims, cuts, -0.22, 0.18) * array
    return jnp.clip(array, min=-limit, max=limit).astype(kind)


def setup_inputs(seed: int = 0) -> dict:
    keys = jax.random.split(jax.random.key(seed), 12)
    tokens = noise(keys[0], (TOKENS, D), 1.0, 6.0, ((0, 128),))
    cotangent = noise(keys[1], (TOKENS, D), 1.0, 6.0, ((0, 128),))
    doc_lengths = draw_doc_lengths(jax.random.fold_in(keys[11], 71), 0)
    group_slot = jax.vmap(lambda own: jax.random.permutation(own, TOK_DEV))(jax.random.split(keys[3], (N_DP * N_TENSOR))).reshape((N_DP * N_TENSOR, TOK_DEV)).astype(jnp.int32)
    norm1_gain = jnp.clip(1.0 + 0.1 * jax.random.normal(keys[4], (D,), jnp.float32), 0.5, 1.5)
    qkv_weight = noise(keys[5], (D, 3 * D), D ** -0.5, 0.25, ((1, 4),))
    out_weight = noise(keys[6], (D, D), (max(D // 256, 1)) ** -0.5, 4.0, ((0, 4),))
    norm2_gain = jnp.clip(1.0 + 0.1 * jax.random.normal(keys[7], (D,), jnp.float32), 0.5, 1.5)
    router_weight = noise(keys[8], (D, EXPERTS), (2 * D) ** -0.5, 0.1875)
    expert_in = noise(keys[9], (EXPERTS, D, FF), (max(D // 32, 1)) ** -0.5, 1.5, ((0, 4),))
    expert_out = noise(keys[10], (EXPERTS, FF, D), (max(FF // 256, 1)) ** -0.5, 2.0, ((0, 4),))
    return dict(tokens=tokens, cotangent=cotangent, doc_lengths=doc_lengths, group_slot=group_slot, norm1_gain=norm1_gain, qkv_weight=qkv_weight, out_weight=out_weight, norm2_gain=norm2_gain, router_weight=router_weight, expert_in=expert_in, expert_out=expert_out)


@jax.custom_vjp
def low(v):
    return lax.optimization_barrier(v.astype(jnp.bfloat16)).astype(jnp.float32)

@jax.custom_vjp
def low_back(v):
    return v

def low_keep(v):
    return (low(v), None)

def low_pass(kept, grad):
    return (grad,)

def back_keep(v):
    return (v, None)

def back_low(kept, grad):
    return (low(grad),)
low.defvjp(low_keep, low_pass)
low_back.defvjp(back_keep, back_low)
eps = 1e-06
highest = lax.Precision.HIGHEST

def normalize(values):
    return values * lax.rsqrt(lax.optimization_barrier(jnp.mean(values * values, axis=-1, keepdims=True)) + eps)

def attend_row(row_tokens, row_lengths, gain_one, qkv_matrix, out_matrix):
    length_all = row_tokens.shape[0]
    head_size = D // HEADS
    hidden_one = low(normalize(row_tokens) * gain_one)
    projected = low(low_back(jnp.dot(hidden_one, qkv_matrix, precision=highest)))
    split_heads = projected.reshape(length_all, HEADS, 3, head_size)
    queries = split_heads[:, :, 0]
    all_keys = split_heads[:, :, 1]
    all_values = split_heads[:, :, 2]
    places = jnp.arange(length_all, dtype=jnp.int32)
    bounds = jnp.cumsum(row_lengths).astype(jnp.int32)
    doc_ids = lax.optimization_barrier(jnp.sum((places[:, None] >= bounds[None, :]).astype(jnp.int32), axis=1))
    allowed = (doc_ids[:, None] == doc_ids[None, :]) & (places[None, :] <= places[:, None])
    scores = low_back(jnp.einsum('qhd,khd->hqk', queries, all_keys, precision=highest)) * head_size ** (-0.5)
    scores = jnp.where(allowed[None], scores, -1e+30)
    exponent = jnp.exp(scores - lax.optimization_barrier(jnp.max(scores, axis=-1, keepdims=True)))
    weights = exponent / lax.optimization_barrier(jnp.sum(exponent, axis=-1, keepdims=True))
    attended = jnp.einsum('hqk,khd->qhd', low(weights), all_values, precision=highest)
    attended = low(low_back(attended.reshape(length_all, D)))
    return low_back(jnp.dot(attended, out_matrix, precision=highest))

def forward(inputs, gain_one, qkv_matrix, out_matrix, gain_two, router_matrix, in_matrices, out_matrices, doc_lengths, group_slot):
    rows_in = inputs.reshape(N_DP, LENGTH, D)

    def row_attention(row_pair):
        return attend_row(row_pair[0], row_pair[1], gain_one, qkv_matrix, out_matrix)
    attn_part = lax.map(jax.checkpoint(row_attention), (rows_in, doc_lengths))
    residual_one = inputs + attn_part.reshape(TOKENS, D)
    hidden_two = low(low_back(normalize(residual_one) * gain_two))
    groups_dev = TOK_DEV // GROUP
    per_source = GROUP // N_DP
    blocks = hidden_two.reshape(N_DP * N_TENSOR, TOK_DEV, D)
    inverse_order = jnp.argsort(group_slot, axis=1).astype(jnp.int32)
    ordered = jnp.take_along_axis(blocks, inverse_order[:, :, None], axis=1)
    members = ordered.reshape(N_DP, N_TENSOR, N_DP, groups_dev, per_source, D)
    logits = low_back(jnp.einsum('ikjgsd,de->ikjgse', members, router_matrix, precision=highest))
    exponent = jnp.exp(logits - lax.optimization_barrier(jnp.max(logits, axis=(0, 4), keepdims=True)))
    mixing_low = low(exponent / lax.optimization_barrier(jnp.sum(exponent, axis=(0, 4), keepdims=True)))
    mixed_rows = low(low_back(jnp.einsum('ikjgse,ikjgsd->kjged', mixing_low, members, precision=highest)))
    pre_act = low_back(jnp.einsum('kjged,edf->kjgef', mixed_rows, in_matrices, precision=highest))
    activated = low(jax.nn.gelu(pre_act, approximate=True))
    produced = low(low_back(jnp.einsum('kjgef,efd->kjged', activated, out_matrices, precision=highest)))
    spread = jnp.einsum('ikjgse,kjged->ikjgsd', mixing_low, produced, precision=highest)
    spread = spread.reshape(N_DP * N_TENSOR, TOK_DEV, D)
    update = jnp.take_along_axis(spread, group_slot[:, :, None], axis=1).reshape(TOKENS, D)
    return residual_one + low(low_back(update))

def reference(tokens, cotangent, doc_lengths, group_slot, norm1_gain, qkv_weight, out_weight, norm2_gain, router_weight, expert_in, expert_out):

    def layer_apply(inputs, gain_one, qkv_matrix, out_matrix, gain_two, router_matrix, in_matrices, out_matrices):
        return forward(inputs, gain_one, qkv_matrix, out_matrix, gain_two, router_matrix, in_matrices, out_matrices, doc_lengths, group_slot)
    result, pullback = jax.vjp(layer_apply, tokens.astype(jnp.float32), norm1_gain.astype(jnp.float32), qkv_weight.astype(jnp.float32), out_weight.astype(jnp.float32), norm2_gain.astype(jnp.float32), router_weight.astype(jnp.float32), expert_in.astype(jnp.float32), expert_out.astype(jnp.float32))
    gradients = pullback(cotangent.astype(jnp.float32))
    return (result.astype(jnp.bfloat16), gradients[0].astype(jnp.bfloat16), gradients[1], gradients[2], gradients[3], gradients[4], gradients[5], gradients[6], gradients[7])
```

```python
from functools import partial

import jax
import jax.numpy as jnp
from jax import lax
from jax.experimental import pallas as pl
from jax.experimental.pallas import tpu as pltpu
from jax.sharding import PartitionSpec as P

D = 512
GROUP = 32
ROWS = 512
LENGTH = 2048
N_DP = 32
PER = ROWS // N_DP
CHUNKS = 4
MESH = pl.DeviceIdType.MESH
NN = (((1,), (0,)), ((), ()))
NT = (((1,), (1,)), ((), ()))
TN = (((0,), (0,)), ((), ()))
f32 = jnp.float32
bf16 = jnp.bfloat16
eps = 1e-06


def dot(a, b, dims=NN):
    return lax.dot_general(a, b, dims, preferred_element_type=f32)


def normalize(values):
    factor = lax.rsqrt(jnp.mean(values * values, axis=-1, keepdims=True) + eps)
    return (values * factor, factor)


def norm_back(grad_hidden, normed, factor, gain_row):
    grad_normed = grad_hidden * gain_row
    inner_sum = jnp.mean(grad_normed * normed, axis=-1, keepdims=True)
    return factor * (grad_normed - normed * inner_sum)


def remote(src, dst, send_sem, recv_sem, device):
    return pltpu.make_async_remote_copy(
        src_ref=src,
        dst_ref=dst,
        send_sem=send_sem,
        recv_sem=recv_sem,
        device_id=device,
        device_id_type=MESH,
    )


def document_starts(lengths, base, count):
    place = lax.broadcasted_iota(jnp.int32, (1, count), 1) + base
    bound = jnp.int32(0)
    first = jnp.zeros((1, count), jnp.int32)
    for slot in range(9):
        bound = bound + lengths[0, slot]
        first = jnp.where(bound <= place, bound, first)
    return place, first


def allowed_pairs(place, first, key_base, keys):
    key = lax.broadcasted_iota(jnp.int32, (keys, place.shape[1]), 0)
    return (key >= first - key_base) & (key <= place - key_base)


def attend_block(lengths, q2, k, v2t, base, rows):
    place, first = document_starts(lengths, base, rows)

    def step(index, carry):
        key_base = pl.multiple_of(index * rows, rows)
        allowed = allowed_pairs(place, first, key_base, rows)
        keys = k[pl.ds(key_base, rows), :]
        result = []
        for head in range(2):
            scores = jnp.where(allowed, dot(keys, q2[head, pl.ds(base, rows), :], NT), -1e30)
            maxima = jnp.max(scores, axis=0, keepdims=True)
            if carry is not None:
                maxima = jnp.maximum(carry[head][0], maxima)
            weights = jnp.exp(scores - maxima).astype(bf16)
            total = dot(v2t[head, :, pl.ds(key_base, rows)], weights)
            if carry is not None:
                total = carry[head][1] * jnp.exp(carry[head][0] - maxima) + total
            result.append((maxima, total))
        return tuple(result)

    blocks = base // rows
    carry = step(blocks, None)
    if blocks > 0:
        carry = lax.fori_loop(0, blocks, lambda i, c: step(blocks - 1 - i, c), carry)
    (max_a, sum_a), (max_b, sum_b) = carry
    norm_a, norm_b = sum_a[64:65], sum_b[0:1]
    attended = jnp.concatenate([sum_a[:64] / norm_a, sum_b[64:] / norm_b], axis=0)
    return attended.T.astype(bf16), max_a + jnp.log(norm_a), max_b + jnp.log(norm_b)


def dp_exchange_start(source, target, send_sems, recv_sems):
    me, t = lax.axis_index("dp"), lax.axis_index("tensor")
    mine = pl.ds(pl.multiple_of(me * PER, PER), PER)

    def send(k, carry):
        peer = (me + k) % N_DP
        remote(
            source.at[pl.ds(pl.multiple_of(peer * PER, PER), PER)],
            target.at[mine],
            send_sems.at[k],
            recv_sems.at[k],
            (peer, t),
        ).start()
        return carry

    lax.fori_loop(1, N_DP, send, 0)
    target[mine] = source[mine]


def dp_exchange_wait(source, target, send_sems, recv_sems):
    me, t = lax.axis_index("dp"), lax.axis_index("tensor")

    def wait(k, carry):
        sent = (me + k) % N_DP
        came = (me + N_DP - k) % N_DP
        remote(
            source.at[pl.ds(pl.multiple_of(sent * PER, PER), PER)],
            target.at[pl.ds(pl.multiple_of(came * PER, PER), PER)],
            send_sems.at[k],
            recv_sems.at[k],
            (sent, t),
        ).wait()
        return carry

    lax.fori_loop(1, N_DP, wait, 0)


def front_kernel(
    lengths,
    tokens,
    cotangent,
    slot,
    gain_one,
    qkv,
    out_w,
    gain_two,
    members,
    grad_update,
    residual,
    hidden,
    q2,
    k,
    v,
    k2t,
    lse,
    att_own,
    att_pos,
    out_all,
    perm,
    sorted_grad,
    sorted_hidden,
    v2t,
    hid_s,
    hid_r,
    out_s,
    out_r,
    att_s,
    att_r,
    grad_s,
    grad_r,
    mem_s,
    mem_r,
):
    me, t = lax.axis_index("dp"), lax.axis_index("tensor")
    sibling, cross, far = t + 1 - 2 * (t % 2), (t + 2) % 4, 3 - t
    barrier = pltpu.get_barrier_semaphore()
    for peer in (sibling, cross, far):
        pl.semaphore_signal(barrier, inc=1, device_id=(me, peer), device_id_type=MESH)

    def greet(i, carry):
        pl.semaphore_signal(barrier, inc=1, device_id=((me + i) % N_DP, t), device_id_type=MESH)
        return carry

    lax.fori_loop(1, N_DP, greet, 0)

    step = ROWS // CHUNKS
    for c in range(CHUNKS):
        values = tokens[c * step : (c + 1) * step, :].astype(f32)
        normed, _ = normalize(values)
        hidden[pl.ds(pl.multiple_of(t * ROWS + c * step, step), step), :] = (
            normed * gain_one[...]
        ).astype(bf16)
    out_all[t] = out_w[...]
    pl.semaphore_wait(barrier, N_DP + 2)

    def hidden_copy(kind, owner, c, device):
        rows = pl.ds(pl.multiple_of(owner * ROWS + c * step, step), step)
        return remote(
            hidden.at[rows], hidden.at[rows], hid_s.at[kind, c], hid_r.at[kind, c], (me, device)
        )

    for c in range(CHUNKS):
        hidden_copy(1, t, c, cross).start()
        hidden_copy(0, t, c, sibling).start()

    place = lax.broadcasted_iota(jnp.int32, (ROWS, ROWS), 0)
    perm[...] = jnp.where(place == slot[...], 1.0, 0.0).astype(bf16)
    sorted_grad[...] = dot(perm[...], cotangent[...]).astype(bf16)

    lane = lax.broadcasted_iota(jnp.int32, (D, 128), 1)
    part_a, part_b, part_c = (qkv[:, 128 * i : 128 * (i + 1)].astype(f32) for i in range(3))
    wq = jnp.where(lane < 64, part_a, part_b).astype(bf16)
    wk = pltpu.roll(jnp.where(lane < 64, part_c, part_a), 64, 1).astype(bf16)
    wv = jnp.where(lane < 64, part_b, part_c).astype(bf16)

    half = lax.broadcasted_iota(jnp.int32, (ROWS, 128), 1) < 64
    half_t = lax.broadcasted_iota(jnp.int32, (128, ROWS), 0) < 64

    def project(owner):
        rows = pl.ds(pl.multiple_of(owner * ROWS, ROWS), ROWS)
        block = hidden[rows, :]
        queries = dot(block, wq).astype(bf16).astype(f32) * 0.125
        q2[0, rows, :] = jnp.where(half, queries, 0.0).astype(bf16)
        q2[1, rows, :] = jnp.where(half, 0.0, queries).astype(bf16)
        keys = dot(block, wk)
        k[rows, :] = keys.astype(bf16)
        keys_t = keys.T
        k2t[0, :, rows] = jnp.where(half_t, keys_t, 0.0).astype(bf16)
        k2t[1, :, rows] = jnp.where(half_t, 0.0, keys_t).astype(bf16)
        values = dot(block, wv)
        v[rows, :] = values.astype(bf16)
        values_t = values.T
        v2t[0, :, rows] = jnp.where(half_t, values_t, 1.0).astype(bf16)
        v2t[1, :, rows] = jnp.where(half_t, 1.0, values_t).astype(bf16)

    project(t)
    for c in range(CHUNKS):
        hidden_copy(0, sibling, c, sibling).wait_recv()
    project(sibling)
    for c in range(CHUNKS):
        hidden_copy(1, cross, c, cross).wait_recv()
        hidden_copy(2, cross, c, sibling).start()
    project(cross)
    for c in range(CHUNKS):
        hidden_copy(2, far, c, sibling).wait_recv()
    project(far)

    def out_copy(i, device):
        return remote(out_all.at[t], out_all.at[t], out_s.at[i], out_r.at[i], (me, device))

    for i, peer in enumerate((sibling, cross, far)):
        out_copy(i, peer).start()
    dp_exchange_start(sorted_grad, grad_update, grad_s, grad_r)

    def att_copy(block, device):
        return remote(
            att_own.at[pl.ds(block * ROWS, ROWS)],
            att_pos.at[t],
            att_s.at[block],
            att_r.at[t],
            (me, device),
        )

    for block in range(4):
        rows = pl.ds(block * ROWS, ROWS)
        attended, lse_a, lse_b = attend_block(lengths, q2, k, v2t, block * ROWS, ROWS)
        att_own[rows, :] = attended
        lse[0:1, rows] = lse_a
        lse[1:2, rows] = lse_b

        @pl.when(t == block)
        def _():
            att_pos[t] = att_own[rows, :]

        @pl.when(t != block)
        def _():
            att_copy(block, block).start()

    for i, peer in enumerate((sibling, cross, far)):
        out_copy(i, peer).wait()
    for block in range(4):

        @pl.when(t != block)
        def _():
            att_copy(block, block).wait_send()

    for peer in (sibling, cross, far):
        remote(
            att_own.at[pl.ds(0, ROWS)], att_pos.at[peer], att_s.at[0], att_r.at[peer], (me, peer)
        ).wait_recv()

    update = dot(att_pos[0], out_all[0])
    for i in range(1, 4):
        update = update + dot(att_pos[i], out_all[i])
    residual[...] = tokens[...].astype(f32) + update
    normed_two, _ = normalize(residual[...])
    hidden_two = (normed_two * gain_two[...]).astype(bf16)
    sorted_hidden[...] = dot(perm[...], hidden_two).astype(bf16)
    dp_exchange_start(sorted_hidden, members, mem_s, mem_r)

    for c in range(CHUNKS):
        hidden_copy(0, t, c, sibling).wait_send()
        hidden_copy(1, t, c, cross).wait_send()
        hidden_copy(2, cross, c, sibling).wait_send()
    dp_exchange_wait(sorted_grad, grad_update, grad_s, grad_r)
    dp_exchange_wait(sorted_hidden, members, mem_s, mem_r)


def front(lengths, tokens, cotangent, slot, gain_one, qkv, out_w, gain_two):
    sds = jax.ShapeDtypeStruct
    vmem = pl.BlockSpec(memory_space=pltpu.VMEM)
    dma = pltpu.SemaphoreType.DMA
    return pl.pallas_call(
        front_kernel,
        name="front",
        out_shape=(
            sds((ROWS, D), bf16),
            sds((ROWS, D), bf16),
            sds((ROWS, D), f32),
            sds((LENGTH, D), bf16),
            sds((2, LENGTH, 128), bf16),
            sds((LENGTH, 128), bf16),
            sds((LENGTH, 128), bf16),
            sds((2, 128, LENGTH), bf16),
            sds((2, LENGTH), f32),
            sds((LENGTH, 128), bf16),
            sds((4, ROWS, 128), bf16),
            sds((4, 128, D), bf16),
            sds((ROWS, ROWS), bf16),
        ),
        in_specs=[pl.BlockSpec(memory_space=pltpu.SMEM)] + [vmem] * 7,
        out_specs=[vmem] * 13,
        scratch_shapes=[
            pltpu.VMEM((ROWS, D), bf16),
            pltpu.VMEM((ROWS, D), bf16),
            pltpu.VMEM((2, 128, LENGTH), bf16),
            dma((3, CHUNKS)),
            dma((3, CHUNKS)),
            dma((3,)),
            dma((3,)),
            dma((4,)),
            dma((4,)),
            dma((N_DP,)),
            dma((N_DP,)),
            dma((N_DP,)),
            dma((N_DP,)),
        ],
        compiler_params=pltpu.CompilerParams(
            collective_id=0, has_side_effects=True, vmem_limit_bytes=56 * 2**20
        ),
    )(lengths, tokens, cotangent, slot, gain_one, qkv, out_w, gain_two)


def back_kernel(lengths, q2, k, k2t, v, do2, delta, lse, dq_t, dk, dv):
    rows = 512
    blocks = LENGTH // rows
    for block in reversed(range(blocks)):
        base = block * rows
        here = pl.ds(base, rows)
        place, first = document_starts(lengths, base, rows)

        def step(index, grad_q):
            key_base = pl.multiple_of(index * rows, rows)
            there = pl.ds(key_base, rows)
            allowed = allowed_pairs(place, first, key_base, rows)
            keys, values = k[there, :], v[there, :]
            grad_v, grad_k = None, None
            for head in range(2):
                queries, grads = q2[head, here, :], do2[head, here, :]
                scores = dot(keys, queries, NT)
                shifted = jnp.where(allowed, scores - lse[head : head + 1, here], -1e30)
                weights = jnp.exp(shifted)
                grad_w = dot(values, grads, NT)
                grad_s = (weights * (grad_w - delta[head : head + 1, here])).astype(bf16)
                part = dot(weights.astype(bf16), grads)
                grad_v = part if grad_v is None else grad_v + part
                part = dot(grad_s, queries)
                grad_k = part if grad_k is None else grad_k + part
                grad_q = grad_q + dot(k2t[head, :, there], grad_s)
            if block == blocks - 1:
                dk[there, :] = grad_k
                dv[there, :] = grad_v
            else:
                dk[there, :] += grad_k
                dv[there, :] += grad_v
            return grad_q

        grad_q = lax.fori_loop(0, block + 1, step, jnp.zeros((128, rows), f32))
        dq_t[:, here] = grad_q * 0.125


def back(*args):
    sds = jax.ShapeDtypeStruct
    vmem = pl.BlockSpec(memory_space=pltpu.VMEM)
    return pl.pallas_call(
        back_kernel,
        name="attention_back",
        out_shape=(sds((128, LENGTH), f32), sds((LENGTH, 128), f32), sds((LENGTH, 128), f32)),
        in_specs=[pl.BlockSpec(memory_space=pltpu.SMEM)] + [vmem] * 7,
        out_specs=[vmem] * 3,
        compiler_params=pltpu.CompilerParams(vmem_limit_bytes=56 * 2**20),
    )(*args)


def local(
    tokens,
    cotangent,
    doc_lengths,
    group_slot,
    norm1_gain,
    qkv_weight,
    out_weight,
    norm2_gain,
    router_weight,
    expert_in,
    expert_out,
):
    data_ranks = N_DP
    tensor_size = 4
    tok_rows = ROWS
    groups_here = PER
    per_source = 1
    experts_here = expert_in.shape[0]
    experts_all = router_weight.shape[1]
    contract_first = TN
    contract_last = NT
    (
        arrived_hidden,
        arrived_grad,
        residual_one,
        rows_one,
        q2,
        k,
        v,
        k2t,
        lse,
        att_own,
        att_pos,
        out_all,
        perm,
    ) = front(
        doc_lengths,
        tokens,
        cotangent,
        group_slot,
        norm1_gain[None],
        qkv_weight,
        out_weight,
        norm2_gain[None],
    )
    inputs = tokens.astype(f32)
    normed_one, scale_one = normalize(inputs)
    normed_two, scale_two = normalize(residual_one)
    slot_row = group_slot[0]
    members = arrived_hidden.reshape(data_ranks, groups_here, per_source, D)
    grad_update = arrived_grad.reshape(data_ranks, groups_here, per_source, D)
    logits = jnp.einsum("ngsd,de->ngse", members, router_weight, preferred_element_type=jnp.float32)
    exponent = jnp.exp(logits - jnp.max(logits, axis=(0, 2), keepdims=True))
    mixing = exponent / jnp.sum(exponent, axis=(0, 2), keepdims=True)
    mixing_low = mixing.astype(jnp.bfloat16)
    mixed_rows = jnp.einsum(
        "ngse,ngsd->egd", mixing_low, members, preferred_element_type=jnp.float32
    ).astype(jnp.bfloat16)
    expert_rows = lax.all_to_all(mixed_rows, "tensor", split_axis=0, concat_axis=0, tiled=True)
    expert_rows = expert_rows.reshape(tensor_size, experts_here, groups_here, D)
    pre_act = jnp.einsum(
        "tegd,edf->tegf", expert_rows, expert_in, preferred_element_type=jnp.float32
    )
    activated = jax.nn.gelu(pre_act, approximate=True).astype(jnp.bfloat16)
    produced = jnp.einsum(
        "tegf,efd->tegd", activated, expert_out, preferred_element_type=jnp.float32
    ).astype(jnp.bfloat16)
    returned = lax.all_to_all(
        produced.reshape(experts_all, groups_here, D),
        "tensor",
        split_axis=0,
        concat_axis=0,
        tiled=True,
    )
    spread = jnp.einsum("ngse,egd->ngsd", mixing_low, returned, preferred_element_type=jnp.float32)
    back_rows = lax.all_to_all(
        spread.reshape(tok_rows, D).astype(jnp.bfloat16),
        "dp",
        split_axis=0,
        concat_axis=0,
        tiled=True,
    )
    block_out = (residual_one + back_rows[slot_row].astype(jnp.float32)).astype(jnp.bfloat16)
    grad_produced = jnp.einsum(
        "ngse,ngsd->egd", mixing_low, grad_update, preferred_element_type=jnp.float32
    ).astype(jnp.bfloat16)
    grad_mixing = jnp.einsum(
        "ngsd,egd->ngse", grad_update, returned, preferred_element_type=jnp.float32
    )
    expert_grads = lax.all_to_all(grad_produced, "tensor", split_axis=0, concat_axis=0, tiled=True)
    expert_grads = expert_grads.reshape(tensor_size, experts_here, groups_here, D)
    grad_act = jnp.einsum(
        "tegd,efd->tegf", expert_grads, expert_out, preferred_element_type=jnp.float32
    )
    gelu_value, gelu_back = jax.vjp(partial(jax.nn.gelu, approximate=True), pre_act)
    grad_pre = gelu_back(grad_act)[0].astype(jnp.bfloat16)
    grad_mixed = jnp.einsum(
        "tegf,edf->tegd", grad_pre, expert_in, preferred_element_type=jnp.float32
    ).astype(jnp.bfloat16)
    local_in = jnp.einsum(
        "tegd,tegf->edf", expert_rows, grad_pre, preferred_element_type=jnp.float32
    )
    local_out = jnp.einsum(
        "tegf,tegd->efd", activated, expert_grads, preferred_element_type=jnp.float32
    )
    grad_mixed_all = lax.all_to_all(
        grad_mixed.reshape(experts_all, groups_here, D),
        "tensor",
        split_axis=0,
        concat_axis=0,
        tiled=True,
    )
    grad_mixing = grad_mixing + jnp.einsum(
        "egd,ngsd->ngse", grad_mixed_all, members, preferred_element_type=jnp.float32
    )
    grad_member = jnp.einsum(
        "ngse,egd->ngsd", mixing_low, grad_mixed_all, preferred_element_type=jnp.float32
    )
    inner_sum = jnp.sum(mixing * grad_mixing, axis=(0, 2), keepdims=True)
    grad_logits = (mixing * (grad_mixing - inner_sum)).astype(jnp.bfloat16)
    router_part = jnp.einsum(
        "ngsd,ngse->de", members, grad_logits, preferred_element_type=jnp.float32
    )
    grad_member = grad_member + jnp.einsum(
        "ngse,de->ngsd", grad_logits, router_weight, preferred_element_type=jnp.float32
    )
    grad_sorted = lax.all_to_all(
        grad_member.reshape(tok_rows, D).astype(jnp.bfloat16),
        "dp",
        split_axis=0,
        concat_axis=0,
        tiled=True,
    )
    grad_hidden_two = grad_sorted[slot_row].astype(jnp.float32)
    gain_two_part = jnp.sum(grad_hidden_two * normed_two, axis=0)
    grad_residual = cotangent.astype(jnp.float32) + norm_back(
        grad_hidden_two, normed_two, scale_two, norm2_gain
    )
    grad_rows = lax.all_gather(grad_residual.astype(jnp.bfloat16), "tensor", axis=0, tiled=True)
    grad_attn_out = lax.dot_general(
        att_own, grad_rows, contract_first, preferred_element_type=jnp.float32
    )
    grad_attended = lax.dot_general(
        grad_rows, out_weight, contract_last, preferred_element_type=jnp.float32
    )
    grad_attended = grad_attended.astype(jnp.bfloat16)
    first_half = (jnp.arange(128) < 64)[None]
    do2 = jnp.stack((jnp.where(first_half, grad_attended, 0), jnp.where(first_half, 0, grad_attended)))
    delta = jnp.sum(
        (grad_attended.astype(f32) * att_own.astype(f32)).reshape(LENGTH, 2, 64), axis=-1
    ).T
    dq_t, dk, dv = back(doc_lengths, q2, k, k2t, v, do2, delta, lse)
    heads = lambda x: x.reshape(LENGTH, 2, 64)
    grad_projected = jnp.stack((heads(dq_t.T), heads(dk), heads(dv)), axis=2)
    grad_projected = grad_projected.reshape(LENGTH, 384).astype(jnp.bfloat16)
    grad_qkv_part = lax.dot_general(
        rows_one, grad_projected, contract_first, preferred_element_type=jnp.float32
    )
    grad_hidden_one = lax.psum_scatter(
        lax.dot_general(
            grad_projected, qkv_weight, contract_last, preferred_element_type=jnp.float32
        ).astype(jnp.bfloat16),
        "tensor",
        scatter_dimension=0,
        tiled=True,
    ).astype(jnp.float32)
    gain_one_part = jnp.sum(grad_hidden_one * normed_one, axis=0)
    grad_tokens = (
        grad_residual + norm_back(grad_hidden_one, normed_one, scale_one, norm1_gain)
    ).astype(jnp.bfloat16)
    grad_norm1, grad_norm2, grad_router = lax.psum(
        (gain_one_part, gain_two_part, router_part), ("dp", "tensor")
    )
    weight_terms = (grad_qkv_part, grad_attn_out, local_in, local_out)
    summed = tuple(lax.psum(w.astype(bf16), "dp").astype(f32) for w in weight_terms)
    return (
        block_out,
        grad_tokens,
        grad_norm1,
        summed[0],
        summed[1],
        grad_norm2,
        grad_router,
        summed[2],
        summed[3],
    )


def solution(mesh):
    in_specs = (
        P(("dp", "tensor"), None),
        P(("dp", "tensor"), None),
        P("dp", None),
        P(("dp", "tensor"), None),
        P(),
        P(None, "tensor"),
        P("tensor", None),
        P(),
        P(),
        P("tensor", None, None),
        P("tensor", None, None),
    )
    out_specs = (
        P(("dp", "tensor"), None),
        P(("dp", "tensor"), None),
        P(),
        P(None, "tensor"),
        P("tensor", None),
        P(),
        P(),
        P("tensor", None, None),
        P("tensor", None, None),
    )
    return jax.shard_map(local, mesh=mesh, in_specs=in_specs, out_specs=out_specs, check_vma=False)
```

```python
from functools import partial

import jax
import jax.numpy as jnp
from jax import lax
from jax.experimental import pallas as pl
from jax.experimental.pallas import tpu as pltpu
from jax.sharding import PartitionSpec as P

D = 512
GROUP = 32
ROWS = 512
LENGTH = 2048
N_DP = 32
PER = ROWS // N_DP
CHUNKS = 4
MESH = pl.DeviceIdType.MESH
NN = (((1,), (0,)), ((), ()))
NT = (((1,), (1,)), ((), ()))
TN = (((0,), (0,)), ((), ()))
f32 = jnp.float32
bf16 = jnp.bfloat16
eps = 1e-06


def dot(a, b, dims=NN):
    return lax.dot_general(a, b, dims, preferred_element_type=f32)


def normalize(values):
    factor = lax.rsqrt(jnp.mean(values * values, axis=-1, keepdims=True) + eps)
    return (values * factor, factor)


def norm_back(grad_hidden, normed, factor, gain_row):
    grad_normed = grad_hidden * gain_row
    inner_sum = jnp.mean(grad_normed * normed, axis=-1, keepdims=True)
    return factor * (grad_normed - normed * inner_sum)


def remote(src, dst, send_sem, recv_sem, device):
    return pltpu.make_async_remote_copy(
        src_ref=src,
        dst_ref=dst,
        send_sem=send_sem,
        recv_sem=recv_sem,
        device_id=device,
        device_id_type=MESH,
    )


def document_starts(lengths, base, count):
    place = lax.broadcasted_iota(jnp.int32, (1, count), 1) + base
    bound = jnp.int32(0)
    first = jnp.zeros((1, count), jnp.int32)
    for slot in range(9):
        bound = bound + lengths[0, slot]
        first = jnp.where(bound <= place, bound, first)
    return place, first


def allowed_pairs(place, first, key_base, keys):
    key = lax.broadcasted_iota(jnp.int32, (keys, place.shape[1]), 0)
    return (key >= first - key_base) & (key <= place - key_base)


def attend_block(lengths, q2, k, v2t, base, rows):
    place, first = document_starts(lengths, base, rows)

    def step(index, carry):
        key_base = pl.multiple_of(index * rows, rows)
        allowed = allowed_pairs(place, first, key_base, rows)
        keys = k[pl.ds(key_base, rows), :]
        result = []
        for head in range(2):
            scores = jnp.where(allowed, dot(keys, q2[head, pl.ds(base, rows), :], NT), -1e30)
            maxima = jnp.max(scores, axis=0, keepdims=True)
            if carry is not None:
                maxima = jnp.maximum(carry[head][0], maxima)
            weights = jnp.exp(scores - maxima).astype(bf16)
            total = dot(v2t[head, :, pl.ds(key_base, rows)], weights)
            if carry is not None:
                total = carry[head][1] * jnp.exp(carry[head][0] - maxima) + total
            result.append((maxima, total))
        return tuple(result)

    blocks = base // rows
    carry = step(blocks, None)
    if blocks > 0:
        carry = lax.fori_loop(0, blocks, lambda i, c: step(blocks - 1 - i, c), carry)
    (max_a, sum_a), (max_b, sum_b) = carry
    norm_a, norm_b = sum_a[64:65], sum_b[0:1]
    attended = jnp.concatenate([sum_a[:64] / norm_a, sum_b[64:] / norm_b], axis=0)
    return attended.T.astype(bf16), max_a + jnp.log(norm_a), max_b + jnp.log(norm_b)


def dp_exchange_start(source, target, send_sems, recv_sems):
    me, t = lax.axis_index("dp"), lax.axis_index("tensor")
    mine = pl.ds(pl.multiple_of(me * PER, PER), PER)

    def send(k, carry):
        peer = (me + k) % N_DP
        remote(
            source.at[pl.ds(pl.multiple_of(peer * PER, PER), PER)],
            target.at[mine],
            send_sems.at[k],
            recv_sems.at[k],
            (peer, t),
        ).start()
        return carry

    lax.fori_loop(1, N_DP, send, 0)
    target[mine] = source[mine]


def dp_exchange_wait(source, target, send_sems, recv_sems):
    me, t = lax.axis_index("dp"), lax.axis_index("tensor")

    def wait(k, carry):
        sent = (me + k) % N_DP
        came = (me + N_DP - k) % N_DP
        remote(
            source.at[pl.ds(pl.multiple_of(sent * PER, PER), PER)],
            target.at[pl.ds(pl.multiple_of(came * PER, PER), PER)],
            send_sems.at[k],
            recv_sems.at[k],
            (sent, t),
        ).wait()
        return carry

    lax.fori_loop(1, N_DP, wait, 0)


def front_kernel(
    lengths,
    tokens,
    cotangent,
    slot,
    gain_one,
    qkv,
    out_w,
    gain_two,
    members,
    grad_update,
    residual,
    hidden,
    q2,
    k,
    v,
    k2t,
    lse,
    att_own,
    att_pos,
    out_all,
    perm,
    sorted_grad,
    sorted_hidden,
    v2t,
    hid_s,
    hid_r,
    out_s,
    out_r,
    att_s,
    att_r,
    grad_s,
    grad_r,
    mem_s,
    mem_r,
):
    me, t = lax.axis_index("dp"), lax.axis_index("tensor")
    sibling, cross, far = t + 1 - 2 * (t % 2), (t + 2) % 4, 3 - t
    barrier = pltpu.get_barrier_semaphore()
    for peer in (sibling, cross, far):
        pl.semaphore_signal(barrier, inc=1, device_id=(me, peer), device_id_type=MESH)

    def greet(i, carry):
        pl.semaphore_signal(barrier, inc=1, device_id=((me + i) % N_DP, t), device_id_type=MESH)
        return carry

    lax.fori_loop(1, N_DP, greet, 0)

    step = ROWS // CHUNKS
    for c in range(CHUNKS):
        values = tokens[c * step : (c + 1) * step, :].astype(f32)
        normed, _ = normalize(values)
        hidden[pl.ds(pl.multiple_of(t * ROWS + c * step, step), step), :] = (
            normed * gain_one[...]
        ).astype(bf16)
    out_all[t] = out_w[...]
    pl.semaphore_wait(barrier, N_DP + 2)

    def hidden_copy(kind, owner, c, device):
        rows = pl.ds(pl.multiple_of(owner * ROWS + c * step, step), step)
        return remote(
            hidden.at[rows], hidden.at[rows], hid_s.at[kind, c], hid_r.at[kind, c], (me, device)
        )

    for c in range(CHUNKS):
        hidden_copy(1, t, c, cross).start()
        hidden_copy(0, t, c, sibling).start()

    place = lax.broadcasted_iota(jnp.int32, (ROWS, ROWS), 0)
    perm[...] = jnp.where(place == slot[...], 1.0, 0.0).astype(bf16)
    sorted_grad[...] = dot(perm[...], cotangent[...]).astype(bf16)

    lane = lax.broadcasted_iota(jnp.int32, (D, 128), 1)
    part_a, part_b, part_c = (qkv[:, 128 * i : 128 * (i + 1)].astype(f32) for i in range(3))
    wq = jnp.where(lane < 64, part_a, part_b).astype(bf16)
    wk = pltpu.roll(jnp.where(lane < 64, part_c, part_a), 64, 1).astype(bf16)
    wv = jnp.where(lane < 64, part_b, part_c).astype(bf16)

    half = lax.broadcasted_iota(jnp.int32, (ROWS, 128), 1) < 64
    half_t = lax.broadcasted_iota(jnp.int32, (128, ROWS), 0) < 64

    def project(owner):
        rows = pl.ds(pl.multiple_of(owner * ROWS, ROWS), ROWS)
        block = hidden[rows, :]
        queries = dot(block, wq).astype(bf16).astype(f32) * 0.125
        q2[0, rows, :] = jnp.where(half, queries, 0.0).astype(bf16)
        q2[1, rows, :] = jnp.where(half, 0.0, queries).astype(bf16)
        keys = dot(block, wk)
        k[rows, :] = keys.astype(bf16)
        keys_t = keys.T
        k2t[0, :, rows] = jnp.where(half_t, keys_t, 0.0).astype(bf16)
        k2t[1, :, rows] = jnp.where(half_t, 0.0, keys_t).astype(bf16)
        values = dot(block, wv)
        v[rows, :] = values.astype(bf16)
        values_t = values.T
        v2t[0, :, rows] = jnp.where(half_t, values_t, 1.0).astype(bf16)
        v2t[1, :, rows] = jnp.where(half_t, 1.0, values_t).astype(bf16)

    project(t)
    for c in range(CHUNKS):
        hidden_copy(0, sibling, c, sibling).wait_recv()
    project(sibling)
    for c in range(CHUNKS):
        hidden_copy(1, cross, c, cross).wait_recv()
        hidden_copy(2, cross, c, sibling).start()
    project(cross)
    for c in range(CHUNKS):
        hidden_copy(2, far, c, sibling).wait_recv()
    project(far)

    def out_copy(i, device):
        return remote(out_all.at[t], out_all.at[t], out_s.at[i], out_r.at[i], (me, device))

    for i, peer in enumerate((sibling, cross, far)):
        out_copy(i, peer).start()
    dp_exchange_start(sorted_grad, grad_update, grad_s, grad_r)

    def att_copy(block, device):
        return remote(
            att_own.at[pl.ds(block * ROWS, ROWS)],
            att_pos.at[t],
            att_s.at[block],
            att_r.at[t],
            (me, device),
        )

    for block in range(4):
        rows = pl.ds(block * ROWS, ROWS)
        attended, lse_a, lse_b = attend_block(lengths, q2, k, v2t, block * ROWS, ROWS)
        att_own[rows, :] = attended
        lse[0:1, rows] = lse_a
        lse[1:2, rows] = lse_b

        @pl.when(t == block)
        def _():
            att_pos[t] = att_own[rows, :]

        @pl.when(t != block)
        def _():
            att_copy(block, block).start()

    for i, peer in enumerate((sibling, cross, far)):
        out_copy(i, peer).wait()
    for block in range(4):

        @pl.when(t != block)
        def _():
            att_copy(block, block).wait_send()

    for peer in (sibling, cross, far):
        remote(
            att_own.at[pl.ds(0, ROWS)], att_pos.at[peer], att_s.at[0], att_r.at[peer], (me, peer)
        ).wait_recv()

    update = dot(att_pos[0], out_all[0])
    for i in range(1, 4):
        update = update + dot(att_pos[i], out_all[i])
    residual[...] = tokens[...].astype(f32) + update
    normed_two, _ = normalize(residual[...])
    hidden_two = (normed_two * gain_two[...]).astype(bf16)
    sorted_hidden[...] = dot(perm[...], hidden_two).astype(bf16)
    dp_exchange_start(sorted_hidden, members, mem_s, mem_r)

    for c in range(CHUNKS):
        hidden_copy(0, t, c, sibling).wait_send()
        hidden_copy(1, t, c, cross).wait_send()
        hidden_copy(2, cross, c, sibling).wait_send()
    dp_exchange_wait(sorted_grad, grad_update, grad_s, grad_r)
    dp_exchange_wait(sorted_hidden, members, mem_s, mem_r)


def front(lengths, tokens, cotangent, slot, gain_one, qkv, out_w, gain_two):
    sds = jax.ShapeDtypeStruct
    vmem = pl.BlockSpec(memory_space=pltpu.VMEM)
    dma = pltpu.SemaphoreType.DMA
    return pl.pallas_call(
        front_kernel,
        name="front",
        out_shape=(
            sds((ROWS, D), bf16),
            sds((ROWS, D), bf16),
            sds((ROWS, D), f32),
            sds((LENGTH, D), bf16),
            sds((2, LENGTH, 128), bf16),
            sds((LENGTH, 128), bf16),
            sds((LENGTH, 128), bf16),
            sds((2, 128, LENGTH), bf16),
            sds((2, LENGTH), f32),
            sds((LENGTH, 128), bf16),
            sds((4, ROWS, 128), bf16),
            sds((4, 128, D), bf16),
            sds((ROWS, ROWS), bf16),
        ),
        in_specs=[pl.BlockSpec(memory_space=pltpu.SMEM)] + [vmem] * 7,
        out_specs=[vmem] * 13,
        scratch_shapes=[
            pltpu.VMEM((ROWS, D), bf16),
            pltpu.VMEM((ROWS, D), bf16),
            pltpu.VMEM((2, 128, LENGTH), bf16),
            dma((3, CHUNKS)),
            dma((3, CHUNKS)),
            dma((3,)),
            dma((3,)),
            dma((4,)),
            dma((4,)),
            dma((N_DP,)),
            dma((N_DP,)),
            dma((N_DP,)),
            dma((N_DP,)),
        ],
        compiler_params=pltpu.CompilerParams(
            collective_id=0, has_side_effects=True, vmem_limit_bytes=56 * 2**20
        ),
    )(lengths, tokens, cotangent, slot, gain_one, qkv, out_w, gain_two)


class Exchange:
    def __init__(self, make, count):
        self.make, self.count = make, count

    def start(self):
        for i in range(self.count):
            self.make(i).start()

    def wait(self):
        for i in range(self.count):
            self.make(i).wait()


GELU_A = 0.7978845608028654
GELU_B = 0.044715


def tail_kernel(
    lengths,
    members,
    grad_update,
    router,
    expert_in,
    expert_out,
    tokens,
    cotangent,
    residual,
    gain_one,
    gain_two,
    qkv,
    hidden,
    q2,
    k,
    v,
    k2t,
    lse,
    att_own,
    att_pos,
    out_all,
    perm,
    block_out,
    grad_tokens,
    grad_small,
    grad_floats,
    grad_gain,
    grad_in,
    grad_out,
    w_in,
    w_out,
    mix,
    mix_send,
    rows_e,
    ret_send,
    ret,
    act_s,
    pre_s,
    xz,
    gz,
    ay,
    cy,
    o_in,
    o_out,
    s2_in,
    s2_out,
    s2_sum,
    s3_got,
    spread_s,
    spread_g,
    gm_s,
    gm_g,
    w_all,
    grad_res,
    gatt_s,
    gatt,
    outp_s,
    outp_g,
    do2,
    delta,
    dq_t,
    dk,
    dv,
    gp_own,
    gp_all,
    small_s,
    small_g,
    floats_s,
    floats_g,
    gain_s,
    gain_g,
    gain_all,
    send,
    recv,
    load,
):
    me, t = lax.axis_index("dp"), lax.axis_index("tensor")
    y, z, xh = me // 8, (me // 2) % 4, me % 2
    sibling, cross, far = t + 1 - 2 * (t % 2), (t + 2) % 4, 3 - t
    barrier = pltpu.get_barrier_semaphore()
    for peer in (sibling, cross, far):
        pl.semaphore_signal(barrier, inc=1, device_id=(me, peer), device_id_type=MESH)

    def greet(i, carry):
        pl.semaphore_signal(barrier, inc=1, device_id=((me + i) % N_DP, t), device_id_type=MESH)
        return carry

    lax.fori_loop(1, N_DP, greet, 0)
    load_in = pltpu.make_async_copy(expert_in, w_in, load.at[0])
    load_out = pltpu.make_async_copy(expert_out, w_out, load.at[1])
    load_in.start()
    load_out.start()

    taken = [0]

    def sems(count):
        first = taken[0]
        taken[0] += count
        return first

    def over_tensor(source, target):
        first = sems(3)

        def make(i):
            peer = (t + 1 + i) % 4
            return remote(
                source(peer), target(t), send.at[first + i], recv.at[first + i], (me, peer)
            )

        return Exchange(make, 3)

    def over_y(source, target):
        first = sems(3)

        def make(i):
            peer = (y + 1 + i) % 4
            return remote(
                source(peer),
                target(y),
                send.at[first + i],
                recv.at[first + i],
                (peer * 8 + z * 2 + xh, t),
            )

        return Exchange(make, 3)

    def over_z(source, target):
        first = sems(3)

        def make(i):
            peer = (z + 1 + i) % 4
            return remote(
                source(peer),
                target(z),
                send.at[first + i],
                recv.at[first + i],
                (y * 8 + peer * 2 + xh, t),
            )

        return Exchange(make, 3)

    def over_x(source, target):
        first = sems(1)

        def make(i):
            return remote(
                source, target, send.at[first], recv.at[first], (y * 8 + z * 2 + 1 - xh, t)
            )

        return Exchange(make, 1)

    class OverDp:
        def __init__(self, source, target):
            first = sems(N_DP)
            pairs = (send.at[pl.ds(first, N_DP)], recv.at[pl.ds(first, N_DP)])
            self.args = (source, target) + pairs

        def start(self):
            dp_exchange_start(*self.args)

        def wait(self):
            dp_exchange_wait(*self.args)

    def group_all(values, op):
        for shift in (16, 32, 64, 128, 256):
            values = op(values, pltpu.roll(values, shift, 1))
        return values

    logits = dot(router[...], members[...], NT)
    exponent = jnp.exp(logits - group_all(logits, jnp.maximum))
    mixing = exponent / group_all(exponent, jnp.add)
    lane = lax.broadcasted_iota(jnp.int32, (PER, ROWS), 1)
    own_group = lax.broadcasted_iota(jnp.int32, (PER, ROWS), 0) == lane % PER
    mix[...] = jnp.concatenate(
        [jnp.where(own_group, mixing[e : e + 1], 0.0) for e in range(8)], axis=0
    ).astype(bf16)
    mix_send[0] = dot(mix[...], members[...]).astype(bf16).reshape(8, PER, D)
    mix_send[1] = dot(mix[...], grad_update[...]).astype(bf16).reshape(8, PER, D)
    pl.semaphore_wait(barrier, N_DP + 2)

    def part(i):
        return pl.ds(pl.multiple_of(i * PER, PER), PER)

    to_experts = over_tensor(
        lambda p: mix_send.at[:, pl.ds(2 * p, 2)], lambda p: rows_e.at[:, :, part(p)]
    )
    to_experts.start()
    for kind in range(2):
        for e in range(2):
            rows_e[kind, e, part(t), :] = mix_send[kind, 2 * t + e]

    to_experts.wait()
    share_x = over_z(lambda p: rows_e.at[0], lambda p: xz.at[:, p])
    share_c = over_y(lambda p: rows_e.at[1], lambda p: cy.at[:, p])
    share_x.start()
    share_c.start()
    load_in.wait()
    load_out.wait()
    for e in range(2):
        rows_x, rows_c = rows_e[0, e], rows_e[1, e]
        for q in range(4):
            cols = pl.ds(512 * q, 512)
            pre = dot(rows_x, w_in[e, :, cols])
            inner = GELU_A * (pre + GELU_B * pre * pre * pre)
            th = jnp.tanh(inner)
            act_s[q, e] = (0.5 * pre * (1.0 + th)).astype(bf16)
            slope = 0.5 * (1.0 + th) + 0.5 * pre * (1.0 - th * th) * (
                GELU_A * (1.0 + 3.0 * GELU_B * pre * pre)
            )
            grad_act = dot(rows_c, w_out[e, cols, :], NT)
            pre_s[q, e] = (grad_act * slope).astype(bf16)
        made = dot(act_s[0, e], w_out[e, 0:512, :])
        mixed = dot(pre_s[0, e], w_in[e, :, 0:512], NT)
        for q in range(1, 4):
            cols = pl.ds(512 * q, 512)
            made = made + dot(act_s[q, e], w_out[e, cols, :])
            mixed = mixed + dot(pre_s[q, e], w_in[e, :, cols], NT)
        ret_send[0, e] = made.astype(bf16)
        ret_send[1, e] = mixed.astype(bf16)

    from_experts = over_tensor(
        lambda p: ret_send.at[:, :, part(p)], lambda p: ret.at[:, pl.ds(2 * p, 2)]
    )
    from_experts.start()
    share_g = over_z(lambda p: pre_s.at[p], lambda p: gz.at[:, p])
    share_a = over_y(lambda p: act_s.at[p], lambda p: ay.at[:, p])
    share_g.start()
    share_a.start()
    for kind in range(2):
        for e in range(2):
            ret[kind, 2 * t + e] = ret_send[kind, e, part(t), :]
    xz[:, z] = rows_e[0]
    cy[:, y] = rows_e[1]
    gz[:, z] = pre_s[z]
    ay[:, y] = act_s[y]
    from_experts.wait()

    produced, mixed_back = ret[0].reshape(8 * PER, D), ret[1].reshape(8 * PER, D)
    scores = dot(produced, grad_update[...], NT) + dot(mixed_back, members[...], NT)
    grad_mixing = jnp.concatenate(
        [
            jnp.sum(
                jnp.where(own_group, scores[PER * e : PER * (e + 1)], 0.0), axis=0, keepdims=True
            )
            for e in range(8)
        ]
        + [jnp.zeros((8, ROWS), f32)],
        axis=0,
    )
    inner_sum = group_all(mixing * grad_mixing, jnp.add)
    grad_logits = (mixing * (grad_mixing - inner_sum)).astype(bf16)
    gm = dot(mix[...], mixed_back, TN) + dot(grad_logits, router[...], TN)
    gm_s[...] = gm.astype(bf16)
    gm_exchange = OverDp(gm_s, gm_g)
    gm_exchange.start()
    spread_s[...] = dot(mix[...], produced, TN).astype(bf16)
    floats_s[0] = dot(grad_logits, members[...])

    lane = lax.broadcasted_iota(jnp.int32, (D, 128), 1)
    part_a, part_b, part_c = (qkv[:, 128 * i : 128 * (i + 1)].astype(f32) for i in range(3))
    w_all[t, :, 0:128] = jnp.where(lane < 64, part_a, part_b).astype(bf16)
    w_all[t, :, 128:256] = pltpu.roll(jnp.where(lane < 64, part_c, part_a), 64, 1).astype(bf16)
    w_all[t, :, 256:384] = jnp.where(lane < 64, part_b, part_c).astype(bf16)

    share_x.wait()
    share_g.wait()
    share_c.wait()
    share_a.wait()
    for e in range(2):
        o_in[e] = dot(xz[e].reshape(256, D), gz[e].reshape(256, 512), TN).astype(bf16).reshape(
            4, 128, 512
        )
        o_out[e] = dot(ay[e].reshape(256, 512), cy[e].reshape(256, D), TN).astype(bf16).reshape(
            4, 128, 512
        )
    sum_in = over_y(lambda p: o_in.at[:, p], lambda p: s2_in.at[p])
    sum_out = over_z(lambda p: o_out.at[:, p], lambda p: s2_out.at[p])
    sum_in.start()
    sum_out.start()
    s2_in[y] = o_in[:, y]
    s2_out[z] = o_out[:, z]
    spread_exchange = OverDp(spread_s, spread_g)
    spread_exchange.start()
    first_w = sems(2)

    def w_copy(kind, owner, peer):
        return remote(
            w_all.at[owner],
            w_all.at[owner],
            send.at[first_w + kind],
            recv.at[first_w + kind],
            (me, peer),
        )

    first_w2 = sems(1)

    def w_forward(owner):
        return remote(
            w_all.at[owner], w_all.at[owner], send.at[first_w2], recv.at[first_w2], (me, sibling)
        )

    w_copy(0, t, cross).start()
    w_copy(1, t, sibling).start()

    cols_z = pl.ds(pl.multiple_of(z * 512, 512), 512)
    half_in = over_x(s2_sum.at[0, 1 - xh], s3_got.at[0])
    half_out = over_x(s2_sum.at[1, 1 - xh], s3_got.at[1])
    pair_in = over_x(grad_in.at[xh, y, :, cols_z], grad_in.at[xh, y, :, cols_z])
    pair_out = over_x(grad_out.at[xh, y, z], grad_out.at[xh, y, z])
    all_in_z = over_z(
        lambda p: grad_in.at[:, y, :, cols_z], lambda p: grad_in.at[:, y, :, cols_z]
    )
    all_out_y = over_y(lambda p: grad_out.at[:, y, z], lambda p: grad_out.at[:, y, z])
    all_in_y = over_y(lambda p: grad_in.at[:, y], lambda p: grad_in.at[:, y])
    all_out_z = over_z(lambda p: grad_out.at[:, :, z], lambda p: grad_out.at[:, :, z])

    def reduce_ring():
        sum_in.wait()
        sum_out.wait()
        for e in range(2):
            total = s2_in[0, e].astype(f32)
            other = s2_out[0, e].astype(f32)
            for i in range(1, 4):
                total = total + s2_in[i, e].astype(f32)
                other = other + s2_out[i, e].astype(f32)
            s2_sum[0, e] = total.astype(bf16)
            s2_sum[1, e] = other.astype(bf16)
        half_in.start()
        half_out.start()

    def reduce_pair():
        half_in.wait()
        half_out.wait()
        grad_in[xh, y, :, cols_z] = (s2_sum[0, xh].astype(f32) + s3_got[0].astype(f32)).astype(bf16)
        grad_out[xh, y, z] = (s2_sum[1, xh].astype(f32) + s3_got[1].astype(f32)).astype(bf16)
        pair_in.start()
        pair_out.start()

    def gather_first():
        pair_in.wait()
        pair_out.wait()
        all_in_z.start()
        all_out_y.start()

    def gather_second():
        all_in_z.wait()
        all_out_y.wait()
        all_in_y.start()
        all_out_z.start()

    gm_exchange.wait()
    normed_two, scale_two = normalize(residual[...])
    grad_hidden_two = dot(perm[...], gm_g[...], TN).astype(bf16).astype(f32)
    floats_s[0, 8:9, :] = jnp.sum(grad_hidden_two * normed_two, axis=0, keepdims=True)
    grad_res[...] = cotangent[...].astype(f32) + norm_back(
        grad_hidden_two, normed_two, scale_two, gain_two[...]
    )
    grad_low = grad_res[...].astype(bf16)
    for i in range(4):
        gatt_s[i] = dot(grad_low, out_all[i], NT).astype(bf16)

    def rows_of(i):
        return pl.ds(pl.multiple_of(i * ROWS, ROWS), ROWS)

    att_exchange = over_tensor(lambda p: gatt_s.at[p], lambda p: gatt.at[rows_of(p)])
    att_exchange.start()
    gatt[rows_of(t), :] = gatt_s[t]
    for i in range(4):
        outp_s[i] = dot(att_pos[i], grad_low, TN).astype(bf16)
    outp_exchange = over_tensor(lambda p: outp_s.at[p], lambda p: outp_g.at[p])
    outp_exchange.start()
    outp_g[t] = outp_s[t]
    floats_exchange = [
        over_tensor(lambda p: floats_s.at[0], lambda p: floats_g.at[0, p]),
        over_y(lambda p: floats_s.at[1], lambda p: floats_g.at[1, p]),
        over_z(lambda p: floats_s.at[2], lambda p: floats_g.at[2, p]),
        over_x(floats_s.at[3], floats_g.at[3, 0]),
    ]
    floats_exchange[0].start()
    floats_g[0, t] = floats_s[0]

    def floats_step(i):
        floats_exchange[i].wait()
        got = floats_g[i, 0]
        for j in range(1, 4):
            got = got + floats_g[i, j]
        floats_s[i + 1] = got
        floats_exchange[i + 1].start()
        if i == 0:
            floats_g[1, y] = got
        if i == 1:
            floats_g[2, z] = got

    def floats_end():
        floats_exchange[3].wait()
        grad_floats[...] = floats_s[3] + floats_g[3, 0]

    reduce_ring()
    w_copy(0, cross, cross).wait_recv()
    w_forward(cross).start()

    att_exchange.wait()
    half = lax.broadcasted_iota(jnp.int32, (ROWS, 128), 1) < 64
    for i in range(4):
        rows = pl.ds(i * ROWS, ROWS)
        grads = gatt[rows, :].astype(f32)
        do2[0, rows, :] = jnp.where(half, grads, 0.0).astype(bf16)
        do2[1, rows, :] = jnp.where(half, 0.0, grads).astype(bf16)
        product = (grads * att_own[rows, :].astype(f32)).T
        delta[0:1, rows] = jnp.sum(product[:64], axis=0, keepdims=True)
        delta[1:2, rows] = jnp.sum(product[64:], axis=0, keepdims=True)

    gp_sems = sems(4)

    def gp_copy(block, source, peer):
        return remote(
            gp_own.at[block],
            gp_all.at[source],
            send.at[gp_sems + block],
            recv.at[gp_sems + source],
            (me, peer),
        )

    def block_out_store():
        spread_exchange.wait()
        update = dot(perm[...], spread_g[...], TN).astype(bf16).astype(f32)
        block_out[...] = (residual[...] + update).astype(bf16)

    def grad_qkv_part(block):
        return dot(hidden[block * ROWS : (block + 1) * ROWS, :], gp_own[block], TN)

    between = {
        (3, 0): reduce_pair,
        (3, 1): gather_first,
        (3, 2): lambda: floats_step(0),
        (3, 3): gather_second,
        (2, 0): lambda: floats_step(1),
        (2, 1): block_out_store,
        (2, 2): lambda: floats_step(2),
        (1, 0): floats_end,
    }
    grad_qkv = None
    rows = ROWS
    for block in (3, 2, 1, 0):
        base = block * rows
        here = pl.ds(base, rows)
        place, first = document_starts(lengths, base, rows)
        grad_q = jnp.zeros((128, rows), f32)
        for index in range(block + 1):
            there = pl.ds(index * rows, rows)
            allowed = allowed_pairs(place, first, index * rows, rows)
            keys, values = k[there, :], v[there, :]
            grad_v, grad_k = None, None
            for head in range(2):
                queries, grads = q2[head, here, :], do2[head, here, :]
                scores = dot(keys, queries, NT)
                shifted = jnp.where(allowed, scores - lse[head : head + 1, here], -1e30)
                weights = jnp.exp(shifted)
                grad_w = dot(values, grads, NT)
                grad_s = (weights * (grad_w - delta[head : head + 1, here])).astype(bf16)
                term = dot(weights.astype(bf16), grads)
                grad_v = term if grad_v is None else grad_v + term
                term = dot(grad_s, queries)
                grad_k = term if grad_k is None else grad_k + term
                grad_q = grad_q + dot(k2t[head, :, there], grad_s)
            if block == 3:
                dk[there, :] = grad_k
                dv[there, :] = grad_v
            else:
                dk[there, :] += grad_k
                dv[there, :] += grad_v
            if (block, index) in between:
                between[block, index]()
        gp_own[block, :, 0:128] = (grad_q * 0.125).T.astype(bf16)
        gp_own[block, :, 128:256] = dk[here, :].astype(bf16)
        gp_own[block, :, 256:384] = dv[here, :].astype(bf16)

        @pl.when(t == block)
        def _():
            gp_all[t] = gp_own[block]

        @pl.when(t != block)
        def _():
            gp_copy(block, t, block).start()

        term = grad_qkv_part(block)
        grad_qkv = term if grad_qkv is None else grad_qkv + term

    outp_exchange.wait()
    lane = lax.broadcasted_iota(jnp.int32, (D, 128), 1)
    part_q, part_k, part_v = (grad_qkv[:, 128 * i : 128 * (i + 1)] for i in range(3))
    part_k = pltpu.roll(part_k, 64, 1)
    small_s[:, 0:128] = jnp.where(lane < 64, part_q, part_k).astype(bf16)
    small_s[:, 128:256] = jnp.where(lane < 64, part_v, part_q).astype(bf16)
    small_s[:, 256:384] = jnp.where(lane < 64, part_k, part_v).astype(bf16)
    out_sum = outp_g[0].astype(f32)
    for i in range(1, 4):
        out_sum = out_sum + outp_g[i].astype(f32)
    for i in range(4):
        small_s[128 * i : 128 * (i + 1), 384:512] = out_sum[:, 128 * i : 128 * (i + 1)].astype(bf16)
    small_exchange = OverDp(small_s, small_g)
    small_exchange.start()

    w_copy(1, sibling, sibling).wait_recv()
    w_forward(far).wait_recv()
    for peer in (sibling, cross, far):
        gp_copy(0, peer, peer).wait_recv()
    normed_one, scale_one = normalize(tokens[...].astype(f32))
    grad_hidden_one = dot(gp_all[0], w_all[0], NT)
    for i in range(1, 4):
        grad_hidden_one = grad_hidden_one + dot(gp_all[i], w_all[i], NT)
    gain = jnp.sum(grad_hidden_one * normed_one, axis=0, keepdims=True)
    gain_s[...] = jnp.concatenate(
        [gain[:, 128 * i : 128 * (i + 1)] for i in range(4)] + [jnp.zeros((4, 128), f32)], axis=0
    )
    gain_exchange = over_tensor(lambda p: gain_s, lambda p: gain_g.at[p])
    gain_exchange.start()
    gain_g[t] = gain_s[...]
    grad_tokens[...] = (
        grad_res[...] + norm_back(grad_hidden_one, normed_one, scale_one, gain_one[...])
    ).astype(bf16)

    small_exchange.wait()
    total = small_g[0:PER, :].astype(f32)
    for i in range(1, N_DP):
        total = total + small_g[PER * i : PER * (i + 1), :].astype(f32)
    mine = part(me)
    grad_small[mine, :] = total.astype(bf16)

    first_small, first_gain = sems(N_DP), sems(N_DP)

    def small_copy(i, peer, owner):
        return remote(
            grad_small.at[part(owner)],
            grad_small.at[part(owner)],
            send.at[first_small + i],
            recv.at[first_small + i],
            (peer, t),
        )

    def gain_copy(i, peer, owner):
        return remote(
            gain_all.at[owner],
            gain_all.at[owner],
            send.at[first_gain + i],
            recv.at[first_gain + i],
            (peer, t),
        )

    def for_dp(body):
        def step(i, carry):
            body(i)
            return carry

        lax.fori_loop(1, N_DP, step, 0)

    for_dp(lambda i: small_copy(i, (me + i) % N_DP, me).start())
    gain_exchange.wait()
    gain_all[me] = (gain_g[0] + gain_g[1]) + (gain_g[2] + gain_g[3])
    for_dp(lambda i: gain_copy(i, (me + i) % N_DP, me).start())

    w_copy(0, t, cross).wait_send()
    w_copy(1, t, sibling).wait_send()
    w_forward(cross).wait_send()
    for block in range(4):

        @pl.when(t != block)
        def _():
            gp_copy(block, t, block).wait_send()

    def finish(i):
        small_copy(i, (me + i) % N_DP, me).wait_send()
        small_copy(i, (me + i) % N_DP, (me + N_DP - i) % N_DP).wait_recv()
        gain_copy(i, (me + i) % N_DP, me).wait_send()
        gain_copy(i, (me + i) % N_DP, (me + N_DP - i) % N_DP).wait_recv()

    for_dp(finish)
    gain_total = gain_all[0]
    for i in range(1, N_DP):
        gain_total = gain_total + gain_all[i]
    grad_gain[...] = gain_total
    all_in_y.wait()
    all_out_z.wait()


def tail(*args):
    sds = jax.ShapeDtypeStruct
    vmem = pl.BlockSpec(memory_space=pltpu.VMEM)
    hbm = pl.BlockSpec(memory_space=pl.ANY)
    dma = pltpu.SemaphoreType.DMA
    buf = lambda *shape: pltpu.VMEM(shape, bf16)
    wide = lambda *shape: pltpu.VMEM(shape, f32)
    specs = [pl.BlockSpec(memory_space=pltpu.SMEM)] + [vmem] * 21
    specs[4] = specs[5] = hbm
    return pl.pallas_call(
        tail_kernel,
        name="tail",
        out_shape=(
            sds((ROWS, D), bf16),
            sds((ROWS, D), bf16),
            sds((ROWS, D), bf16),
            sds((16, D), f32),
            sds((8, 128), f32),
            sds((2, 4, 128, 2048), bf16),
            sds((2, 4, 4, 128, 512), bf16),
        ),
        in_specs=specs,
        out_specs=[vmem] * 7,
        scratch_shapes=[
            buf(2, 512, 2048),
            buf(2, 2048, 512),
            buf(128, ROWS),
            buf(2, 8, PER, D),
            buf(2, 2, 64, D),
            buf(2, 2, 64, D),
            buf(2, 8, PER, D),
            buf(4, 2, 64, 512),
            buf(4, 2, 64, 512),
            buf(2, 4, 64, 512),
            buf(2, 4, 64, 512),
            buf(2, 4, 64, 512),
            buf(2, 4, 64, 512),
            buf(2, 4, 128, 512),
            buf(2, 4, 128, 512),
            buf(4, 2, 128, 512),
            buf(4, 2, 128, 512),
            buf(2, 2, 128, 512),
            buf(2, 128, 512),
            buf(ROWS, D),
            buf(ROWS, D),
            buf(ROWS, D),
            buf(ROWS, D),
            buf(4, D, 384),
            wide(ROWS, D),
            buf(4, ROWS, 128),
            buf(LENGTH, 128),
            buf(4, 128, D),
            buf(4, 128, D),
            buf(2, LENGTH, 128),
            wide(2, LENGTH),
            wide(8, 128),
            wide(LENGTH, 128),
            wide(LENGTH, 128),
            buf(4, ROWS, 384),
            buf(4, ROWS, 384),
            buf(ROWS, D),
            buf(ROWS, D),
            wide(4, 16, D),
            wide(4, 4, 16, D),
            wide(8, 128),
            wide(4, 8, 128),
            wide(N_DP, 8, 128),
            dma((256,)),
            dma((256,)),
            dma((2,)),
        ],
        compiler_params=pltpu.CompilerParams(
            collective_id=1, has_side_effects=True, vmem_limit_bytes=60 * 2**20
        ),
    )(*args)


def local(
    tokens,
    cotangent,
    doc_lengths,
    group_slot,
    norm1_gain,
    qkv_weight,
    out_weight,
    norm2_gain,
    router_weight,
    expert_in,
    expert_out,
):
    gain_one, gain_two = norm1_gain[None], norm2_gain[None]
    router = jnp.concatenate([router_weight.T, jnp.zeros((8, D), bf16)], axis=0)
    (members, grad_update, residual, hidden, q2, k, v, k2t, lse, att_own, att_pos, out_all, perm) = (
        front(
            doc_lengths,
            tokens,
            cotangent,
            group_slot,
            gain_one,
            qkv_weight,
            out_weight,
            gain_two,
        )
    )
    block_out, grad_tokens, small, floats, gain, grad_in, grad_out = tail(
        doc_lengths,
        members,
        grad_update,
        router,
        expert_in,
        expert_out,
        tokens,
        cotangent,
        residual,
        gain_one,
        gain_two,
        qkv_weight,
        hidden,
        q2,
        k,
        v,
        k2t,
        lse,
        att_own,
        att_pos,
        out_all,
        perm,
    )
    grad_out_w = jnp.swapaxes(small[:, 384:].reshape(4, 128, 128), 0, 1).reshape(128, D)
    return (
        block_out,
        grad_tokens,
        gain[:4].reshape(D),
        small[:, :384].astype(f32),
        grad_out_w.astype(f32),
        floats[8],
        floats[:8].T,
        grad_in.reshape(2, 512, 2048).astype(f32),
        grad_out.reshape(2, 2048, 512).astype(f32),
    )


def solution(mesh):
    in_specs = (
        P(("dp", "tensor"), None),
        P(("dp", "tensor"), None),
        P("dp", None),
        P(("dp", "tensor"), None),
        P(),
        P(None, "tensor"),
        P("tensor", None),
        P(),
        P(),
        P("tensor", None, None),
        P("tensor", None, None),
    )
    out_specs = (
        P(("dp", "tensor"), None),
        P(("dp", "tensor"), None),
        P(),
        P(None, "tensor"),
        P("tensor", None),
        P(),
        P(),
        P("tensor", None, None),
        P("tensor", None, None),
    )
    return jax.shard_map(local, mesh=mesh, in_specs=in_specs, out_specs=out_specs, check_vma=False)
```

```python
from types import SimpleNamespace

import jax
import jax.numpy as jnp
from jax import lax
from jax.experimental import pallas as pl
from jax.experimental.pallas import tpu as pltpu
from jax.sharding import PartitionSpec as P

D = 512
GROUP = 32
ROWS = 512
LENGTH = 2048
N_DP = 32
PER = ROWS // N_DP
CHUNKS = 4
MESH = pl.DeviceIdType.MESH
NN = (((1,), (0,)), ((), ()))
NT = (((1,), (1,)), ((), ()))
TN = (((0,), (0,)), ((), ()))
f32 = jnp.float32
bf16 = jnp.bfloat16
eps = 1e-06


def dot(a, b, dims=NN):
    return lax.dot_general(a, b, dims, preferred_element_type=f32)


def normalize(values):
    factor = lax.rsqrt(jnp.mean(values * values, axis=-1, keepdims=True) + eps)
    return (values * factor, factor)


def norm_back(grad_hidden, normed, factor, gain_row):
    grad_normed = grad_hidden * gain_row
    inner_sum = jnp.mean(grad_normed * normed, axis=-1, keepdims=True)
    return factor * (grad_normed - normed * inner_sum)


def remote(src, dst, send_sem, recv_sem, device):
    return pltpu.make_async_remote_copy(
        src_ref=src,
        dst_ref=dst,
        send_sem=send_sem,
        recv_sem=recv_sem,
        device_id=device,
        device_id_type=MESH,
    )


def document_starts(lengths, base, count):
    place = lax.broadcasted_iota(jnp.int32, (1, count), 1) + base
    bound = jnp.int32(0)
    first = jnp.zeros((1, count), jnp.int32)
    for slot in range(9):
        bound = bound + lengths[0, slot]
        first = jnp.where(bound <= place, bound, first)
    return place, first


def allowed_pairs(place, first, key_base, keys):
    key = lax.broadcasted_iota(jnp.int32, (keys, place.shape[1]), 0)
    return (key >= first - key_base) & (key <= place - key_base)


def dp_exchange_start(source, target, send_sem, recv_sem):
    me, t = lax.axis_index("dp"), lax.axis_index("tensor")
    mine = pl.ds(pl.multiple_of(me * PER, PER), PER)

    def step(k, carry):
        peer = (me + k) % N_DP
        theirs = pl.ds(pl.multiple_of(peer * PER, PER), PER)
        remote(source.at[theirs], target.at[mine], send_sem, recv_sem, (peer, t)).start()
        return carry

    lax.fori_loop(1, N_DP, step, 0)
    target[mine] = source[mine]


def dp_exchange_wait(source, target, send_sem, recv_sem):
    me, t = lax.axis_index("dp"), lax.axis_index("tensor")
    most = pl.ds(0, (N_DP - 1) * PER)
    remote(source.at[most], target.at[most], send_sem, recv_sem, ((me + 1) % N_DP, t)).wait()


class Exchange:
    def __init__(self, make, count, total):
        self.make, self.count, self.total = make, count, total

    def start(self):
        for i in range(self.count):
            self.make(i).start()

    def wait(self):
        self.total.wait()


GELU_A = 0.7978845608028654
GELU_B = 0.044715

ARGUMENTS = {
    "tokens": ((ROWS, D), bf16),
    "gain_one": ((1, D), f32),
    "out_w": ((128, D), bf16),
    "qkv": ((D, 384), bf16),
    "slot": ((1, ROWS), jnp.int32),
    "cotangent": ((ROWS, D), bf16),
    "lengths": ((1, 9), jnp.int32),
    "gain_two": ((1, D), f32),
    "router": ((8, D), bf16),
}
WEIGHTS = ["expert_in", "expert_out"]
OUTPUTS = {
    "block_out": ((ROWS, D), bf16),
    "grad_tokens": ((ROWS, D), bf16),
    "grad_small": ((ROWS, D), bf16),
    "grad_floats": ((16, D), f32),
    "grad_gain": ((8, 128), f32),
    "grad_in": ((2, 4, 128, 2048), bf16),
    "grad_out": ((2, 4, 4, 128, 512), bf16),
}
SCRATCH = {
    "members": ((ROWS, D), bf16),
    "grad_update": ((ROWS, D), bf16),
    "residual": ((ROWS, D), f32),
    "hidden": ((LENGTH, D), bf16),
    "q2": ((2, LENGTH, 128), bf16),
    "k": ((LENGTH, 128), bf16),
    "v": ((LENGTH, 128), bf16),
    "k2t": ((2, 128, LENGTH), bf16),
    "v2t": ((2, 128, LENGTH), bf16),
    "lse": ((2, LENGTH), f32),
    "att_max": ((4, 2, 1, ROWS), f32),
    "att_sum": ((4, 2, 128, ROWS), f32),
    "att_own": ((LENGTH, 128), bf16),
    "att_pos": ((4, ROWS, 128), bf16),
    "out_all": ((4, 128, D), bf16),
    "perm": ((ROWS, ROWS), bf16),
    "sorted_grad": ((ROWS, D), bf16),
    "sorted_hidden": ((ROWS, D), bf16),
    "w_own": ((D, 384), bf16),
    "mix": ((128, ROWS), bf16),
    "mix_send": ((2, 8, PER, D), bf16),
    "rows_e": ((2, 2, 64, D), bf16),
    "ret_send": ((2, 2, 64, D), bf16),
    "ret": ((2, 8, PER, D), bf16),
    "act_s": ((4, 2, 64, 512), bf16),
    "pre_s": ((4, 2, 64, 512), bf16),
    "xz": ((2, 4, 64, 512), bf16),
    "gz": ((2, 4, 64, 512), bf16),
    "ay": ((2, 4, 64, 512), bf16),
    "cy": ((2, 4, 64, 512), bf16),
    "o_in": ((2, 4, 128, 512), bf16),
    "o_out": ((2, 4, 128, 512), bf16),
    "s2_in": ((2, 4, 128, 512), bf16),
    "s2_out": ((2, 4, 128, 512), bf16),
    "s3_send": ((2, 2, 128, 512), bf16),
    "s3_got": ((2, 2, 128, 512), bf16),
    "spread_s": ((ROWS, D), bf16),
    "spread_g": ((ROWS, D), bf16),
    "gm_s": ((ROWS, D), bf16),
    "gm_g": ((ROWS, D), bf16),
    "grad_res": ((ROWS, D), f32),
    "gatt_s": ((4, ROWS, 128), bf16),
    "gatt": ((LENGTH, 128), bf16),
    "outp_s": ((4, 128, D), bf16),
    "outp_g": ((3, 128, D), bf16),
    "outp_f": ((128, D), bf16),
    "do2": ((2, LENGTH, 128), bf16),
    "delta": ((2, LENGTH), f32),
    "dk": ((LENGTH, 128), f32),
    "dv": ((LENGTH, 128), f32),
    "gp": ((ROWS, 384), bf16),
    "back_s": ((4, ROWS, D), bf16),
    "back_g": ((3, ROWS, D), bf16),
    "back_f": ((ROWS, D), bf16),
    "small_s": ((ROWS, D), bf16),
    "small_g": ((ROWS, D), bf16),
    "floats_s": ((4, 16, D), f32),
    "floats_g": ((4, 4, 16, D), f32),
    "gain_s": ((8, 128), f32),
    "gain_g": ((4, 8, 128), f32),
    "gain_all": ((N_DP, 8, 128), f32),
}
N_SEMS = 66


def block_kernel(*refs):
    names = ["from_" + name for name in ARGUMENTS] + WEIGHTS + list(OUTPUTS)
    names += list(ARGUMENTS) + list(SCRATCH) + ["send", "recv", "load"]
    r = SimpleNamespace(**dict(zip(names, refs)))
    send, recv = r.send, r.recv
    me, t = lax.axis_index("dp"), lax.axis_index("tensor")
    y, z, xh = me // 8, (me // 2) % 4, me % 2
    sibling, cross, far = t + 1 - 2 * (t % 2), (t + 2) % 4, 3 - t
    loads = {
        name: pltpu.make_async_copy(getattr(r, "from_" + name), getattr(r, name), r.load.at[2 + i])
        for i, name in enumerate(ARGUMENTS)
    }
    for copy in loads.values():
        copy.start()
    barrier = pltpu.get_barrier_semaphore()
    for peer in (sibling, cross, far):
        pl.semaphore_signal(barrier, inc=1, device_id=(me, peer), device_id_type=MESH)

    def for_dp(body):
        def step(i, carry):
            body(i)
            return carry

        lax.fori_loop(1, N_DP, step, 0)

    def greet(i):
        pl.semaphore_signal(barrier, inc=1, device_id=((me + i) % N_DP, t), device_id_type=MESH)

    for_dp(greet)

    taken = [0]

    def sems(count):
        first = taken[0]
        taken[0] += count
        assert taken[0] <= N_SEMS
        return first

    def dp_id(y_, z_, x_):
        return y_ * 8 + z_ * 2 + x_

    def over(size, place, device, source, target, total):
        at = sems(1)

        def make(i):
            peer = (place + 1 + i) % size
            return remote(source(peer), target(place), send.at[at], recv.at[at], device(peer))

        every = remote(total, total, send.at[at], recv.at[at], device((place + 1) % size))
        return Exchange(make, size - 1, every)

    def over_tensor(source, target, total):
        return over(4, t, lambda p: (me, p), source, target, total)

    def over_y(source, target, total):
        return over(4, y, lambda p: (dp_id(p, z, xh), t), source, target, total)

    def over_z(source, target, total):
        return over(4, z, lambda p: (dp_id(y, p, xh), t), source, target, total)

    def over_x(source, target):
        return over(
            2, xh, lambda p: (dp_id(y, z, p), t), lambda p: source, lambda p: target, target
        )

    def pair(source, target, peer):
        at = sems(1)
        copy = remote(source, target, send.at[at], recv.at[at], (me, peer))
        return Exchange(lambda i: copy, 1, copy)

    class OverDp:
        def __init__(self, source, target):
            at = sems(1)
            self.args = (source, target, send.at[at], recv.at[at])

        def start(self):
            dp_exchange_start(*self.args)

        def wait(self):
            dp_exchange_wait(*self.args)

    three = pl.ds(0, 3)

    def rows_of(i):
        return pl.ds(pl.multiple_of(i * ROWS, ROWS), ROWS)

    def part(i):
        return pl.ds(pl.multiple_of(i * PER, PER), PER)

    load_in = pltpu.make_async_copy(r.expert_in, r.grad_in, r.load.at[0])
    load_out = pltpu.make_async_copy(r.expert_out, r.grad_out, r.load.at[1])

    step = ROWS // CHUNKS
    loads["tokens"].wait()
    loads["gain_one"].wait()
    for c in range(CHUNKS):
        values = r.tokens[c * step : (c + 1) * step, :].astype(f32)
        normed, _ = normalize(values)
        r.hidden[pl.ds(pl.multiple_of(t * ROWS + c * step, step), step), :] = (
            normed * r.gain_one[...]
        ).astype(bf16)
    loads["out_w"].wait()
    r.out_all[t] = r.out_w[...]
    pl.semaphore_wait(barrier, N_DP + 2)

    hid = sems(3 * CHUNKS)

    def hidden_copy(kind, owner, c, device):
        rows = pl.ds(pl.multiple_of(owner * ROWS + c * step, step), step)
        at = hid + kind * CHUNKS + c
        return remote(r.hidden.at[rows], r.hidden.at[rows], send.at[at], recv.at[at], (me, device))

    for c in range(CHUNKS):
        hidden_copy(1, t, c, cross).start()
        hidden_copy(0, t, c, sibling).start()

    for name in ("slot", "cotangent", "qkv", "lengths", "gain_two", "router"):
        loads[name].wait()
    place = lax.broadcasted_iota(jnp.int32, (ROWS, ROWS), 0)
    r.perm[...] = jnp.where(place == r.slot[...], 1.0, 0.0).astype(bf16)
    r.sorted_grad[...] = dot(r.perm[...], r.cotangent[...]).astype(bf16)

    lane = lax.broadcasted_iota(jnp.int32, (D, 128), 1)
    part_a, part_b, part_c = (r.qkv[:, 128 * i : 128 * (i + 1)].astype(f32) for i in range(3))
    r.w_own[:, 0:128] = jnp.where(lane < 64, part_a, part_b).astype(bf16)
    r.w_own[:, 128:256] = pltpu.roll(jnp.where(lane < 64, part_c, part_a), 64, 1).astype(bf16)
    r.w_own[:, 256:384] = jnp.where(lane < 64, part_b, part_c).astype(bf16)

    half = lax.broadcasted_iota(jnp.int32, (ROWS, 128), 1) < 64
    half_t = lax.broadcasted_iota(jnp.int32, (128, ROWS), 0) < 64

    def project(owner):
        rows = rows_of(owner)
        block = r.hidden[rows, :]
        queries = dot(block, r.w_own[:, 0:128]).astype(bf16).astype(f32) * 0.125
        r.q2[0, rows, :] = jnp.where(half, queries, 0.0).astype(bf16)
        r.q2[1, rows, :] = jnp.where(half, 0.0, queries).astype(bf16)
        keys = dot(block, r.w_own[:, 128:256])
        r.k[rows, :] = keys.astype(bf16)
        keys_t = keys.T
        r.k2t[0, :, rows] = jnp.where(half_t, keys_t, 0.0).astype(bf16)
        r.k2t[1, :, rows] = jnp.where(half_t, 0.0, keys_t).astype(bf16)
        values = dot(block, r.w_own[:, 256:384])
        r.v[rows, :] = values.astype(bf16)
        values_t = values.T
        r.v2t[0, :, rows] = jnp.where(half_t, values_t, 1.0).astype(bf16)
        r.v2t[1, :, rows] = jnp.where(half_t, 1.0, values_t).astype(bf16)

    out_exchange = over_tensor(
        lambda p: r.out_all.at[t], lambda p: r.out_all.at[t], r.out_all.at[three]
    )
    grad_exchange = OverDp(r.sorted_grad, r.grad_update)

    att_sems = sems(4)

    def att_copy(block, source, device):
        return remote(
            r.att_own.at[rows_of(block)],
            r.att_pos.at[source],
            send.at[att_sems + block],
            recv.at[att_sems + source],
            (me, device),
        )

    def attend(query_block, key_block, fresh):
        rows, keys_at = rows_of(query_block), rows_of(key_block)
        place, first = document_starts(r.lengths, query_block * ROWS, ROWS)
        allowed = allowed_pairs(place, first, key_block * ROWS, ROWS)
        keys = r.k[keys_at, :]
        for head in range(2):
            scores = jnp.where(allowed, dot(keys, r.q2[head, rows, :], NT), -1e30)
            maxima = jnp.max(scores, axis=0, keepdims=True)
            if not fresh:
                before = r.att_max[query_block, head]
                maxima = jnp.maximum(before, maxima)
            weights = jnp.exp(scores - maxima).astype(bf16)
            total = dot(r.v2t[head, :, keys_at], weights)
            if not fresh:
                total = r.att_sum[query_block, head] * jnp.exp(before - maxima) + total
            r.att_max[query_block, head] = maxima
            r.att_sum[query_block, head] = total

    def attended_block(block):
        rows = rows_of(block)
        sum_a, sum_b = r.att_sum[block, 0], r.att_sum[block, 1]
        norm_a, norm_b = sum_a[64:65], sum_b[0:1]
        attended = jnp.concatenate([sum_a[:64] / norm_a, sum_b[64:] / norm_b], axis=0)
        r.att_own[rows, :] = attended.T.astype(bf16)
        r.lse[0:1, rows] = r.att_max[block, 0] + jnp.log(norm_a)
        r.lse[1:2, rows] = r.att_max[block, 1] + jnp.log(norm_b)

        @pl.when(t == block)
        def _():
            r.att_pos[t] = r.att_own[rows, :]

        @pl.when(t != block)
        def _():
            att_copy(block, t, block).start()

    chip = t // 2
    project(t)
    for c in range(CHUNKS):
        hidden_copy(0, sibling, c, sibling).wait_recv()
    project(sibling)
    low, high = 2 * chip, 2 * chip + 1
    attend(low, low, True)
    attend(high, high, True)
    attend(high, low, False)
    for c in range(CHUNKS):
        hidden_copy(1, cross, c, cross).wait_recv()
        hidden_copy(2, cross, c, sibling).start()
        if c == CHUNKS - 2:
            grad_exchange.start()
    load_in.start()
    load_out.start()
    project(cross)
    out_exchange.start()
    for c in range(CHUNKS):
        hidden_copy(2, far, c, sibling).wait_recv()
    project(far)

    @pl.when(chip == 0)
    def _():
        attended_block(0)
        attended_block(1)

    def choose(first, second):
        return first + (second - first) * chip

    plan = (
        ((2, 2), (0, 0), True, True, None, 0),
        ((2, 0), (1, 1), False, True, None, None),
        ((2, 1), (1, 0), False, False, 2, 1),
        ((3, 3), (2, 0), True, False, None, None),
        ((3, 0), (2, 1), False, False, None, 2),
        ((3, 1), (3, 0), False, False, None, None),
        ((3, 2), (3, 1), False, False, 3, 3),
    )
    for pair_a, pair_b, fresh_a, fresh_b, end_a, end_b in plan:
        if fresh_a != fresh_b:
            block = choose(pair_a[0], pair_b[0])

            @pl.when(chip == (0 if fresh_a else 1))
            def _():
                for head in range(2):
                    r.att_max[block, head] = jnp.full((1, ROWS), -1e30, f32)
                    r.att_sum[block, head] = jnp.zeros((128, ROWS), f32)

        attend(
            choose(pair_a[0], pair_b[0]), choose(pair_a[1], pair_b[1]), fresh_a and fresh_b
        )
        if end_a == end_b:
            if end_a is not None:
                attended_block(end_a)
        else:
            for which, end in enumerate((end_a, end_b)):
                if end is not None:

                    @pl.when(chip == which)
                    def _():
                        attended_block(end)

    out_exchange.wait()
    for peer in (sibling, cross, far):
        att_copy(0, peer, peer).wait_recv()

    update = dot(r.att_pos[0], r.out_all[0])
    for i in range(1, 4):
        update = update + dot(r.att_pos[i], r.out_all[i])
    r.residual[...] = r.tokens[...].astype(f32) + update
    normed_two, _ = normalize(r.residual[...])
    hidden_two = (normed_two * r.gain_two[...]).astype(bf16)
    r.sorted_hidden[...] = dot(r.perm[...], hidden_two).astype(bf16)
    member_exchange = OverDp(r.sorted_hidden, r.members)
    member_exchange.start()

    for c in range(CHUNKS):
        hidden_copy(0, t, c, sibling).wait_send()
        hidden_copy(1, t, c, cross).wait_send()
        hidden_copy(2, cross, c, sibling).wait_send()
    for block in range(4):

        @pl.when(t != block)
        def _():
            att_copy(block, t, block).wait_send()

    router = jnp.concatenate(
        [r.router[...].astype(f32), jnp.zeros((8, D), f32)], axis=0
    ).astype(bf16)
    grad_exchange.wait()
    load_in.wait()
    load_out.wait()
    member_exchange.wait()

    def group_all(values, op):
        for shift in (16, 32, 64, 128, 256):
            values = op(values, pltpu.roll(values, shift, 1))
        return values

    logits = dot(router, r.members[...], NT)
    exponent = jnp.exp(logits - group_all(logits, jnp.maximum))
    mixing = exponent / group_all(exponent, jnp.add)
    lane = lax.broadcasted_iota(jnp.int32, (PER, ROWS), 1)
    own_group = lax.broadcasted_iota(jnp.int32, (PER, ROWS), 0) == lane % PER
    r.mix[...] = jnp.concatenate(
        [jnp.where(own_group, mixing[e : e + 1], 0.0) for e in range(8)], axis=0
    ).astype(bf16)
    r.mix_send[0] = dot(r.mix[...], r.members[...]).astype(bf16).reshape(8, PER, D)
    r.mix_send[1] = dot(r.mix[...], r.grad_update[...]).astype(bf16).reshape(8, PER, D)

    to_experts = over_tensor(
        lambda p: r.mix_send.at[:, pl.ds(2 * p, 2)],
        lambda p: r.rows_e.at[:, :, part(p)],
        r.rows_e.at[:, :, pl.ds(0, 3 * PER)],
    )
    to_experts.start()
    for kind in range(2):
        for e in range(2):
            r.rows_e[kind, e, part(t), :] = r.mix_send[kind, 2 * t + e]

    to_experts.wait()
    share_x = over_z(lambda p: r.rows_e.at[0], lambda p: r.xz.at[:, p], r.xz.at[:, three])
    share_c = over_y(lambda p: r.rows_e.at[1], lambda p: r.cy.at[:, p], r.cy.at[:, three])
    share_x.start()
    share_c.start()

    def share_factors(e):
        return (
            over_z(lambda p: r.pre_s.at[p, e], lambda p: r.gz.at[e, p], r.gz.at[e, three]),
            over_y(lambda p: r.act_s.at[p, e], lambda p: r.ay.at[e, p], r.ay.at[e, three]),
        )

    share_pre, share_act = zip(*(share_factors(e) for e in range(2)))
    for e in range(2):
        rows_x, rows_c = r.rows_e[0, e], r.rows_e[1, e]

        def in_cols(q):
            return r.grad_in[e, :, :, pl.ds(512 * q, 512)].reshape(D, 512)

        def out_rows(q):
            return r.grad_out[e, q].reshape(512, D)

        for q in range(4):
            pre = dot(rows_x, in_cols(q))
            inner = GELU_A * (pre + GELU_B * pre * pre * pre)
            th = jnp.tanh(inner)
            r.act_s[q, e] = (0.5 * pre * (1.0 + th)).astype(bf16)
            slope = 0.5 * (1.0 + th) + 0.5 * pre * (1.0 - th * th) * (
                GELU_A * (1.0 + 3.0 * GELU_B * pre * pre)
            )
            grad_act = dot(rows_c, out_rows(q), NT)
            r.pre_s[q, e] = (grad_act * slope).astype(bf16)
        made = dot(r.act_s[0, e], out_rows(0))
        mixed = dot(r.pre_s[0, e], in_cols(0), NT)
        for q in range(1, 4):
            made = made + dot(r.act_s[q, e], out_rows(q))
            mixed = mixed + dot(r.pre_s[q, e], in_cols(q), NT)
        r.ret_send[0, e] = made.astype(bf16)
        r.ret_send[1, e] = mixed.astype(bf16)
        if e == 0:
            share_pre[e].start()
            share_act[e].start()

    from_experts = over_tensor(
        lambda p: r.ret_send.at[:, :, part(p)],
        lambda p: r.ret.at[:, pl.ds(2 * p, 2)],
        r.ret.at[:, pl.ds(0, 6)],
    )
    from_experts.start()
    share_pre[1].start()
    share_act[1].start()
    for kind in range(2):
        for e in range(2):
            r.ret[kind, 2 * t + e] = r.ret_send[kind, e, part(t), :]
    r.xz[:, z] = r.rows_e[0]
    r.cy[:, y] = r.rows_e[1]
    for e in range(2):
        r.gz[e, z] = r.pre_s[z, e]
        r.ay[e, y] = r.act_s[y, e]

    def ring_sums(e):
        return (
            over_y(lambda p: r.o_in.at[e, p], lambda p: r.s2_in.at[e, p], r.s2_in.at[e, three]),
            over_z(lambda p: r.o_out.at[e, p], lambda p: r.s2_out.at[e, p], r.s2_out.at[e, three]),
        )

    sum_in, sum_out = zip(*(ring_sums(e) for e in range(2)))

    def multiply_factors(e):
        share_pre[e].wait()
        share_act[e].wait()
        product = dot(r.xz[e].reshape(256, D), r.gz[e].reshape(256, 512), TN)
        r.o_in[e] = product.astype(bf16).reshape(4, 128, 512)
        product = dot(r.ay[e].reshape(256, 512), r.cy[e].reshape(256, D), TN)
        r.o_out[e] = product.astype(bf16).reshape(4, 128, 512)
        sum_in[e].start()
        sum_out[e].start()
        r.s2_in[e, y] = r.o_in[e, y]
        r.s2_out[e, z] = r.o_out[e, z]

    share_x.wait()
    share_c.wait()
    multiply_factors(0)
    from_experts.wait()

    produced, mixed_back = r.ret[0].reshape(8 * PER, D), r.ret[1].reshape(8 * PER, D)
    scores = dot(produced, r.grad_update[...], NT) + dot(mixed_back, r.members[...], NT)
    grad_mixing = jnp.concatenate(
        [
            jnp.sum(
                jnp.where(own_group, scores[PER * e : PER * (e + 1)], 0.0), axis=0, keepdims=True
            )
            for e in range(8)
        ]
        + [jnp.zeros((8, ROWS), f32)],
        axis=0,
    )
    inner_sum = group_all(mixing * grad_mixing, jnp.add)
    grad_logits = (mixing * (grad_mixing - inner_sum)).astype(bf16)
    gm = dot(r.mix[...], mixed_back, TN) + dot(grad_logits, router, TN)
    r.gm_s[...] = gm.astype(bf16)
    gm_exchange = OverDp(r.gm_s, r.gm_g)
    gm_exchange.start()

    multiply_factors(1)
    r.spread_s[...] = dot(r.mix[...], produced, TN).astype(bf16)
    r.floats_s[0] = dot(grad_logits, r.members[...])
    spread_exchange = OverDp(r.spread_s, r.spread_g)

    cols_z = pl.ds(pl.multiple_of(z * 512, 512), 512)

    def gather_first_ring(e):
        def in_part(p):
            return r.grad_in.at[e, y, :, cols_z]

        def out_part(p):
            return r.grad_out.at[e, y, z]

        return (
            over_z(in_part, in_part, r.grad_in.at[e, y, :, pl.ds(0, 3 * 512)]),
            over_y(out_part, out_part, r.grad_out.at[e, three, z]),
        )

    both = [over_x(r.s3_send.at[e], r.s3_got.at[e]) for e in range(2)]
    all_in_z, all_out_y = zip(*(gather_first_ring(e) for e in range(2)))

    def reduce_ring(e):
        sum_in[e].wait()
        sum_out[e].wait()
        total = r.s2_in[e, 0].astype(f32)
        other = r.s2_out[e, 0].astype(f32)
        for i in range(1, 4):
            total = total + r.s2_in[e, i].astype(f32)
            other = other + r.s2_out[e, i].astype(f32)
        r.s3_send[e, 0] = total.astype(bf16)
        r.s3_send[e, 1] = other.astype(bf16)
        both[e].start()

    def reduce_pair(e):
        both[e].wait()
        total = r.s3_send[e, 0].astype(f32) + r.s3_got[e, 0].astype(f32)
        other = r.s3_send[e, 1].astype(f32) + r.s3_got[e, 1].astype(f32)
        r.grad_in[e, y, :, cols_z] = total.astype(bf16)
        r.grad_out[e, y, z] = other.astype(bf16)
        all_in_z[e].start()
        all_out_y[e].start()

    ring_sems = sems(12)

    def ring_copy(axis, direction, kind, e):
        at = y if axis == 0 else z
        to = (at + 1 + 2 * direction) % 4
        owner = at if kind == 0 else (at + 3 - 2 * direction) % 4
        index = ring_sems + 6 * axis + (2 * direction + e if kind == 0 else 4 + direction)
        if axis == 0:
            here, device = r.grad_in.at[e, owner], (dp_id(to, z, xh), t)
        else:
            here, device = r.grad_out.at[e, :, owner], (dp_id(y, to, xh), t)
        return remote(here, here, send.at[index], recv.at[index], device)

    def gather_second(e):
        all_in_z[e].wait()
        all_out_y[e].wait()
        for direction in (e, 1 - e):
            for axis in range(2):
                ring_copy(axis, direction, 0, e).start()

    def hand_on(e):
        for axis in range(2):
            ring_copy(axis, e, 0, e).wait_recv()
            ring_copy(axis, e, 1, e).start()

    def gather_end(e):
        for axis in range(2):
            ring_copy(axis, e, 0, e).wait_send()
            ring_copy(axis, 1 - e, 0, e).wait()
            ring_copy(axis, e, 1, e).wait()

    reduce_ring(0)
    gm_exchange.wait()
    reduce_pair(0)
    normed_two, scale_two = normalize(r.residual[...])
    grad_hidden_two = dot(r.perm[...], r.gm_g[...], TN).astype(bf16).astype(f32)
    r.floats_s[0, 8:9, :] = jnp.sum(grad_hidden_two * normed_two, axis=0, keepdims=True)
    r.grad_res[...] = r.cotangent[...].astype(f32) + norm_back(
        grad_hidden_two, normed_two, scale_two, r.gain_two[...]
    )
    grad_low = r.grad_res[...].astype(bf16)
    for i in range(4):
        r.gatt_s[i] = dot(grad_low, r.out_all[i], NT).astype(bf16)

    att_exchange = over_tensor(lambda p: r.gatt_s.at[p], lambda p: r.gatt.at[rows_of(p)], r.gatt.at[pl.ds(0, 3 * ROWS)])
    att_exchange.start()
    reduce_ring(1)
    spread_exchange.start()
    r.gatt[rows_of(t), :] = r.gatt_s[t]
    for i in range(4):
        r.outp_s[i] = dot(r.att_pos[i], grad_low, TN).astype(bf16)
    outp = [
        pair(r.outp_s.at[sibling], r.outp_g.at[0], sibling),
        pair(r.outp_s.at[far], r.outp_g.at[1], sibling),
        pair(r.outp_f, r.outp_g.at[2], cross),
    ]
    outp[0].start()
    outp[1].start()
    floats_exchange = [
        over_tensor(lambda p: r.floats_s.at[0], lambda p: r.floats_g.at[0, p], r.floats_g.at[0, three]),
        over_y(lambda p: r.floats_s.at[1], lambda p: r.floats_g.at[1, p], r.floats_g.at[1, three]),
        over_z(lambda p: r.floats_s.at[2], lambda p: r.floats_g.at[2, p], r.floats_g.at[2, three]),
        over_x(r.floats_s.at[3], r.floats_g.at[3, 0]),
    ]
    floats_exchange[0].start()
    r.floats_g[0, t] = r.floats_s[0]

    def outp_forward():
        outp[1].wait()
        r.outp_f[...] = (r.outp_s[cross].astype(f32) + r.outp_g[1].astype(f32)).astype(bf16)
        outp[2].start()

    def floats_step(i):
        floats_exchange[i].wait()
        got = r.floats_g[i, 0]
        for j in range(1, 4):
            got = got + r.floats_g[i, j]
        r.floats_s[i + 1] = got
        floats_exchange[i + 1].start()
        if i == 0:
            r.floats_g[1, y] = got
        if i == 1:
            r.floats_g[2, z] = got

    def floats_end():
        floats_exchange[3].wait()
        r.grad_floats[...] = r.floats_s[3] + r.floats_g[3, 0]

    def block_out_store():
        spread_exchange.wait()
        update = dot(r.perm[...], r.spread_g[...], TN).astype(bf16).astype(f32)
        r.block_out[...] = (r.residual[...] + update).astype(bf16)

    att_exchange.wait()
    reduce_pair(1)
    gather_second(0)
    for i in range(4):
        rows = pl.ds(i * ROWS, ROWS)
        grads = r.gatt[rows, :].astype(f32)
        r.do2[0, rows, :] = jnp.where(half, grads, 0.0).astype(bf16)
        r.do2[1, rows, :] = jnp.where(half, 0.0, grads).astype(bf16)
        product = (grads * r.att_own[rows, :].astype(f32)).T
        r.delta[0:1, rows] = jnp.sum(product[:64], axis=0, keepdims=True)
        r.delta[1:2, rows] = jnp.sum(product[64:], axis=0, keepdims=True)

    back_sibling, back_far = sems(1), sems(1)
    back_cross = sems(1)

    def to_sibling(block, first, slot):
        return remote(
            r.back_s.at[block], r.back_g.at[slot], send.at[first], recv.at[first], (me, sibling)
        )

    def to_cross():
        return remote(
            r.back_f, r.back_g.at[2], send.at[back_cross], recv.at[back_cross], (me, cross)
        )

    def back_send(block):
        @pl.when(block == sibling)
        def _():
            to_sibling(block, back_sibling, 0).start()

        @pl.when(block == far)
        def _():
            to_sibling(block, back_far, 1).start()

    def back_forward(block):
        @pl.when(block == cross)
        def _():
            to_sibling(block, back_far, 1).wait_recv()
            r.back_f[...] = (r.back_s[block].astype(f32) + r.back_g[1].astype(f32)).astype(bf16)
            to_cross().start()

    between = {
        (3, 0): outp_forward,
        (3, 1): lambda: floats_step(0),
        (3, 2): lambda: gather_second(1),
        (2, 0): lambda: (back_forward(3), floats_step(1)),
        (2, 1): lambda: (block_out_store(), hand_on(0)),
        (2, 2): lambda: floats_step(2),
        (1, 0): lambda: (back_forward(2), hand_on(1)),
        (1, 1): floats_end,
        (0, 0): lambda: back_forward(1),
    }
    grad_qkv = None
    rows = ROWS
    for block in (3, 2, 1, 0):
        base = block * rows
        here = pl.ds(base, rows)
        place, first = document_starts(r.lengths, base, rows)
        grad_q = jnp.zeros((128, rows), f32)
        for index in range(block + 1):
            there = pl.ds(index * rows, rows)
            allowed = allowed_pairs(place, first, index * rows, rows)
            keys, values = r.k[there, :], r.v[there, :]
            grad_v, grad_k = None, None
            for head in range(2):
                queries, grads = r.q2[head, here, :], r.do2[head, here, :]
                scores = dot(keys, queries, NT)
                shifted = jnp.where(allowed, scores - r.lse[head : head + 1, here], -1e30)
                weights = jnp.exp(shifted)
                grad_w = dot(values, grads, NT)
                grad_s = (weights * (grad_w - r.delta[head : head + 1, here])).astype(bf16)
                term = dot(weights.astype(bf16), grads)
                grad_v = term if grad_v is None else grad_v + term
                term = dot(grad_s, queries)
                grad_k = term if grad_k is None else grad_k + term
                grad_q = grad_q + dot(r.k2t[head, :, there], grad_s)
            if block == 3:
                r.dk[there, :] = grad_k
                r.dv[there, :] = grad_v
            else:
                r.dk[there, :] += grad_k
                r.dv[there, :] += grad_v
            if (block, index) in between:
                between[block, index]()
        r.gp[:, 0:128] = (grad_q * 0.125).T.astype(bf16)
        r.gp[:, 128:256] = r.dk[here, :].astype(bf16)
        r.gp[:, 256:384] = r.dv[here, :].astype(bf16)
        r.back_s[block] = dot(r.gp[...], r.w_own[...], NT).astype(bf16)
        back_send(block)
        term = dot(r.hidden[base : base + rows, :], r.gp[...], TN)
        grad_qkv = term if grad_qkv is None else grad_qkv + term
    back_forward(0)

    outp[0].wait()
    outp[2].wait()
    lane = lax.broadcasted_iota(jnp.int32, (D, 128), 1)
    part_q, part_k, part_v = (grad_qkv[:, 128 * i : 128 * (i + 1)] for i in range(3))
    part_k = pltpu.roll(part_k, 64, 1)
    r.small_s[:, 0:128] = jnp.where(lane < 64, part_q, part_k).astype(bf16)
    r.small_s[:, 128:256] = jnp.where(lane < 64, part_v, part_q).astype(bf16)
    r.small_s[:, 256:384] = jnp.where(lane < 64, part_k, part_v).astype(bf16)
    out_sum = r.outp_s[t].astype(f32) + r.outp_g[0].astype(f32) + r.outp_g[2].astype(f32)
    for i in range(4):
        r.small_s[128 * i : 128 * (i + 1), 384:512] = out_sum[:, 128 * i : 128 * (i + 1)].astype(
            bf16
        )
    small_exchange = OverDp(r.small_s, r.small_g)
    small_exchange.start()

    normed_one, scale_one = normalize(r.tokens[...].astype(f32))
    to_sibling(sibling, back_sibling, 0).wait_recv()
    to_cross().wait_recv()
    grad_hidden_one = (
        r.back_s[t].astype(f32) + r.back_g[0].astype(f32) + r.back_g[2].astype(f32)
    )
    gain = jnp.sum(grad_hidden_one * normed_one, axis=0, keepdims=True)
    r.gain_s[...] = jnp.concatenate(
        [gain[:, 128 * i : 128 * (i + 1)] for i in range(4)] + [jnp.zeros((4, 128), f32)], axis=0
    )
    gain_exchange = over_tensor(lambda p: r.gain_s, lambda p: r.gain_g.at[p], r.gain_g.at[three])
    gain_exchange.start()
    r.gain_g[t] = r.gain_s[...]
    r.grad_tokens[...] = (
        r.grad_res[...] + norm_back(grad_hidden_one, normed_one, scale_one, r.gain_one[...])
    ).astype(bf16)

    small_exchange.wait()
    total = r.small_g[0:PER, :].astype(f32)
    for i in range(1, N_DP):
        total = total + r.small_g[PER * i : PER * (i + 1), :].astype(f32)
    r.grad_small[part(me), :] = total.astype(bf16)

    at_small, at_gain = sems(1), sems(1)

    def small_copy(i, here):
        peer = (me + i) % N_DP
        return remote(here, here, send.at[at_small], recv.at[at_small], (peer, t))

    def gain_copy(i, here):
        peer = (me + i) % N_DP
        return remote(here, here, send.at[at_gain], recv.at[at_gain], (peer, t))

    for_dp(lambda i: small_copy(i, r.grad_small.at[part(me)]).start())
    gain_exchange.wait()
    r.gain_all[me] = (r.gain_g[0] + r.gain_g[1]) + (r.gain_g[2] + r.gain_g[3])
    for_dp(lambda i: gain_copy(i, r.gain_all.at[me]).start())

    to_sibling(sibling, back_sibling, 0).wait_send()
    to_sibling(far, back_far, 1).wait_send()
    to_cross().wait_send()

    for e in range(2):
        gather_end(e)

    small_copy(1, r.grad_small.at[pl.ds(0, (N_DP - 1) * PER)]).wait()
    gain_copy(1, r.gain_all.at[pl.ds(0, N_DP - 1)]).wait()
    gain_total = r.gain_all[0]
    for i in range(1, N_DP):
        gain_total = gain_total + r.gain_all[i]
    r.grad_gain[...] = gain_total


def block(*args):
    vmem = pl.BlockSpec(memory_space=pltpu.VMEM)
    hbm = pl.BlockSpec(memory_space=pltpu.HBM)
    held = [
        (pltpu.SMEM if name == "lengths" else pltpu.VMEM)(*shape)
        for name, shape in ARGUMENTS.items()
    ]
    dma = pltpu.SemaphoreType.DMA
    return pl.pallas_call(
        block_kernel,
        name="block",
        out_shape=tuple(pltpu.VMEM(*shape) for shape in OUTPUTS.values()),
        in_specs=[hbm] * (len(ARGUMENTS) + len(WEIGHTS)),
        out_specs=[vmem] * len(OUTPUTS),
        scratch_shapes=held
        + [pltpu.VMEM(*shape) for shape in SCRATCH.values()]
        + [dma((N_SEMS,)), dma((N_SEMS,)), dma((2 + len(ARGUMENTS),))],
        compiler_params=pltpu.CompilerParams(
            collective_id=0, has_side_effects=True, vmem_limit_bytes=50 * 2**20
        ),
    )(*args)


SLOTS = 4


def finish_kernel(
    block_in,
    tokens_in,
    small,
    floats,
    gain,
    in_low,
    out_low,
    block_out,
    grad_tokens,
    grad_one,
    grad_qkv,
    grad_w,
    grad_two,
    grad_router,
    grad_in,
    grad_out,
    wide_in,
    wide_out,
    sems,
):
    whole = [
        pltpu.make_async_copy(block_in, block_out, sems.at[2 * SLOTS]),
        pltpu.make_async_copy(tokens_in, grad_tokens, sems.at[2 * SLOTS + 1]),
    ]
    for copy in whole:
        copy.start()
    parts = [(e, i) for e in range(2) for i in range(4)]

    def copies(n):
        e, i = parts[n]
        slot = n % SLOTS
        return (
            pltpu.make_async_copy(wide_in.at[slot], grad_in.at[e, i], sems.at[slot]),
            pltpu.make_async_copy(wide_out.at[slot], grad_out.at[e, i], sems.at[SLOTS + slot]),
        )

    for n, (e, i) in enumerate(parts):
        slot = n % SLOTS
        to_in, to_out = copies(n)
        if n >= SLOTS:
            copies(n - SLOTS)[0].wait()
        wide_in[slot] = in_low[e, i].astype(f32)
        to_in.start()
        if n >= SLOTS:
            copies(n - SLOTS)[1].wait()
        wide_out[slot] = out_low[e, i].astype(f32)
        to_out.start()
    grad_qkv[...] = small[:, :384].astype(f32)
    for i in range(4):
        cols = slice(128 * i, 128 * (i + 1))
        grad_w[:, cols] = small[cols, 384:512].astype(f32)
        grad_one[:, cols] = gain[i : i + 1, :]
    grad_two[...] = floats[8:9, :]
    grad_router[...] = floats[0:8, :]
    for n in range(len(parts) - SLOTS, len(parts)):
        for copy in copies(n):
            copy.wait()
    for copy in whole:
        copy.wait()


def finish(*results):
    sds = jax.ShapeDtypeStruct
    vmem = pl.BlockSpec(memory_space=pltpu.VMEM)
    hbm = pl.BlockSpec(memory_space=pl.ANY)
    return pl.pallas_call(
        finish_kernel,
        name="finish",
        out_shape=(
            sds((ROWS, D), bf16),
            sds((ROWS, D), bf16),
            sds((1, D), f32),
            sds((D, 384), f32),
            sds((128, D), f32),
            sds((1, D), f32),
            sds((8, D), f32),
            sds((2, 4, 128, 2048), f32),
            sds((2, 4, 4, 128, 512), f32),
        ),
        in_specs=[vmem] * 7,
        out_specs=[hbm, hbm, vmem, vmem, vmem, vmem, vmem, hbm, hbm],
        scratch_shapes=[
            pltpu.VMEM((SLOTS, 128, 2048), f32),
            pltpu.VMEM((SLOTS, 4, 128, 512), f32),
            pltpu.SemaphoreType.DMA((2 * SLOTS + 2,)),
        ],
        compiler_params=pltpu.CompilerParams(vmem_limit_bytes=50 * 2**20),
    )(*(pltpu.with_memory_space_constraint(x, pltpu.VMEM) for x in results))


def local(
    tokens,
    cotangent,
    doc_lengths,
    group_slot,
    norm1_gain,
    qkv_weight,
    out_weight,
    norm2_gain,
    router_weight,
    expert_in,
    expert_out,
):
    results = block(
        tokens,
        norm1_gain[None],
        out_weight,
        qkv_weight,
        group_slot,
        cotangent,
        doc_lengths,
        norm2_gain[None],
        router_weight.T,
        expert_in.reshape(2, 4, 128, 2048),
        expert_out.reshape(2, 4, 4, 128, 512),
    )
    block_out, grad_tokens, one, grad_qkv, grad_w, two, grad_router, grad_in, grad_out = finish(
        *results
    )
    return (
        block_out,
        grad_tokens,
        one.reshape(D),
        grad_qkv,
        grad_w,
        two.reshape(D),
        grad_router.T,
        grad_in.reshape(2, 512, 2048),
        grad_out.reshape(2, 2048, 512),
    )


def solution(mesh):
    in_specs = (
        P(("dp", "tensor"), None),
        P(("dp", "tensor"), None),
        P("dp", None),
        P(("dp", "tensor"), None),
        P(),
        P(None, "tensor"),
        P("tensor", None),
        P(),
        P(),
        P("tensor", None, None),
        P("tensor", None, None),
    )
    out_specs = (
        P(("dp", "tensor"), None),
        P(("dp", "tensor"), None),
        P(),
        P(None, "tensor"),
        P("tensor", None),
        P(),
        P(),
        P("tensor", None, None),
        P("tensor", None, None),
    )
    return jax.shard_map(local, mesh=mesh, in_specs=in_specs, out_specs=out_specs, check_vma=False)
```

```python
from types import SimpleNamespace

import jax
import jax.numpy as jnp
from jax import lax
from jax.experimental import pallas as pl
from jax.experimental.pallas import tpu as pltpu
from jax.sharding import PartitionSpec as P

D = 512
GROUP = 32
ROWS = 512
LENGTH = 2048
N_DP = 32
PER = ROWS // N_DP
CHUNKS = 4
MESH = pl.DeviceIdType.MESH
NN = (((1,), (0,)), ((), ()))
NT = (((1,), (1,)), ((), ()))
TN = (((0,), (0,)), ((), ()))
f32 = jnp.float32
bf16 = jnp.bfloat16
eps = 1e-06


def dot(a, b, dims=NN):
    return lax.dot_general(a, b, dims, preferred_element_type=f32)


def normalize(values):
    factor = lax.rsqrt(jnp.mean(values * values, axis=-1, keepdims=True) + eps)
    return (values * factor, factor)


def norm_back(grad_hidden, normed, factor, gain_row):
    grad_normed = grad_hidden * gain_row
    inner_sum = jnp.mean(grad_normed * normed, axis=-1, keepdims=True)
    return factor * (grad_normed - normed * inner_sum)


def remote(src, dst, send_sem, recv_sem, device):
    return pltpu.make_async_remote_copy(
        src_ref=src,
        dst_ref=dst,
        send_sem=send_sem,
        recv_sem=recv_sem,
        device_id=device,
        device_id_type=MESH,
    )


def document_starts(lengths, base, count):
    place = lax.broadcasted_iota(jnp.int32, (1, count), 1) + base
    bound = jnp.int32(0)
    first = jnp.zeros((1, count), jnp.int32)
    for slot in range(9):
        bound = bound + lengths[0, slot]
        first = jnp.where(bound <= place, bound, first)
    return place, first


def allowed_pairs(place, first, key_base, keys):
    key = lax.broadcasted_iota(jnp.int32, (keys, place.shape[1]), 0)
    return (key >= first - key_base) & (key <= place - key_base)


def dp_exchange_start(source, target, send_sem, recv_sem):
    me, t = lax.axis_index("dp"), lax.axis_index("tensor")
    mine = pl.ds(pl.multiple_of(me * PER, PER), PER)

    def step(k, carry):
        peer = (me + k) % N_DP
        theirs = pl.ds(pl.multiple_of(peer * PER, PER), PER)
        remote(source.at[theirs], target.at[mine], send_sem, recv_sem, (peer, t)).start()
        return carry

    lax.fori_loop(1, N_DP, step, 0)
    target[mine] = source[mine]


def dp_exchange_wait(source, target, send_sem, recv_sem):
    me, t = lax.axis_index("dp"), lax.axis_index("tensor")
    most = pl.ds(0, (N_DP - 1) * PER)
    remote(source.at[most], target.at[most], send_sem, recv_sem, ((me + 1) % N_DP, t)).wait()


class Exchange:
    def __init__(self, make, count, total):
        self.make, self.count, self.total = make, count, total

    def start(self):
        for i in range(self.count):
            self.make(i).start()

    def wait(self):
        self.total.wait()


GELU_A = 0.7978845608028654
GELU_B = 0.044715

ARGUMENTS = {
    "tokens": ((ROWS, D), bf16),
    "gain_one": ((1, D), f32),
    "out_w": ((128, D), bf16),
    "qkv": ((D, 384), bf16),
    "slot": ((1, ROWS), jnp.int32),
    "cotangent": ((ROWS, D), bf16),
    "lengths": ((1, 9), jnp.int32),
    "gain_two": ((1, D), f32),
    "router": ((8, D), bf16),
}
WEIGHTS = ["expert_in", "expert_out"]
OUTPUTS = {
    "block_out": ((ROWS, D), bf16),
    "grad_tokens": ((ROWS, D), bf16),
    "grad_small": ((ROWS, D), bf16),
    "grad_floats": ((16, D), f32),
    "grad_gain": ((8, 128), f32),
    "grad_in": ((2, 4, 128, 2048), bf16),
    "grad_out": ((2, 4, 4, 128, 512), bf16),
}
SCRATCH = {
    "members": ((ROWS, D), bf16),
    "grad_update": ((ROWS, D), bf16),
    "residual": ((ROWS, D), f32),
    "hidden": ((LENGTH, D), bf16),
    "q2": ((2, LENGTH, 128), bf16),
    "k": ((LENGTH, 128), bf16),
    "v": ((LENGTH, 128), bf16),
    "k2t": ((2, 128, LENGTH), bf16),
    "v2t": ((2, 128, LENGTH), bf16),
    "lse": ((2, LENGTH), f32),
    "att_max": ((4, 2, 1, ROWS), f32),
    "att_sum": ((4, 2, 128, ROWS), f32),
    "att_own": ((LENGTH, 128), bf16),
    "att_pos": ((4, ROWS, 128), bf16),
    "out_all": ((4, 128, D), bf16),
    "perm": ((ROWS, ROWS), bf16),
    "sorted_grad": ((ROWS, D), bf16),
    "sorted_hidden": ((ROWS, D), bf16),
    "w_own": ((D, 384), bf16),
    "mix": ((128, ROWS), bf16),
    "mix_send": ((2, 8, PER, D), bf16),
    "rows_e": ((2, 2, 64, D), bf16),
    "ret_send": ((2, 2, 64, D), bf16),
    "ret": ((2, 8, PER, D), bf16),
    "act_s": ((4, 2, 64, 512), bf16),
    "pre_s": ((4, 2, 64, 512), bf16),
    "xz": ((2, 4, 64, 512), bf16),
    "gz": ((2, 4, 64, 512), bf16),
    "ay": ((2, 4, 64, 512), bf16),
    "cy": ((2, 4, 64, 512), bf16),
    "o_in": ((2, 4, 128, 512), bf16),
    "o_out": ((2, 4, 128, 512), bf16),
    "s2_in": ((2, 4, 128, 512), bf16),
    "s2_out": ((2, 4, 128, 512), bf16),
    "s3_send": ((2, 2, 128, 512), bf16),
    "s3_got": ((2, 2, 128, 512), bf16),
    "spread_s": ((ROWS, D), bf16),
    "spread_g": ((ROWS, D), bf16),
    "gm_s": ((ROWS, D), bf16),
    "gm_g": ((ROWS, D), bf16),
    "grad_res": ((ROWS, D), f32),
    "gatt_s": ((4, ROWS, 128), bf16),
    "gatt": ((LENGTH, 128), bf16),
    "outp_s": ((4, 128, D), bf16),
    "outp_g": ((3, 128, D), bf16),
    "outp_f": ((128, D), bf16),
    "do2": ((2, LENGTH, 128), bf16),
    "delta": ((2, LENGTH), f32),
    "dk": ((LENGTH, 128), f32),
    "dv": ((LENGTH, 128), f32),
    "gp": ((ROWS, 384), bf16),
    "back_s": ((4, ROWS, D), bf16),
    "back_g": ((3, ROWS, D), bf16),
    "back_f": ((ROWS, D), bf16),
    "small_s": ((ROWS, D), bf16),
    "small_g": ((ROWS, D), bf16),
    "floats_s": ((4, 16, D), f32),
    "floats_g": ((4, 4, 16, D), f32),
    "gain_s": ((8, 128), f32),
    "gain_g": ((4, 8, 128), f32),
    "gain_all": ((N_DP, 8, 128), f32),
}
N_SEMS = 66


def block_kernel(*refs):
    names = ["from_" + name for name in ARGUMENTS] + WEIGHTS + list(OUTPUTS)
    names += list(ARGUMENTS) + list(SCRATCH) + ["send", "recv", "load"]
    r = SimpleNamespace(**dict(zip(names, refs)))
    send, recv = r.send, r.recv
    me, t = lax.axis_index("dp"), lax.axis_index("tensor")
    y, z, xh = me // 8, (me // 2) % 4, me % 2
    sibling, cross, far = t + 1 - 2 * (t % 2), (t + 2) % 4, 3 - t
    loads = {
        name: pltpu.make_async_copy(getattr(r, "from_" + name), getattr(r, name), r.load.at[2 + i])
        for i, name in enumerate(ARGUMENTS)
    }
    for copy in loads.values():
        copy.start()
    barrier = pltpu.get_barrier_semaphore()
    for peer in (sibling, cross, far):
        pl.semaphore_signal(barrier, inc=1, device_id=(me, peer), device_id_type=MESH)

    def for_dp(body):
        def step(i, carry):
            body(i)
            return carry

        lax.fori_loop(1, N_DP, step, 0)

    def greet(i):
        pl.semaphore_signal(barrier, inc=1, device_id=((me + i) % N_DP, t), device_id_type=MESH)

    for_dp(greet)

    taken = [0]

    def sems(count):
        first = taken[0]
        taken[0] += count
        assert taken[0] <= N_SEMS
        return first

    def dp_id(y_, z_, x_):
        return y_ * 8 + z_ * 2 + x_

    def over(size, place, device, source, target, total):
        at = sems(1)

        def make(i):
            peer = (place + 1 + i) % size
            return remote(source(peer), target(place), send.at[at], recv.at[at], device(peer))

        every = remote(total, total, send.at[at], recv.at[at], device((place + 1) % size))
        return Exchange(make, size - 1, every)

    def over_tensor(source, target, total):
        return over(4, t, lambda p: (me, p), source, target, total)

    def over_y(source, target, total):
        return over(4, y, lambda p: (dp_id(p, z, xh), t), source, target, total)

    def over_z(source, target, total):
        return over(4, z, lambda p: (dp_id(y, p, xh), t), source, target, total)

    def over_x(source, target):
        return over(
            2, xh, lambda p: (dp_id(y, z, p), t), lambda p: source, lambda p: target, target
        )

    def pair(source, target, peer):
        at = sems(1)
        copy = remote(source, target, send.at[at], recv.at[at], (me, peer))
        return Exchange(lambda i: copy, 1, copy)

    class OverDp:
        def __init__(self, source, target):
            at = sems(1)
            self.args = (source, target, send.at[at], recv.at[at])

        def start(self):
            dp_exchange_start(*self.args)

        def wait(self):
            dp_exchange_wait(*self.args)

    three = pl.ds(0, 3)

    def rows_of(i):
        return pl.ds(pl.multiple_of(i * ROWS, ROWS), ROWS)

    def part(i):
        return pl.ds(pl.multiple_of(i * PER, PER), PER)

    load_in = pltpu.make_async_copy(r.expert_in, r.grad_in, r.load.at[0])
    load_out = pltpu.make_async_copy(r.expert_out, r.grad_out, r.load.at[1])

    step = ROWS // CHUNKS
    loads["tokens"].wait()
    loads["gain_one"].wait()
    for c in range(CHUNKS):
        values = r.tokens[c * step : (c + 1) * step, :].astype(f32)
        normed, _ = normalize(values)
        r.hidden[pl.ds(pl.multiple_of(t * ROWS + c * step, step), step), :] = (
            normed * r.gain_one[...]
        ).astype(bf16)
    loads["out_w"].wait()
    r.out_all[t] = r.out_w[...]
    pl.semaphore_wait(barrier, N_DP + 2)

    hid = sems(3 * CHUNKS)

    def hidden_copy(kind, owner, c, device):
        rows = pl.ds(pl.multiple_of(owner * ROWS + c * step, step), step)
        at = hid + kind * CHUNKS + c
        return remote(r.hidden.at[rows], r.hidden.at[rows], send.at[at], recv.at[at], (me, device))

    for c in range(CHUNKS):
        hidden_copy(1, t, c, cross).start()
        hidden_copy(0, t, c, sibling).start()

    for name in ("slot", "cotangent", "qkv", "lengths", "gain_two", "router"):
        loads[name].wait()
    place = lax.broadcasted_iota(jnp.int32, (ROWS, ROWS), 0)
    r.perm[...] = jnp.where(place == r.slot[...], 1.0, 0.0).astype(bf16)
    r.sorted_grad[...] = dot(r.perm[...], r.cotangent[...]).astype(bf16)

    lane = lax.broadcasted_iota(jnp.int32, (D, 128), 1)
    part_a, part_b, part_c = (r.qkv[:, 128 * i : 128 * (i + 1)].astype(f32) for i in range(3))
    r.w_own[:, 0:128] = jnp.where(lane < 64, part_a, part_b).astype(bf16)
    r.w_own[:, 128:256] = pltpu.roll(jnp.where(lane < 64, part_c, part_a), 64, 1).astype(bf16)
    r.w_own[:, 256:384] = jnp.where(lane < 64, part_b, part_c).astype(bf16)

    half = lax.broadcasted_iota(jnp.int32, (ROWS, 128), 1) < 64
    half_t = lax.broadcasted_iota(jnp.int32, (128, ROWS), 0) < 64

    def project(owner):
        rows = rows_of(owner)
        block = r.hidden[rows, :]
        queries = dot(block, r.w_own[:, 0:128]).astype(bf16).astype(f32) * 0.125
        r.q2[0, rows, :] = jnp.where(half, queries, 0.0).astype(bf16)
        r.q2[1, rows, :] = jnp.where(half, 0.0, queries).astype(bf16)
        keys = dot(block, r.w_own[:, 128:256])
        r.k[rows, :] = keys.astype(bf16)
        keys_t = keys.T
        r.k2t[0, :, rows] = jnp.where(half_t, keys_t, 0.0).astype(bf16)
        r.k2t[1, :, rows] = jnp.where(half_t, 0.0, keys_t).astype(bf16)
        values = dot(block, r.w_own[:, 256:384])
        r.v[rows, :] = values.astype(bf16)
        values_t = values.T
        r.v2t[0, :, rows] = jnp.where(half_t, values_t, 1.0).astype(bf16)
        r.v2t[1, :, rows] = jnp.where(half_t, 1.0, values_t).astype(bf16)

    out_exchange = over_tensor(
        lambda p: r.out_all.at[t], lambda p: r.out_all.at[t], r.out_all.at[three]
    )
    grad_exchange = OverDp(r.sorted_grad, r.grad_update)

    att_sems = sems(4)

    def att_copy(block, source, device):
        return remote(
            r.att_own.at[rows_of(block)],
            r.att_pos.at[source],
            send.at[att_sems + block],
            recv.at[att_sems + source],
            (me, device),
        )

    def attend(query_block, key_block, fresh):
        rows, keys_at = rows_of(query_block), rows_of(key_block)
        place, first = document_starts(r.lengths, query_block * ROWS, ROWS)
        allowed = allowed_pairs(place, first, key_block * ROWS, ROWS)
        keys = r.k[keys_at, :]
        for head in range(2):
            scores = jnp.where(allowed, dot(keys, r.q2[head, rows, :], NT), -1e30)
            maxima = jnp.max(scores, axis=0, keepdims=True)
            if not fresh:
                before = r.att_max[query_block, head]
                maxima = jnp.maximum(before, maxima)
            weights = jnp.exp(scores - maxima).astype(bf16)
            total = dot(r.v2t[head, :, keys_at], weights)
            if not fresh:
                total = r.att_sum[query_block, head] * jnp.exp(before - maxima) + total
            r.att_max[query_block, head] = maxima
            r.att_sum[query_block, head] = total

    def attended_block(block):
        rows = rows_of(block)
        sum_a, sum_b = r.att_sum[block, 0], r.att_sum[block, 1]
        norm_a, norm_b = sum_a[64:65], sum_b[0:1]
        attended = jnp.concatenate([sum_a[:64] / norm_a, sum_b[64:] / norm_b], axis=0)
        r.att_own[rows, :] = attended.T.astype(bf16)
        r.lse[0:1, rows] = r.att_max[block, 0] + jnp.log(norm_a)
        r.lse[1:2, rows] = r.att_max[block, 1] + jnp.log(norm_b)

        @pl.when(t == block)
        def _():
            r.att_pos[t] = r.att_own[rows, :]

        @pl.when(t != block)
        def _():
            att_copy(block, t, block).start()

    chip = t // 2
    project(t)
    for c in range(CHUNKS):
        hidden_copy(0, sibling, c, sibling).wait_recv()
    project(sibling)
    low, high = 2 * chip, 2 * chip + 1
    attend(low, low, True)
    attend(high, high, True)
    attend(high, low, False)
    for c in range(CHUNKS):
        hidden_copy(1, cross, c, cross).wait_recv()
        hidden_copy(2, cross, c, sibling).start()
        if c == CHUNKS - 2:
            grad_exchange.start()
    load_in.start()
    load_out.start()
    project(cross)
    out_exchange.start()
    for c in range(CHUNKS):
        hidden_copy(2, far, c, sibling).wait_recv()
    project(far)

    @pl.when(chip == 0)
    def _():
        attended_block(0)
        attended_block(1)

    def choose(first, second):
        return first + (second - first) * chip

    plan = (
        ((2, 2), (0, 0), True, True, None, 0),
        ((2, 0), (1, 1), False, True, None, None),
        ((2, 1), (1, 0), False, False, 2, 1),
        ((3, 3), (2, 0), True, False, None, None),
        ((3, 0), (2, 1), False, False, None, 2),
        ((3, 1), (3, 0), False, False, None, None),
        ((3, 2), (3, 1), False, False, 3, 3),
    )
    for pair_a, pair_b, fresh_a, fresh_b, end_a, end_b in plan:
        if fresh_a != fresh_b:
            block = choose(pair_a[0], pair_b[0])

            @pl.when(chip == (0 if fresh_a else 1))
            def _():
                for head in range(2):
                    r.att_max[block, head] = jnp.full((1, ROWS), -1e30, f32)
                    r.att_sum[block, head] = jnp.zeros((128, ROWS), f32)

        attend(
            choose(pair_a[0], pair_b[0]), choose(pair_a[1], pair_b[1]), fresh_a and fresh_b
        )
        if end_a == end_b:
            if end_a is not None:
                attended_block(end_a)
        else:
            for which, end in enumerate((end_a, end_b)):
                if end is not None:

                    @pl.when(chip == which)
                    def _():
                        attended_block(end)

    out_exchange.wait()
    for peer in (sibling, cross, far):
        att_copy(0, peer, peer).wait_recv()

    update = dot(r.att_pos[0], r.out_all[0])
    for i in range(1, 4):
        update = update + dot(r.att_pos[i], r.out_all[i])
    r.residual[...] = r.tokens[...].astype(f32) + update
    normed_two, _ = normalize(r.residual[...])
    hidden_two = (normed_two * r.gain_two[...]).astype(bf16)
    r.sorted_hidden[...] = dot(r.perm[...], hidden_two).astype(bf16)
    member_exchange = OverDp(r.sorted_hidden, r.members)
    member_exchange.start()

    for c in range(CHUNKS):
        hidden_copy(0, t, c, sibling).wait_send()
        hidden_copy(1, t, c, cross).wait_send()
        hidden_copy(2, cross, c, sibling).wait_send()
    for block in range(4):

        @pl.when(t != block)
        def _():
            att_copy(block, t, block).wait_send()

    router = jnp.concatenate(
        [r.router[...].astype(f32), jnp.zeros((8, D), f32)], axis=0
    ).astype(bf16)
    grad_exchange.wait()
    load_in.wait()
    load_out.wait()
    member_exchange.wait()

    def group_all(values, op):
        for shift in (16, 32, 64, 128, 256):
            values = op(values, pltpu.roll(values, shift, 1))
        return values

    logits = dot(router, r.members[...], NT)
    exponent = jnp.exp(logits - group_all(logits, jnp.maximum))
    mixing = exponent / group_all(exponent, jnp.add)
    lane = lax.broadcasted_iota(jnp.int32, (PER, ROWS), 1)
    own_group = lax.broadcasted_iota(jnp.int32, (PER, ROWS), 0) == lane % PER
    r.mix[...] = jnp.concatenate(
        [jnp.where(own_group, mixing[e : e + 1], 0.0) for e in range(8)], axis=0
    ).astype(bf16)
    r.mix_send[0] = dot(r.mix[...], r.members[...]).astype(bf16).reshape(8, PER, D)
    r.mix_send[1] = dot(r.mix[...], r.grad_update[...]).astype(bf16).reshape(8, PER, D)

    to_experts = over_tensor(
        lambda p: r.mix_send.at[:, pl.ds(2 * p, 2)],
        lambda p: r.rows_e.at[:, :, part(p)],
        r.rows_e.at[:, :, pl.ds(0, 3 * PER)],
    )
    to_experts.start()
    for kind in range(2):
        for e in range(2):
            r.rows_e[kind, e, part(t), :] = r.mix_send[kind, 2 * t + e]

    to_experts.wait()
    share_x = over_z(lambda p: r.rows_e.at[0], lambda p: r.xz.at[:, p], r.xz.at[:, three])
    share_c = over_y(lambda p: r.rows_e.at[1], lambda p: r.cy.at[:, p], r.cy.at[:, three])
    share_x.start()
    share_c.start()

    def share_factors(e):
        return (
            over_z(lambda p: r.pre_s.at[p, e], lambda p: r.gz.at[e, p], r.gz.at[e, three]),
            over_y(lambda p: r.act_s.at[p, e], lambda p: r.ay.at[e, p], r.ay.at[e, three]),
        )

    share_pre, share_act = zip(*(share_factors(e) for e in range(2)))
    for e in range(2):
        rows_x, rows_c = r.rows_e[0, e], r.rows_e[1, e]

        def in_cols(q):
            return r.grad_in[e, :, :, pl.ds(512 * q, 512)].reshape(D, 512)

        def out_rows(q):
            return r.grad_out[e, q].reshape(512, D)

        for q in range(4):
            pre = dot(rows_x, in_cols(q))
            inner = GELU_A * (pre + GELU_B * pre * pre * pre)
            th = jnp.tanh(inner)
            r.act_s[q, e] = (0.5 * pre * (1.0 + th)).astype(bf16)
            slope = 0.5 * (1.0 + th) + 0.5 * pre * (1.0 - th * th) * (
                GELU_A * (1.0 + 3.0 * GELU_B * pre * pre)
            )
            grad_act = dot(rows_c, out_rows(q), NT)
            r.pre_s[q, e] = (grad_act * slope).astype(bf16)
        made = dot(r.act_s[0, e], out_rows(0))
        mixed = dot(r.pre_s[0, e], in_cols(0), NT)
        for q in range(1, 4):
            made = made + dot(r.act_s[q, e], out_rows(q))
            mixed = mixed + dot(r.pre_s[q, e], in_cols(q), NT)
        r.ret_send[0, e] = made.astype(bf16)
        r.ret_send[1, e] = mixed.astype(bf16)
        if e == 0:
            share_pre[e].start()
            share_act[e].start()

    from_experts = over_tensor(
        lambda p: r.ret_send.at[:, :, part(p)],
        lambda p: r.ret.at[:, pl.ds(2 * p, 2)],
        r.ret.at[:, pl.ds(0, 6)],
    )
    from_experts.start()
    share_pre[1].start()
    share_act[1].start()
    for kind in range(2):
        for e in range(2):
            r.ret[kind, 2 * t + e] = r.ret_send[kind, e, part(t), :]
    r.xz[:, z] = r.rows_e[0]
    r.cy[:, y] = r.rows_e[1]
    for e in range(2):
        r.gz[e, z] = r.pre_s[z, e]
        r.ay[e, y] = r.act_s[y, e]

    def ring_sums(e):
        return (
            over_y(lambda p: r.o_in.at[e, p], lambda p: r.s2_in.at[e, p], r.s2_in.at[e, three]),
            over_z(lambda p: r.o_out.at[e, p], lambda p: r.s2_out.at[e, p], r.s2_out.at[e, three]),
        )

    sum_in, sum_out = zip(*(ring_sums(e) for e in range(2)))

    def multiply_factors(e):
        share_pre[e].wait()
        share_act[e].wait()
        product = dot(r.xz[e].reshape(256, D), r.gz[e].reshape(256, 512), TN)
        r.o_in[e] = product.astype(bf16).reshape(4, 128, 512)
        product = dot(r.ay[e].reshape(256, 512), r.cy[e].reshape(256, D), TN)
        r.o_out[e] = product.astype(bf16).reshape(4, 128, 512)
        if e == 0:
            sum_in[e].start()
            sum_out[e].start()
        r.s2_in[e, y] = r.o_in[e, y]
        r.s2_out[e, z] = r.o_out[e, z]

    share_x.wait()
    share_c.wait()
    multiply_factors(0)
    from_experts.wait()

    produced, mixed_back = r.ret[0].reshape(8 * PER, D), r.ret[1].reshape(8 * PER, D)
    scores = dot(produced, r.grad_update[...], NT) + dot(mixed_back, r.members[...], NT)
    grad_mixing = jnp.concatenate(
        [
            jnp.sum(
                jnp.where(own_group, scores[PER * e : PER * (e + 1)], 0.0), axis=0, keepdims=True
            )
            for e in range(8)
        ]
        + [jnp.zeros((8, ROWS), f32)],
        axis=0,
    )
    inner_sum = group_all(mixing * grad_mixing, jnp.add)
    grad_logits = (mixing * (grad_mixing - inner_sum)).astype(bf16)
    gm = dot(r.mix[...], mixed_back, TN) + dot(grad_logits, router, TN)
    r.gm_s[...] = gm.astype(bf16)
    gm_exchange = OverDp(r.gm_s, r.gm_g)
    gm_exchange.start()

    multiply_factors(1)
    r.spread_s[...] = dot(r.mix[...], produced, TN).astype(bf16)
    r.floats_s[0] = dot(grad_logits, r.members[...])
    spread_exchange = OverDp(r.spread_s, r.spread_g)

    cols_z = pl.ds(pl.multiple_of(z * 512, 512), 512)

    def gather_first_ring(e):
        def in_part(p):
            return r.grad_in.at[e, y, :, cols_z]

        def out_part(p):
            return r.grad_out.at[e, y, z]

        return (
            over_z(in_part, in_part, r.grad_in.at[e, y, :, pl.ds(0, 3 * 512)]),
            over_y(out_part, out_part, r.grad_out.at[e, three, z]),
        )

    both = [over_x(r.s3_send.at[e], r.s3_got.at[e]) for e in range(2)]
    all_in_z, all_out_y = zip(*(gather_first_ring(e) for e in range(2)))

    def reduce_ring(e):
        sum_in[e].wait()
        sum_out[e].wait()
        total = r.s2_in[e, 0].astype(f32)
        other = r.s2_out[e, 0].astype(f32)
        for i in range(1, 4):
            total = total + r.s2_in[e, i].astype(f32)
            other = other + r.s2_out[e, i].astype(f32)
        r.s3_send[e, 0] = total.astype(bf16)
        r.s3_send[e, 1] = other.astype(bf16)
        both[e].start()

    def reduce_pair(e):
        both[e].wait()
        total = r.s3_send[e, 0].astype(f32) + r.s3_got[e, 0].astype(f32)
        other = r.s3_send[e, 1].astype(f32) + r.s3_got[e, 1].astype(f32)
        r.grad_in[e, y, :, cols_z] = total.astype(bf16)
        r.grad_out[e, y, z] = other.astype(bf16)
        all_in_z[e].start()
        all_out_y[e].start()

    ring_sems = sems(12)

    def ring_copy(axis, direction, kind, e):
        at = y if axis == 0 else z
        to = (at + 1 + 2 * direction) % 4
        owner = at if kind == 0 else (at + 3 - 2 * direction) % 4
        index = ring_sems + 6 * axis + (2 * direction + e if kind == 0 else 4 + direction)
        if axis == 0:
            here, device = r.grad_in.at[e, owner], (dp_id(to, z, xh), t)
        else:
            here, device = r.grad_out.at[e, :, owner], (dp_id(y, to, xh), t)
        return remote(here, here, send.at[index], recv.at[index], device)

    def gather_second(e):
        all_in_z[e].wait()
        all_out_y[e].wait()
        for direction in (e, 1 - e):
            for axis in range(2):
                ring_copy(axis, direction, 0, e).start()

    def hand_on(e):
        for axis in range(2):
            ring_copy(axis, e, 0, e).wait_recv()
            ring_copy(axis, e, 1, e).start()

    def gather_end(e):
        for axis in range(2):
            ring_copy(axis, e, 0, e).wait_send()
            ring_copy(axis, 1 - e, 0, e).wait()
            ring_copy(axis, e, 1, e).wait()

    gm_exchange.wait()
    sum_in[1].start()
    sum_out[1].start()
    reduce_ring(0)
    normed_two, scale_two = normalize(r.residual[...])
    grad_hidden_two = dot(r.perm[...], r.gm_g[...], TN).astype(bf16).astype(f32)
    r.floats_s[0, 8:9, :] = jnp.sum(grad_hidden_two * normed_two, axis=0, keepdims=True)
    r.grad_res[...] = r.cotangent[...].astype(f32) + norm_back(
        grad_hidden_two, normed_two, scale_two, r.gain_two[...]
    )
    grad_low = r.grad_res[...].astype(bf16)
    for i in range(4):
        r.gatt_s[i] = dot(grad_low, r.out_all[i], NT).astype(bf16)

    att_exchange = over_tensor(lambda p: r.gatt_s.at[p], lambda p: r.gatt.at[rows_of(p)], r.gatt.at[pl.ds(0, 3 * ROWS)])
    att_exchange.start()
    spread_exchange.start()
    r.gatt[rows_of(t), :] = r.gatt_s[t]
    for i in range(4):
        r.outp_s[i] = dot(r.att_pos[i], grad_low, TN).astype(bf16)
    outp = [
        pair(r.outp_s.at[sibling], r.outp_g.at[0], sibling),
        pair(r.outp_s.at[far], r.outp_g.at[1], sibling),
        pair(r.outp_f, r.outp_g.at[2], cross),
    ]
    outp[0].start()
    outp[1].start()
    floats_exchange = [
        over_tensor(lambda p: r.floats_s.at[0], lambda p: r.floats_g.at[0, p], r.floats_g.at[0, three]),
        over_y(lambda p: r.floats_s.at[1], lambda p: r.floats_g.at[1, p], r.floats_g.at[1, three]),
        over_z(lambda p: r.floats_s.at[2], lambda p: r.floats_g.at[2, p], r.floats_g.at[2, three]),
        over_x(r.floats_s.at[3], r.floats_g.at[3, 0]),
    ]
    floats_exchange[0].start()
    r.floats_g[0, t] = r.floats_s[0]

    def outp_forward():
        outp[1].wait()
        r.outp_f[...] = (r.outp_s[cross].astype(f32) + r.outp_g[1].astype(f32)).astype(bf16)
        outp[2].start()

    def floats_step(i):
        floats_exchange[i].wait()
        got = r.floats_g[i, 0]
        for j in range(1, 4):
            got = got + r.floats_g[i, j]
        r.floats_s[i + 1] = got
        floats_exchange[i + 1].start()
        if i == 0:
            r.floats_g[1, y] = got
        if i == 1:
            r.floats_g[2, z] = got

    def floats_end():
        floats_exchange[3].wait()
        r.grad_floats[...] = r.floats_s[3] + r.floats_g[3, 0]

    def block_out_store():
        spread_exchange.wait()
        update = dot(r.perm[...], r.spread_g[...], TN).astype(bf16).astype(f32)
        r.block_out[...] = (r.residual[...] + update).astype(bf16)

    att_exchange.wait()
    reduce_pair(0)
    reduce_ring(1)
    for i in range(4):
        rows = pl.ds(i * ROWS, ROWS)
        grads = r.gatt[rows, :].astype(f32)
        r.do2[0, rows, :] = jnp.where(half, grads, 0.0).astype(bf16)
        r.do2[1, rows, :] = jnp.where(half, 0.0, grads).astype(bf16)
        product = (grads * r.att_own[rows, :].astype(f32)).T
        r.delta[0:1, rows] = jnp.sum(product[:64], axis=0, keepdims=True)
        r.delta[1:2, rows] = jnp.sum(product[64:], axis=0, keepdims=True)

    back_sibling, back_far = sems(1), sems(1)
    back_cross = sems(1)

    def to_sibling(block, first, slot):
        return remote(
            r.back_s.at[block], r.back_g.at[slot], send.at[first], recv.at[first], (me, sibling)
        )

    def to_cross():
        return remote(
            r.back_f, r.back_g.at[2], send.at[back_cross], recv.at[back_cross], (me, cross)
        )

    def back_send(block):
        @pl.when(block == sibling)
        def _():
            to_sibling(block, back_sibling, 0).start()

        @pl.when(block == far)
        def _():
            to_sibling(block, back_far, 1).start()

    def back_forward(block):
        @pl.when(block == cross)
        def _():
            to_sibling(block, back_far, 1).wait_recv()
            r.back_f[...] = (r.back_s[block].astype(f32) + r.back_g[1].astype(f32)).astype(bf16)
            to_cross().start()

    between = {
        (3, 0): lambda: (outp_forward(),),
        (3, 1): lambda: (floats_step(0),),
        (3, 2): lambda: (reduce_pair(1),),
        (3, 3): lambda: (gather_second(0),),
        (2, 0): lambda: (back_forward(3), floats_step(1),),
        (2, 2): lambda: (floats_step(2), block_out_store(),),
        (1, 0): lambda: (back_forward(2), gather_second(1),),
        (1, 1): lambda: (floats_end(),),
        (0, 0): lambda: (back_forward(1),),
    }
    grad_qkv = None
    rows = ROWS
    for block in (3, 2, 1, 0):
        base = block * rows
        here = pl.ds(base, rows)
        place, first = document_starts(r.lengths, base, rows)
        grad_q = jnp.zeros((128, rows), f32)
        for index in range(block + 1):
            there = pl.ds(index * rows, rows)
            allowed = allowed_pairs(place, first, index * rows, rows)
            keys, values = r.k[there, :], r.v[there, :]
            grad_v, grad_k = None, None
            for head in range(2):
                queries, grads = r.q2[head, here, :], r.do2[head, here, :]
                scores = dot(keys, queries, NT)
                shifted = jnp.where(allowed, scores - r.lse[head : head + 1, here], -1e30)
                weights = jnp.exp(shifted)
                grad_w = dot(values, grads, NT)
                grad_s = (weights * (grad_w - r.delta[head : head + 1, here])).astype(bf16)
                term = dot(weights.astype(bf16), grads)
                grad_v = term if grad_v is None else grad_v + term
                term = dot(grad_s, queries)
                grad_k = term if grad_k is None else grad_k + term
                grad_q = grad_q + dot(r.k2t[head, :, there], grad_s)
            if block == 3:
                r.dk[there, :] = grad_k
                r.dv[there, :] = grad_v
            else:
                r.dk[there, :] += grad_k
                r.dv[there, :] += grad_v
            if (block, index) in between:
                between[block, index]()
        r.gp[:, 0:128] = (grad_q * 0.125).T.astype(bf16)
        r.gp[:, 128:256] = r.dk[here, :].astype(bf16)
        r.gp[:, 256:384] = r.dv[here, :].astype(bf16)
        r.back_s[block] = dot(r.gp[...], r.w_own[...], NT).astype(bf16)
        back_send(block)
        term = dot(r.hidden[base : base + rows, :], r.gp[...], TN)
        grad_qkv = term if grad_qkv is None else grad_qkv + term

    outp[0].wait()
    outp[2].wait()
    lane = lax.broadcasted_iota(jnp.int32, (D, 128), 1)
    part_q, part_k, part_v = (grad_qkv[:, 128 * i : 128 * (i + 1)] for i in range(3))
    part_k = pltpu.roll(part_k, 64, 1)
    r.small_s[:, 0:128] = jnp.where(lane < 64, part_q, part_k).astype(bf16)
    r.small_s[:, 128:256] = jnp.where(lane < 64, part_v, part_q).astype(bf16)
    r.small_s[:, 256:384] = jnp.where(lane < 64, part_k, part_v).astype(bf16)
    out_sum = r.outp_s[t].astype(f32) + r.outp_g[0].astype(f32) + r.outp_g[2].astype(f32)
    for i in range(4):
        r.small_s[128 * i : 128 * (i + 1), 384:512] = out_sum[:, 128 * i : 128 * (i + 1)].astype(
            bf16
        )
    small_exchange = OverDp(r.small_s, r.small_g)
    back_forward(0)
    small_exchange.start()
    hand_on(0)
    hand_on(1)

    normed_one, scale_one = normalize(r.tokens[...].astype(f32))
    to_sibling(sibling, back_sibling, 0).wait_recv()
    to_cross().wait_recv()
    grad_hidden_one = (
        r.back_s[t].astype(f32) + r.back_g[0].astype(f32) + r.back_g[2].astype(f32)
    )
    gain = jnp.sum(grad_hidden_one * normed_one, axis=0, keepdims=True)
    r.gain_s[...] = jnp.concatenate(
        [gain[:, 128 * i : 128 * (i + 1)] for i in range(4)] + [jnp.zeros((4, 128), f32)], axis=0
    )
    gain_exchange = over_tensor(lambda p: r.gain_s, lambda p: r.gain_g.at[p], r.gain_g.at[three])
    gain_exchange.start()
    r.gain_g[t] = r.gain_s[...]
    r.grad_tokens[...] = (
        r.grad_res[...] + norm_back(grad_hidden_one, normed_one, scale_one, r.gain_one[...])
    ).astype(bf16)

    small_exchange.wait()
    total = r.small_g[0:PER, :].astype(f32)
    for i in range(1, N_DP):
        total = total + r.small_g[PER * i : PER * (i + 1), :].astype(f32)
    r.grad_small[part(me), :] = total.astype(bf16)

    at_small, at_gain = sems(1), sems(1)

    def small_copy(i, here):
        peer = (me + i) % N_DP
        return remote(here, here, send.at[at_small], recv.at[at_small], (peer, t))

    def gain_copy(i, here):
        peer = (me + i) % N_DP
        return remote(here, here, send.at[at_gain], recv.at[at_gain], (peer, t))

    for_dp(lambda i: small_copy(i, r.grad_small.at[part(me)]).start())
    gain_exchange.wait()
    r.gain_all[me] = (r.gain_g[0] + r.gain_g[1]) + (r.gain_g[2] + r.gain_g[3])
    for_dp(lambda i: gain_copy(i, r.gain_all.at[me]).start())

    to_sibling(sibling, back_sibling, 0).wait_send()
    to_sibling(far, back_far, 1).wait_send()
    to_cross().wait_send()

    for e in range(2):
        gather_end(e)

    small_copy(1, r.grad_small.at[pl.ds(0, (N_DP - 1) * PER)]).wait()
    gain_copy(1, r.gain_all.at[pl.ds(0, N_DP - 1)]).wait()
    gain_total = r.gain_all[0]
    for i in range(1, N_DP):
        gain_total = gain_total + r.gain_all[i]
    r.grad_gain[...] = gain_total


def block(*args):
    vmem = pl.BlockSpec(memory_space=pltpu.VMEM)
    hbm = pl.BlockSpec(memory_space=pltpu.HBM)
    held = [
        (pltpu.SMEM if name == "lengths" else pltpu.VMEM)(*shape)
        for name, shape in ARGUMENTS.items()
    ]
    dma = pltpu.SemaphoreType.DMA
    return pl.pallas_call(
        block_kernel,
        name="block",
        out_shape=tuple(pltpu.VMEM(*shape) for shape in OUTPUTS.values()),
        in_specs=[hbm] * (len(ARGUMENTS) + len(WEIGHTS)),
        out_specs=[vmem] * len(OUTPUTS),
        scratch_shapes=held
        + [pltpu.VMEM(*shape) for shape in SCRATCH.values()]
        + [dma((N_SEMS,)), dma((N_SEMS,)), dma((2 + len(ARGUMENTS),))],
        compiler_params=pltpu.CompilerParams(
            collective_id=0, has_side_effects=True, vmem_limit_bytes=50 * 2**20
        ),
    )(*args)


SLOTS = 4


def finish_kernel(
    block_in,
    tokens_in,
    small,
    floats,
    gain,
    in_low,
    out_low,
    block_out,
    grad_tokens,
    grad_one,
    grad_qkv,
    grad_w,
    grad_two,
    grad_router,
    grad_in,
    grad_out,
    wide_in,
    wide_out,
    sems,
):
    whole = [
        pltpu.make_async_copy(block_in, block_out, sems.at[2 * SLOTS]),
        pltpu.make_async_copy(tokens_in, grad_tokens, sems.at[2 * SLOTS + 1]),
    ]
    for copy in whole:
        copy.start()
    parts = [(e, i) for e in range(2) for i in range(4)]

    def copies(n):
        e, i = parts[n]
        slot = n % SLOTS
        return (
            pltpu.make_async_copy(wide_in.at[slot], grad_in.at[e, i], sems.at[slot]),
            pltpu.make_async_copy(wide_out.at[slot], grad_out.at[e, i], sems.at[SLOTS + slot]),
        )

    for n, (e, i) in enumerate(parts):
        slot = n % SLOTS
        to_in, to_out = copies(n)
        if n >= SLOTS:
            copies(n - SLOTS)[0].wait()
        wide_in[slot] = in_low[e, i].astype(f32)
        to_in.start()
        if n >= SLOTS:
            copies(n - SLOTS)[1].wait()
        wide_out[slot] = out_low[e, i].astype(f32)
        to_out.start()
    grad_qkv[...] = small[:, :384].astype(f32)
    for i in range(4):
        cols = slice(128 * i, 128 * (i + 1))
        grad_w[:, cols] = small[cols, 384:512].astype(f32)
        grad_one[:, cols] = gain[i : i + 1, :]
    grad_two[...] = floats[8:9, :]
    grad_router[...] = floats[0:8, :]
    for n in range(len(parts) - SLOTS, len(parts)):
        for copy in copies(n):
            copy.wait()
    for copy in whole:
        copy.wait()


def finish(*results):
    sds = jax.ShapeDtypeStruct
    vmem = pl.BlockSpec(memory_space=pltpu.VMEM)
    hbm = pl.BlockSpec(memory_space=pl.ANY)
    return pl.pallas_call(
        finish_kernel,
        name="finish",
        out_shape=(
            sds((ROWS, D), bf16),
            sds((ROWS, D), bf16),
            sds((1, D), f32),
            sds((D, 384), f32),
            sds((128, D), f32),
            sds((1, D), f32),
            sds((8, D), f32),
            sds((2, 4, 128, 2048), f32),
            sds((2, 4, 4, 128, 512), f32),
        ),
        in_specs=[vmem] * 7,
        out_specs=[hbm, hbm, vmem, vmem, vmem, vmem, vmem, hbm, hbm],
        scratch_shapes=[
            pltpu.VMEM((SLOTS, 128, 2048), f32),
            pltpu.VMEM((SLOTS, 4, 128, 512), f32),
            pltpu.SemaphoreType.DMA((2 * SLOTS + 2,)),
        ],
        compiler_params=pltpu.CompilerParams(vmem_limit_bytes=50 * 2**20),
    )(*(pltpu.with_memory_space_constraint(x, pltpu.VMEM) for x in results))


def local(
    tokens,
    cotangent,
    doc_lengths,
    group_slot,
    norm1_gain,
    qkv_weight,
    out_weight,
    norm2_gain,
    router_weight,
    expert_in,
    expert_out,
):
    results = block(
        tokens,
        norm1_gain[None],
        out_weight,
        qkv_weight,
        group_slot,
        cotangent,
        doc_lengths,
        norm2_gain[None],
        router_weight.T,
        expert_in.reshape(2, 4, 128, 2048),
        expert_out.reshape(2, 4, 4, 128, 512),
    )
    block_out, grad_tokens, one, grad_qkv, grad_w, two, grad_router, grad_in, grad_out = finish(
        *results
    )
    return (
        block_out,
        grad_tokens,
        one.reshape(D),
        grad_qkv,
        grad_w,
        two.reshape(D),
        grad_router.T,
        grad_in.reshape(2, 512, 2048),
        grad_out.reshape(2, 2048, 512),
    )


def solution(mesh):
    in_specs = (
        P(("dp", "tensor"), None),
        P(("dp", "tensor"), None),
        P("dp", None),
        P(("dp", "tensor"), None),
        P(),
        P(None, "tensor"),
        P("tensor", None),
        P(),
        P(),
        P("tensor", None, None),
        P("tensor", None, None),
    )
    out_specs = (
        P(("dp", "tensor"), None),
        P(("dp", "tensor"), None),
        P(),
        P(None, "tensor"),
        P("tensor", None),
        P(),
        P(),
        P("tensor", None, None),
        P("tensor", None, None),
    )
    return jax.shard_map(local, mesh=mesh, in_specs=in_specs, out_specs=out_specs, check_vma=False)
```

```python
from types import SimpleNamespace

import jax
import jax.numpy as jnp
from jax import lax
from jax.experimental import pallas as pl
from jax.experimental.pallas import tpu as pltpu
from jax.sharding import PartitionSpec as P

D = 512
GROUP = 32
ROWS = 512
LENGTH = 2048
N_DP = 32
PER = ROWS // N_DP
CHUNKS = 4
MESH = pl.DeviceIdType.MESH
NN = (((1,), (0,)), ((), ()))
NT = (((1,), (1,)), ((), ()))
TN = (((0,), (0,)), ((), ()))
f32 = jnp.float32
bf16 = jnp.bfloat16
eps = 1e-06


def dot(a, b, dims=NN):
    return lax.dot_general(a, b, dims, preferred_element_type=f32)


def normalize(values):
    factor = lax.rsqrt(jnp.mean(values * values, axis=-1, keepdims=True) + eps)
    return (values * factor, factor)


def norm_back(grad_hidden, normed, factor, gain_row):
    grad_normed = grad_hidden * gain_row
    inner_sum = jnp.mean(grad_normed * normed, axis=-1, keepdims=True)
    return factor * (grad_normed - normed * inner_sum)


def remote(src, dst, send_sem, recv_sem, device):
    return pltpu.make_async_remote_copy(
        src_ref=src,
        dst_ref=dst,
        send_sem=send_sem,
        recv_sem=recv_sem,
        device_id=device,
        device_id_type=MESH,
    )


def document_starts(lengths, base, count):
    place = lax.broadcasted_iota(jnp.int32, (1, count), 1) + base
    bound = jnp.int32(0)
    first = jnp.zeros((1, count), jnp.int32)
    for slot in range(9):
        bound = bound + lengths[0, slot]
        first = jnp.where(bound <= place, bound, first)
    return place, first


def allowed_pairs(place, first, key_base, keys):
    key = lax.broadcasted_iota(jnp.int32, (keys, place.shape[1]), 0)
    return (key >= first - key_base) & (key <= place - key_base)


def dp_exchange_start(source, target, send_sem, recv_sem):
    me, t = lax.axis_index("dp"), lax.axis_index("tensor")
    mine = pl.ds(pl.multiple_of(me * PER, PER), PER)

    def step(k, carry):
        peer = (me + k) % N_DP
        theirs = pl.ds(pl.multiple_of(peer * PER, PER), PER)
        remote(source.at[theirs], target.at[mine], send_sem, recv_sem, (peer, t)).start()
        return carry

    lax.fori_loop(1, N_DP, step, 0)
    target[mine] = source[mine]


def dp_exchange_wait(source, target, send_sem, recv_sem):
    me, t = lax.axis_index("dp"), lax.axis_index("tensor")
    most = pl.ds(0, (N_DP - 1) * PER)
    remote(source.at[most], target.at[most], send_sem, recv_sem, ((me + 1) % N_DP, t)).wait()


class Exchange:
    def __init__(self, make, count, total):
        self.make, self.count, self.total = make, count, total

    def start(self):
        for i in range(self.count):
            self.make(i).start()

    def wait(self):
        self.total.wait()


GELU_A = 0.7978845608028654
GELU_B = 0.044715

ARGUMENTS = {
    "tokens": ((ROWS, D), bf16),
    "gain_one": ((1, D), f32),
    "out_w": ((128, D), bf16),
    "qkv": ((D, 384), bf16),
    "slot": ((1, ROWS), jnp.int32),
    "cotangent": ((ROWS, D), bf16),
    "lengths": ((1, 9), jnp.int32),
    "gain_two": ((1, D), f32),
    "router": ((8, D), bf16),
}
WEIGHTS = ["expert_in", "expert_out"]
OUTPUTS = {
    "block_out": ((ROWS, D), bf16),
    "grad_tokens": ((ROWS, D), bf16),
    "grad_small": ((ROWS, D), bf16),
    "grad_floats": ((16, D), f32),
    "grad_gain": ((8, 128), f32),
    "grad_in": ((2, 4, 128, 2048), bf16),
    "grad_out": ((2, 4, 4, 128, 512), bf16),
}
SCRATCH = {
    "members": ((ROWS, D), bf16),
    "grad_update": ((ROWS, D), bf16),
    "residual": ((ROWS, D), f32),
    "hidden": ((LENGTH, D), bf16),
    "q2": ((2, LENGTH, 128), bf16),
    "k": ((LENGTH, 128), bf16),
    "v": ((LENGTH, 128), bf16),
    "k2t": ((2, 128, LENGTH), bf16),
    "v2t": ((2, 128, LENGTH), bf16),
    "lse": ((2, LENGTH), f32),
    "att_max": ((4, 2, 1, ROWS), f32),
    "att_sum": ((4, 2, 128, ROWS), f32),
    "att_own": ((LENGTH, 128), bf16),
    "att_pos": ((4, ROWS, 128), bf16),
    "out_all": ((4, 128, D), bf16),
    "perm": ((ROWS, ROWS), bf16),
    "sorted_grad": ((ROWS, D), bf16),
    "sorted_hidden": ((ROWS, D), bf16),
    "w_own": ((D, 384), bf16),
    "mix": ((128, ROWS), bf16),
    "mix_send": ((2, 8, PER, D), bf16),
    "rows_e": ((2, 2, 64, D), bf16),
    "ret_send": ((2, 2, 64, D), bf16),
    "ret": ((2, 8, PER, D), bf16),
    "act_s": ((4, 2, 64, 512), bf16),
    "pre_s": ((4, 2, 64, 512), bf16),
    "xz": ((2, 4, 64, 512), bf16),
    "gz": ((2, 4, 64, 512), bf16),
    "ay": ((2, 4, 64, 512), bf16),
    "cy": ((2, 4, 64, 512), bf16),
    "o_in": ((2, 4, 128, 512), bf16),
    "o_out": ((2, 4, 128, 512), bf16),
    "s2_in": ((2, 4, 128, 512), bf16),
    "s2_out": ((2, 4, 128, 512), bf16),
    "s3_send": ((2, 2, 128, 512), bf16),
    "s3_got": ((2, 2, 128, 512), bf16),
    "spread_s": ((ROWS, D), bf16),
    "spread_g": ((ROWS, D), bf16),
    "gm_s": ((ROWS, D), bf16),
    "gm_g": ((ROWS, D), bf16),
    "grad_res": ((ROWS, D), f32),
    "gatt_s": ((4, ROWS, 128), bf16),
    "gatt": ((LENGTH, 128), bf16),
    "outp_s": ((4, 128, D), bf16),
    "outp_g": ((3, 128, D), bf16),
    "outp_f": ((128, D), bf16),
    "do2": ((2, LENGTH, 128), bf16),
    "delta": ((2, LENGTH), f32),
    "dk": ((LENGTH, 128), f32),
    "dv": ((LENGTH, 128), f32),
    "gp": ((ROWS, 384), bf16),
    "back_s": ((4, ROWS, D), bf16),
    "back_g": ((3, ROWS, D), bf16),
    "back_f": ((ROWS, D), bf16),
    "small_s": ((ROWS, D), bf16),
    "small_g": ((ROWS, D), bf16),
    "floats_s": ((4, 16, D), f32),
    "floats_g": ((4, 4, 16, D), f32),
    "gain_s": ((8, 128), f32),
    "gain_g": ((4, 8, 128), f32),
    "gain_all": ((N_DP, 8, 128), f32),
}
N_SEMS = 66


def block_kernel(*refs):
    names = ["from_" + name for name in ARGUMENTS] + WEIGHTS + list(OUTPUTS)
    names += list(ARGUMENTS) + list(SCRATCH) + ["send", "recv", "load"]
    r = SimpleNamespace(**dict(zip(names, refs)))
    send, recv = r.send, r.recv
    me, t = lax.axis_index("dp"), lax.axis_index("tensor")
    y, z, xh = me // 8, (me // 2) % 4, me % 2
    sibling, cross, far = t + 1 - 2 * (t % 2), (t + 2) % 4, 3 - t
    loads = {
        name: pltpu.make_async_copy(getattr(r, "from_" + name), getattr(r, name), r.load.at[2 + i])
        for i, name in enumerate(ARGUMENTS)
    }
    for copy in loads.values():
        copy.start()
    barrier = pltpu.get_barrier_semaphore()
    for peer in (sibling, cross, far):
        pl.semaphore_signal(barrier, inc=1, device_id=(me, peer), device_id_type=MESH)

    def for_dp(body):
        def step(i, carry):
            body(i)
            return carry

        lax.fori_loop(1, N_DP, step, 0)

    def greet(i):
        pl.semaphore_signal(barrier, inc=1, device_id=((me + i) % N_DP, t), device_id_type=MESH)

    for_dp(greet)

    taken = [0]

    def sems(count):
        first = taken[0]
        taken[0] += count
        assert taken[0] <= N_SEMS
        return first

    def dp_id(y_, z_, x_):
        return y_ * 8 + z_ * 2 + x_

    def over(size, place, device, source, target, total):
        at = sems(1)

        def make(i):
            peer = (place + 1 + i) % size
            return remote(source(peer), target(place), send.at[at], recv.at[at], device(peer))

        every = remote(total, total, send.at[at], recv.at[at], device((place + 1) % size))
        return Exchange(make, size - 1, every)

    def over_tensor(source, target, total):
        return over(4, t, lambda p: (me, p), source, target, total)

    def over_y(source, target, total):
        return over(4, y, lambda p: (dp_id(p, z, xh), t), source, target, total)

    def over_z(source, target, total):
        return over(4, z, lambda p: (dp_id(y, p, xh), t), source, target, total)

    def over_x(source, target):
        return over(
            2, xh, lambda p: (dp_id(y, z, p), t), lambda p: source, lambda p: target, target
        )

    def pair(source, target, peer):
        at = sems(1)
        copy = remote(source, target, send.at[at], recv.at[at], (me, peer))
        return Exchange(lambda i: copy, 1, copy)

    class OverDp:
        def __init__(self, source, target):
            at = sems(1)
            self.args = (source, target, send.at[at], recv.at[at])

        def start(self):
            dp_exchange_start(*self.args)

        def wait(self):
            dp_exchange_wait(*self.args)

    three = pl.ds(0, 3)

    def rows_of(i):
        return pl.ds(pl.multiple_of(i * ROWS, ROWS), ROWS)

    def part(i):
        return pl.ds(pl.multiple_of(i * PER, PER), PER)

    load_in = pltpu.make_async_copy(r.expert_in, r.grad_in, r.load.at[0])
    load_out = pltpu.make_async_copy(r.expert_out, r.grad_out, r.load.at[1])

    step = ROWS // CHUNKS
    loads["tokens"].wait()
    loads["gain_one"].wait()
    for c in range(CHUNKS):
        values = r.tokens[c * step : (c + 1) * step, :].astype(f32)
        normed, _ = normalize(values)
        r.hidden[pl.ds(pl.multiple_of(t * ROWS + c * step, step), step), :] = (
            normed * r.gain_one[...]
        ).astype(bf16)
    loads["out_w"].wait()
    r.out_all[t] = r.out_w[...]
    pl.semaphore_wait(barrier, N_DP + 2)

    hid = sems(3 * CHUNKS)

    def hidden_copy(kind, owner, c, device):
        rows = pl.ds(pl.multiple_of(owner * ROWS + c * step, step), step)
        at = hid + kind * CHUNKS + c
        return remote(r.hidden.at[rows], r.hidden.at[rows], send.at[at], recv.at[at], (me, device))

    for c in range(CHUNKS):
        hidden_copy(1, t, c, cross).start()
        hidden_copy(0, t, c, sibling).start()

    for name in ("slot", "cotangent", "qkv", "lengths", "gain_two", "router"):
        loads[name].wait()
    place = lax.broadcasted_iota(jnp.int32, (ROWS, ROWS), 0)
    r.perm[...] = jnp.where(place == r.slot[...], 1.0, 0.0).astype(bf16)
    r.sorted_grad[...] = dot(r.perm[...], r.cotangent[...]).astype(bf16)

    lane = lax.broadcasted_iota(jnp.int32, (D, 128), 1)
    part_a, part_b, part_c = (r.qkv[:, 128 * i : 128 * (i + 1)].astype(f32) for i in range(3))
    r.w_own[:, 0:128] = jnp.where(lane < 64, part_a, part_b).astype(bf16)
    r.w_own[:, 128:256] = pltpu.roll(jnp.where(lane < 64, part_c, part_a), 64, 1).astype(bf16)
    r.w_own[:, 256:384] = jnp.where(lane < 64, part_b, part_c).astype(bf16)

    half = lax.broadcasted_iota(jnp.int32, (ROWS, 128), 1) < 64
    half_t = lax.broadcasted_iota(jnp.int32, (128, ROWS), 0) < 64

    def project(owner):
        rows = rows_of(owner)
        block = r.hidden[rows, :]
        queries = dot(block, r.w_own[:, 0:128]).astype(bf16).astype(f32) * 0.125
        r.q2[0, rows, :] = jnp.where(half, queries, 0.0).astype(bf16)
        r.q2[1, rows, :] = jnp.where(half, 0.0, queries).astype(bf16)
        keys = dot(block, r.w_own[:, 128:256])
        r.k[rows, :] = keys.astype(bf16)
        keys_t = keys.T
        r.k2t[0, :, rows] = jnp.where(half_t, keys_t, 0.0).astype(bf16)
        r.k2t[1, :, rows] = jnp.where(half_t, 0.0, keys_t).astype(bf16)
        values = dot(block, r.w_own[:, 256:384])
        r.v[rows, :] = values.astype(bf16)
        values_t = values.T
        r.v2t[0, :, rows] = jnp.where(half_t, values_t, 1.0).astype(bf16)
        r.v2t[1, :, rows] = jnp.where(half_t, 1.0, values_t).astype(bf16)

    out_exchange = over_tensor(
        lambda p: r.out_all.at[t], lambda p: r.out_all.at[t], r.out_all.at[three]
    )
    grad_exchange = OverDp(r.sorted_grad, r.grad_update)

    att_sems = sems(4)

    def att_copy(block, source, device):
        return remote(
            r.att_own.at[rows_of(block)],
            r.att_pos.at[source],
            send.at[att_sems + block],
            recv.at[att_sems + source],
            (me, device),
        )

    def attend(query_block, key_block, fresh):
        rows, keys_at = rows_of(query_block), rows_of(key_block)
        place, first = document_starts(r.lengths, query_block * ROWS, ROWS)
        allowed = allowed_pairs(place, first, key_block * ROWS, ROWS)
        keys = r.k[keys_at, :]
        for head in range(2):
            scores = jnp.where(allowed, dot(keys, r.q2[head, rows, :], NT), -1e30)
            maxima = jnp.max(scores, axis=0, keepdims=True)
            if not fresh:
                before = r.att_max[query_block, head]
                maxima = jnp.maximum(before, maxima)
            weights = jnp.exp(scores - maxima).astype(bf16)
            total = dot(r.v2t[head, :, keys_at], weights)
            if not fresh:
                total = r.att_sum[query_block, head] * jnp.exp(before - maxima) + total
            r.att_max[query_block, head] = maxima
            r.att_sum[query_block, head] = total

    def attended_block(block):
        rows = rows_of(block)
        sum_a, sum_b = r.att_sum[block, 0], r.att_sum[block, 1]
        norm_a, norm_b = sum_a[64:65], sum_b[0:1]
        attended = jnp.concatenate([sum_a[:64] / norm_a, sum_b[64:] / norm_b], axis=0)
        r.att_own[rows, :] = attended.T.astype(bf16)
        r.lse[0:1, rows] = r.att_max[block, 0] + jnp.log(norm_a)
        r.lse[1:2, rows] = r.att_max[block, 1] + jnp.log(norm_b)

        @pl.when(t == block)
        def _():
            r.att_pos[t] = r.att_own[rows, :]

        @pl.when(t != block)
        def _():
            att_copy(block, t, block).start()

    chip = t // 2
    project(t)
    for c in range(CHUNKS):
        hidden_copy(0, sibling, c, sibling).wait_recv()
    project(sibling)
    low, high = 2 * chip, 2 * chip + 1
    attend(low, low, True)
    attend(high, high, True)
    attend(high, low, False)
    for c in range(CHUNKS):
        hidden_copy(1, cross, c, cross).wait_recv()
        hidden_copy(2, cross, c, sibling).start()
        if c == CHUNKS - 2:
            grad_exchange.start()
    load_in.start()
    load_out.start()
    project(cross)
    out_exchange.start()
    for c in range(CHUNKS):
        hidden_copy(2, far, c, sibling).wait_recv()
    project(far)

    @pl.when(chip == 0)
    def _():
        attended_block(0)
        attended_block(1)

    def choose(first, second):
        return first + (second - first) * chip

    plan = (
        ((2, 2), (0, 0), True, True, None, 0),
        ((2, 0), (1, 1), False, True, None, None),
        ((2, 1), (1, 0), False, False, 2, 1),
        ((3, 3), (2, 0), True, False, None, None),
        ((3, 0), (2, 1), False, False, None, 2),
        ((3, 1), (3, 0), False, False, None, None),
        ((3, 2), (3, 1), False, False, 3, 3),
    )
    for pair_a, pair_b, fresh_a, fresh_b, end_a, end_b in plan:
        if fresh_a != fresh_b:
            block = choose(pair_a[0], pair_b[0])

            @pl.when(chip == (0 if fresh_a else 1))
            def _():
                for head in range(2):
                    r.att_max[block, head] = jnp.full((1, ROWS), -1e30, f32)
                    r.att_sum[block, head] = jnp.zeros((128, ROWS), f32)

        attend(
            choose(pair_a[0], pair_b[0]), choose(pair_a[1], pair_b[1]), fresh_a and fresh_b
        )
        if end_a == end_b:
            if end_a is not None:
                attended_block(end_a)
        else:
            for which, end in enumerate((end_a, end_b)):
                if end is not None:

                    @pl.when(chip == which)
                    def _():
                        attended_block(end)

    out_exchange.wait()
    for peer in (sibling, cross, far):
        att_copy(0, peer, peer).wait_recv()

    update = dot(r.att_pos[0], r.out_all[0])
    for i in range(1, 4):
        update = update + dot(r.att_pos[i], r.out_all[i])
    r.residual[...] = r.tokens[...].astype(f32) + update
    normed_two, _ = normalize(r.residual[...])
    hidden_two = (normed_two * r.gain_two[...]).astype(bf16)
    r.sorted_hidden[...] = dot(r.perm[...], hidden_two).astype(bf16)
    member_exchange = OverDp(r.sorted_hidden, r.members)
    member_exchange.start()

    for c in range(CHUNKS):
        hidden_copy(0, t, c, sibling).wait_send()
        hidden_copy(1, t, c, cross).wait_send()
        hidden_copy(2, cross, c, sibling).wait_send()
    for block in range(4):

        @pl.when(t != block)
        def _():
            att_copy(block, t, block).wait_send()

    router = jnp.concatenate(
        [r.router[...].astype(f32), jnp.zeros((8, D), f32)], axis=0
    ).astype(bf16)
    grad_exchange.wait()
    load_in.wait()
    load_out.wait()
    member_exchange.wait()

    def group_all(values, op):
        for shift in (16, 32, 64, 128, 256):
            values = op(values, pltpu.roll(values, shift, 1))
        return values

    logits = dot(router, r.members[...], NT)
    exponent = jnp.exp(logits - group_all(logits, jnp.maximum))
    mixing = exponent / group_all(exponent, jnp.add)
    lane = lax.broadcasted_iota(jnp.int32, (PER, ROWS), 1)
    own_group = lax.broadcasted_iota(jnp.int32, (PER, ROWS), 0) == lane % PER
    r.mix[...] = jnp.concatenate(
        [jnp.where(own_group, mixing[e : e + 1], 0.0) for e in range(8)], axis=0
    ).astype(bf16)
    r.mix_send[0] = dot(r.mix[...], r.members[...]).astype(bf16).reshape(8, PER, D)
    r.mix_send[1] = dot(r.mix[...], r.grad_update[...]).astype(bf16).reshape(8, PER, D)

    to_experts = over_tensor(
        lambda p: r.mix_send.at[:, pl.ds(2 * p, 2)],
        lambda p: r.rows_e.at[:, :, part(p)],
        r.rows_e.at[:, :, pl.ds(0, 3 * PER)],
    )
    to_experts.start()
    for kind in range(2):
        for e in range(2):
            r.rows_e[kind, e, part(t), :] = r.mix_send[kind, 2 * t + e]

    to_experts.wait()
    share_x = over_z(lambda p: r.rows_e.at[0], lambda p: r.xz.at[:, p], r.xz.at[:, three])
    share_c = over_y(lambda p: r.rows_e.at[1], lambda p: r.cy.at[:, p], r.cy.at[:, three])
    share_x.start()
    share_c.start()

    def share_factors(e):
        return (
            over_z(lambda p: r.pre_s.at[p, e], lambda p: r.gz.at[e, p], r.gz.at[e, three]),
            over_y(lambda p: r.act_s.at[p, e], lambda p: r.ay.at[e, p], r.ay.at[e, three]),
        )

    share_pre, share_act = zip(*(share_factors(e) for e in range(2)))
    for e in range(2):
        rows_x, rows_c = r.rows_e[0, e], r.rows_e[1, e]

        def in_cols(q):
            return r.grad_in[e, :, :, pl.ds(512 * q, 512)].reshape(D, 512)

        def out_rows(q):
            return r.grad_out[e, q].reshape(512, D)

        for q in range(4):
            pre = dot(rows_x, in_cols(q))
            inner = GELU_A * (pre + GELU_B * pre * pre * pre)
            th = jnp.tanh(inner)
            r.act_s[q, e] = (0.5 * pre * (1.0 + th)).astype(bf16)
            slope = 0.5 * (1.0 + th) + 0.5 * pre * (1.0 - th * th) * (
                GELU_A * (1.0 + 3.0 * GELU_B * pre * pre)
            )
            grad_act = dot(rows_c, out_rows(q), NT)
            r.pre_s[q, e] = (grad_act * slope).astype(bf16)
        made = dot(r.act_s[0, e], out_rows(0))
        mixed = dot(r.pre_s[0, e], in_cols(0), NT)
        for q in range(1, 4):
            made = made + dot(r.act_s[q, e], out_rows(q))
            mixed = mixed + dot(r.pre_s[q, e], in_cols(q), NT)
        r.ret_send[0, e] = made.astype(bf16)
        r.ret_send[1, e] = mixed.astype(bf16)
        if e == 0:
            share_pre[e].start()
            share_act[e].start()

    from_experts = over_tensor(
        lambda p: r.ret_send.at[:, :, part(p)],
        lambda p: r.ret.at[:, pl.ds(2 * p, 2)],
        r.ret.at[:, pl.ds(0, 6)],
    )
    from_experts.start()
    share_pre[1].start()
    share_act[1].start()
    for kind in range(2):
        for e in range(2):
            r.ret[kind, 2 * t + e] = r.ret_send[kind, e, part(t), :]
    r.xz[:, z] = r.rows_e[0]
    r.cy[:, y] = r.rows_e[1]
    for e in range(2):
        r.gz[e, z] = r.pre_s[z, e]
        r.ay[e, y] = r.act_s[y, e]

    def ring_sums(e):
        return (
            over_y(lambda p: r.o_in.at[e, p], lambda p: r.s2_in.at[e, p], r.s2_in.at[e, three]),
            over_z(lambda p: r.o_out.at[e, p], lambda p: r.s2_out.at[e, p], r.s2_out.at[e, three]),
        )

    sum_in, sum_out = zip(*(ring_sums(e) for e in range(2)))

    def multiply_factors(e):
        share_pre[e].wait()
        share_act[e].wait()
        product = dot(r.xz[e].reshape(256, D), r.gz[e].reshape(256, 512), TN)
        r.o_in[e] = product.astype(bf16).reshape(4, 128, 512)
        product = dot(r.ay[e].reshape(256, 512), r.cy[e].reshape(256, D), TN)
        r.o_out[e] = product.astype(bf16).reshape(4, 128, 512)
        if e == 0:
            sum_in[e].start()
            sum_out[e].start()
        r.s2_in[e, y] = r.o_in[e, y]
        r.s2_out[e, z] = r.o_out[e, z]

    share_x.wait()
    share_c.wait()
    multiply_factors(0)
    from_experts.wait()

    produced, mixed_back = r.ret[0].reshape(8 * PER, D), r.ret[1].reshape(8 * PER, D)
    scores = dot(produced, r.grad_update[...], NT) + dot(mixed_back, r.members[...], NT)
    grad_mixing = jnp.concatenate(
        [
            jnp.sum(
                jnp.where(own_group, scores[PER * e : PER * (e + 1)], 0.0), axis=0, keepdims=True
            )
            for e in range(8)
        ]
        + [jnp.zeros((8, ROWS), f32)],
        axis=0,
    )
    inner_sum = group_all(mixing * grad_mixing, jnp.add)
    grad_logits = (mixing * (grad_mixing - inner_sum)).astype(bf16)
    gm = dot(r.mix[...], mixed_back, TN) + dot(grad_logits, router, TN)
    r.gm_s[...] = gm.astype(bf16)
    gm_exchange = OverDp(r.gm_s, r.gm_g)
    gm_exchange.start()

    multiply_factors(1)
    r.spread_s[...] = dot(r.mix[...], produced, TN).astype(bf16)
    r.floats_s[0] = dot(grad_logits, r.members[...])
    spread_exchange = OverDp(r.spread_s, r.spread_g)

    cols_z = pl.ds(pl.multiple_of(z * 512, 512), 512)

    def gather_first_ring(e):
        def in_part(p):
            return r.grad_in.at[e, y, :, cols_z]

        def out_part(p):
            return r.grad_out.at[e, y, z]

        return (
            over_z(in_part, in_part, r.grad_in.at[e, y, :, pl.ds(0, 3 * 512)]),
            over_y(out_part, out_part, r.grad_out.at[e, three, z]),
        )

    both = [over_x(r.s3_send.at[e], r.s3_got.at[e]) for e in range(2)]
    all_in_z, all_out_y = zip(*(gather_first_ring(e) for e in range(2)))

    def reduce_ring(e):
        sum_in[e].wait()
        sum_out[e].wait()
        total = r.s2_in[e, 0].astype(f32)
        other = r.s2_out[e, 0].astype(f32)
        for i in range(1, 4):
            total = total + r.s2_in[e, i].astype(f32)
            other = other + r.s2_out[e, i].astype(f32)
        r.s3_send[e, 0] = total.astype(bf16)
        r.s3_send[e, 1] = other.astype(bf16)
        both[e].start()

    def reduce_pair(e):
        both[e].wait()
        total = r.s3_send[e, 0].astype(f32) + r.s3_got[e, 0].astype(f32)
        other = r.s3_send[e, 1].astype(f32) + r.s3_got[e, 1].astype(f32)
        r.grad_in[e, y, :, cols_z] = total.astype(bf16)
        r.grad_out[e, y, z] = other.astype(bf16)
        all_in_z[e].start()
        all_out_y[e].start()

    ring_sems = sems(12)

    def ring_copy(axis, direction, kind, e):
        at = y if axis == 0 else z
        to = (at + 1 + 2 * direction) % 4
        owner = at if kind == 0 else (at + 3 - 2 * direction) % 4
        index = ring_sems + 6 * axis + (2 * direction + e if kind == 0 else 4 + direction)
        if axis == 0:
            here, device = r.grad_in.at[e, owner], (dp_id(to, z, xh), t)
        else:
            here, device = r.grad_out.at[e, :, owner], (dp_id(y, to, xh), t)
        return remote(here, here, send.at[index], recv.at[index], device)

    def gather_second(e):
        all_in_z[e].wait()
        all_out_y[e].wait()
        for direction in (e, 1 - e):
            for axis in range(2):
                ring_copy(axis, direction, 0, e).start()

    def hand_on(e):
        for axis in range(2):
            ring_copy(axis, e, 0, e).wait_recv()
            ring_copy(axis, e, 1, e).start()

    def gather_end(e):
        for axis in range(2):
            ring_copy(axis, e, 0, e).wait_send()
            ring_copy(axis, 1 - e, 0, e).wait()
            ring_copy(axis, e, 1, e).wait()

    gm_exchange.wait()
    sum_in[1].start()
    sum_out[1].start()
    reduce_ring(0)
    normed_two, scale_two = normalize(r.residual[...])
    grad_hidden_two = dot(r.perm[...], r.gm_g[...], TN).astype(bf16).astype(f32)
    r.floats_s[0, 8:9, :] = jnp.sum(grad_hidden_two * normed_two, axis=0, keepdims=True)
    r.grad_res[...] = r.cotangent[...].astype(f32) + norm_back(
        grad_hidden_two, normed_two, scale_two, r.gain_two[...]
    )
    grad_low = r.grad_res[...].astype(bf16)
    for i in range(4):
        r.gatt_s[i] = dot(grad_low, r.out_all[i], NT).astype(bf16)

    att_exchange = over_tensor(lambda p: r.gatt_s.at[p], lambda p: r.gatt.at[rows_of(p)], r.gatt.at[pl.ds(0, 3 * ROWS)])
    att_exchange.start()
    spread_exchange.start()
    r.gatt[rows_of(t), :] = r.gatt_s[t]
    for i in range(4):
        r.outp_s[i] = dot(r.att_pos[i], grad_low, TN).astype(bf16)
    outp = [
        pair(r.outp_s.at[sibling], r.outp_g.at[0], sibling),
        pair(r.outp_s.at[far], r.outp_g.at[1], sibling),
        pair(r.outp_f, r.outp_g.at[2], cross),
    ]
    outp[0].start()
    outp[1].start()
    floats_exchange = [
        over_tensor(lambda p: r.floats_s.at[0], lambda p: r.floats_g.at[0, p], r.floats_g.at[0, three]),
        over_y(lambda p: r.floats_s.at[1], lambda p: r.floats_g.at[1, p], r.floats_g.at[1, three]),
        over_z(lambda p: r.floats_s.at[2], lambda p: r.floats_g.at[2, p], r.floats_g.at[2, three]),
        over_x(r.floats_s.at[3], r.floats_g.at[3, 0]),
    ]
    floats_exchange[0].start()
    r.floats_g[0, t] = r.floats_s[0]

    def outp_forward():
        outp[1].wait()
        r.outp_f[...] = (r.outp_s[cross].astype(f32) + r.outp_g[1].astype(f32)).astype(bf16)
        outp[2].start()

    def floats_step(i):
        floats_exchange[i].wait()
        got = r.floats_g[i, 0]
        for j in range(1, 4):
            got = got + r.floats_g[i, j]
        r.floats_s[i + 1] = got
        floats_exchange[i + 1].start()
        if i == 0:
            r.floats_g[1, y] = got
        if i == 1:
            r.floats_g[2, z] = got

    def floats_end():
        floats_exchange[3].wait()
        r.grad_floats[...] = r.floats_s[3] + r.floats_g[3, 0]

    def block_out_store():
        spread_exchange.wait()
        update = dot(r.perm[...], r.spread_g[...], TN).astype(bf16).astype(f32)
        r.block_out[...] = (r.residual[...] + update).astype(bf16)

    att_exchange.wait()
    reduce_pair(0)
    reduce_ring(1)
    for i in range(4):
        rows = pl.ds(i * ROWS, ROWS)
        grads = r.gatt[rows, :].astype(f32)
        r.do2[0, rows, :] = jnp.where(half, grads, 0.0).astype(bf16)
        r.do2[1, rows, :] = jnp.where(half, 0.0, grads).astype(bf16)
        product = (grads * r.att_own[rows, :].astype(f32)).T
        r.delta[0:1, rows] = jnp.sum(product[:64], axis=0, keepdims=True)
        r.delta[1:2, rows] = jnp.sum(product[64:], axis=0, keepdims=True)

    back_sibling, back_far = sems(1), sems(1)
    back_cross = sems(1)

    def to_sibling(block, first, slot):
        return remote(
            r.back_s.at[block], r.back_g.at[slot], send.at[first], recv.at[first], (me, sibling)
        )

    def to_cross():
        return remote(
            r.back_f, r.back_g.at[2], send.at[back_cross], recv.at[back_cross], (me, cross)
        )

    def back_send(block):
        @pl.when(block == sibling)
        def _():
            to_sibling(block, back_sibling, 0).start()

        @pl.when(block == far)
        def _():
            to_sibling(block, back_far, 1).start()

    def back_forward(block):
        @pl.when(block == cross)
        def _():
            to_sibling(block, back_far, 1).wait_recv()
            r.back_f[...] = (r.back_s[block].astype(f32) + r.back_g[1].astype(f32)).astype(bf16)
            to_cross().start()

    between = {
        (3, 0): lambda: (outp_forward(),),
        (3, 1): lambda: (floats_step(0),),
        (3, 2): lambda: (reduce_pair(1),),
        (3, 3): lambda: (gather_second(0),),
        (2, 0): lambda: (back_forward(3), floats_step(1),),
        (2, 2): lambda: (gather_second(1), floats_step(2), block_out_store(),),
        (1, 0): lambda: (back_forward(2),),
        (1, 1): lambda: (floats_end(),),
        (0, 0): lambda: (back_forward(1),),
    }
    grad_qkv = None
    rows = ROWS
    for block in (3, 2, 1, 0):
        base = block * rows
        here = pl.ds(base, rows)
        place, first = document_starts(r.lengths, base, rows)
        grad_q = jnp.zeros((128, rows), f32)
        for index in range(block + 1):
            there = pl.ds(index * rows, rows)
            allowed = allowed_pairs(place, first, index * rows, rows)
            keys, values = r.k[there, :], r.v[there, :]
            grad_v, grad_k = None, None
            for head in range(2):
                queries, grads = r.q2[head, here, :], r.do2[head, here, :]
                scores = dot(keys, queries, NT)
                shifted = jnp.where(allowed, scores - r.lse[head : head + 1, here], -1e30)
                weights = jnp.exp(shifted)
                grad_w = dot(values, grads, NT)
                grad_s = (weights * (grad_w - r.delta[head : head + 1, here])).astype(bf16)
                term = dot(weights.astype(bf16), grads)
                grad_v = term if grad_v is None else grad_v + term
                term = dot(grad_s, queries)
                grad_k = term if grad_k is None else grad_k + term
                grad_q = grad_q + dot(r.k2t[head, :, there], grad_s)
            if block == 3:
                r.dk[there, :] = grad_k
                r.dv[there, :] = grad_v
            else:
                r.dk[there, :] += grad_k
                r.dv[there, :] += grad_v
            if (block, index) in between:
                between[block, index]()
        r.gp[:, 0:128] = (grad_q * 0.125).T.astype(bf16)
        r.gp[:, 128:256] = r.dk[here, :].astype(bf16)
        r.gp[:, 256:384] = r.dv[here, :].astype(bf16)
        r.back_s[block] = dot(r.gp[...], r.w_own[...], NT).astype(bf16)
        back_send(block)
        term = dot(r.hidden[base : base + rows, :], r.gp[...], TN)
        grad_qkv = term if grad_qkv is None else grad_qkv + term

    outp[0].wait()
    outp[2].wait()
    lane = lax.broadcasted_iota(jnp.int32, (D, 128), 1)
    part_q, part_k, part_v = (grad_qkv[:, 128 * i : 128 * (i + 1)] for i in range(3))
    part_k = pltpu.roll(part_k, 64, 1)
    r.small_s[:, 0:128] = jnp.where(lane < 64, part_q, part_k).astype(bf16)
    r.small_s[:, 128:256] = jnp.where(lane < 64, part_v, part_q).astype(bf16)
    r.small_s[:, 256:384] = jnp.where(lane < 64, part_k, part_v).astype(bf16)
    out_sum = r.outp_s[t].astype(f32) + r.outp_g[0].astype(f32) + r.outp_g[2].astype(f32)
    for i in range(4):
        r.small_s[128 * i : 128 * (i + 1), 384:512] = out_sum[:, 128 * i : 128 * (i + 1)].astype(
            bf16
        )
    small_exchange = OverDp(r.small_s, r.small_g)
    back_forward(0)
    small_exchange.start()
    hand_on(0)
    hand_on(1)

    normed_one, scale_one = normalize(r.tokens[...].astype(f32))
    to_sibling(sibling, back_sibling, 0).wait_recv()
    to_cross().wait_recv()
    grad_hidden_one = (
        r.back_s[t].astype(f32) + r.back_g[0].astype(f32) + r.back_g[2].astype(f32)
    )
    gain = jnp.sum(grad_hidden_one * normed_one, axis=0, keepdims=True)
    r.gain_s[...] = jnp.concatenate(
        [gain[:, 128 * i : 128 * (i + 1)] for i in range(4)] + [jnp.zeros((4, 128), f32)], axis=0
    )
    gain_exchange = over_tensor(lambda p: r.gain_s, lambda p: r.gain_g.at[p], r.gain_g.at[three])
    gain_exchange.start()
    r.gain_g[t] = r.gain_s[...]
    r.grad_tokens[...] = (
        r.grad_res[...] + norm_back(grad_hidden_one, normed_one, scale_one, r.gain_one[...])
    ).astype(bf16)

    small_exchange.wait()
    total = r.small_g[0:PER, :].astype(f32)
    for i in range(1, N_DP):
        total = total + r.small_g[PER * i : PER * (i + 1), :].astype(f32)
    r.grad_small[part(me), :] = total.astype(bf16)

    at_small, at_gain = sems(1), sems(1)

    def small_copy(i, here):
        peer = (me + i) % N_DP
        return remote(here, here, send.at[at_small], recv.at[at_small], (peer, t))

    def gain_copy(i, here):
        peer = (me + i) % N_DP
        return remote(here, here, send.at[at_gain], recv.at[at_gain], (peer, t))

    for_dp(lambda i: small_copy(i, r.grad_small.at[part(me)]).start())
    gain_exchange.wait()
    r.gain_all[me] = (r.gain_g[0] + r.gain_g[1]) + (r.gain_g[2] + r.gain_g[3])
    for_dp(lambda i: gain_copy(i, r.gain_all.at[me]).start())

    to_sibling(sibling, back_sibling, 0).wait_send()
    to_sibling(far, back_far, 1).wait_send()
    to_cross().wait_send()

    for e in range(2):
        gather_end(e)

    small_copy(1, r.grad_small.at[pl.ds(0, (N_DP - 1) * PER)]).wait()
    gain_copy(1, r.gain_all.at[pl.ds(0, N_DP - 1)]).wait()
    gain_total = r.gain_all[0]
    for i in range(1, N_DP):
        gain_total = gain_total + r.gain_all[i]
    r.grad_gain[...] = gain_total


def block(*args):
    vmem = pl.BlockSpec(memory_space=pltpu.VMEM)
    hbm = pl.BlockSpec(memory_space=pltpu.HBM)
    held = [
        (pltpu.SMEM if name == "lengths" else pltpu.VMEM)(*shape)
        for name, shape in ARGUMENTS.items()
    ]
    dma = pltpu.SemaphoreType.DMA
    return pl.pallas_call(
        block_kernel,
        name="block",
        out_shape=tuple(pltpu.VMEM(*shape) for shape in OUTPUTS.values()),
        in_specs=[hbm] * (len(ARGUMENTS) + len(WEIGHTS)),
        out_specs=[vmem] * len(OUTPUTS),
        scratch_shapes=held
        + [pltpu.VMEM(*shape) for shape in SCRATCH.values()]
        + [dma((N_SEMS,)), dma((N_SEMS,)), dma((2 + len(ARGUMENTS),))],
        compiler_params=pltpu.CompilerParams(
            collective_id=0, has_side_effects=True, vmem_limit_bytes=50 * 2**20
        ),
    )(*args)


SLOTS = 8


def finish_kernel(
    block_in,
    tokens_in,
    small,
    floats,
    gain,
    in_low,
    out_low,
    block_out,
    grad_tokens,
    grad_one,
    grad_qkv,
    grad_w,
    grad_two,
    grad_router,
    grad_in,
    grad_out,
    wide_in,
    wide_out,
    sems,
):
    whole = [
        pltpu.make_async_copy(block_in, block_out, sems.at[2 * SLOTS]),
        pltpu.make_async_copy(tokens_in, grad_tokens, sems.at[2 * SLOTS + 1]),
    ]
    for copy in whole:
        copy.start()
    parts = [(e, i) for e in range(2) for i in range(4)]

    def copies(n):
        e, i = parts[n]
        slot = n % SLOTS
        return (
            pltpu.make_async_copy(wide_in.at[slot], grad_in.at[e, i], sems.at[slot]),
            pltpu.make_async_copy(wide_out.at[slot], grad_out.at[e, i], sems.at[SLOTS + slot]),
        )

    for n, (e, i) in enumerate(parts):
        slot = n % SLOTS
        to_in, to_out = copies(n)
        if n >= SLOTS:
            copies(n - SLOTS)[0].wait()
        wide_in[slot] = in_low[e, i].astype(f32)
        to_in.start()
        if n >= SLOTS:
            copies(n - SLOTS)[1].wait()
        wide_out[slot] = out_low[e, i].astype(f32)
        to_out.start()
    grad_qkv[...] = small[:, :384].astype(f32)
    for i in range(4):
        cols = slice(128 * i, 128 * (i + 1))
        grad_w[:, cols] = small[cols, 384:512].astype(f32)
        grad_one[:, cols] = gain[i : i + 1, :]
    grad_two[...] = floats[8:9, :]
    grad_router[...] = floats[0:8, :]
    for n in range(len(parts) - SLOTS, len(parts)):
        for copy in copies(n):
            copy.wait()
    for copy in whole:
        copy.wait()


def finish(*results):
    sds = jax.ShapeDtypeStruct
    vmem = pl.BlockSpec(memory_space=pltpu.VMEM)
    hbm = pl.BlockSpec(memory_space=pl.ANY)
    return pl.pallas_call(
        finish_kernel,
        name="finish",
        out_shape=(
            sds((ROWS, D), bf16),
            sds((ROWS, D), bf16),
            sds((1, D), f32),
            sds((D, 384), f32),
            sds((128, D), f32),
            sds((1, D), f32),
            sds((8, D), f32),
            sds((2, 4, 128, 2048), f32),
            sds((2, 4, 4, 128, 512), f32),
        ),
        in_specs=[vmem] * 7,
        out_specs=[hbm, hbm, vmem, vmem, vmem, vmem, vmem, hbm, hbm],
        scratch_shapes=[
            pltpu.VMEM((SLOTS, 128, 2048), f32),
            pltpu.VMEM((SLOTS, 4, 128, 512), f32),
            pltpu.SemaphoreType.DMA((2 * SLOTS + 2,)),
        ],
        compiler_params=pltpu.CompilerParams(vmem_limit_bytes=50 * 2**20),
    )(*(pltpu.with_memory_space_constraint(x, pltpu.VMEM) for x in results))


def local(
    tokens,
    cotangent,
    doc_lengths,
    group_slot,
    norm1_gain,
    qkv_weight,
    out_weight,
    norm2_gain,
    router_weight,
    expert_in,
    expert_out,
):
    results = block(
        tokens,
        norm1_gain[None],
        out_weight,
        qkv_weight,
        group_slot,
        cotangent,
        doc_lengths,
        norm2_gain[None],
        router_weight.T,
        expert_in.reshape(2, 4, 128, 2048),
        expert_out.reshape(2, 4, 4, 128, 512),
    )
    block_out, grad_tokens, one, grad_qkv, grad_w, two, grad_router, grad_in, grad_out = finish(
        *results
    )
    return (
        block_out,
        grad_tokens,
        one.reshape(D),
        grad_qkv,
        grad_w,
        two.reshape(D),
        grad_router.T,
        grad_in.reshape(2, 512, 2048),
        grad_out.reshape(2, 2048, 512),
    )


def solution(mesh):
    in_specs = (
        P(("dp", "tensor"), None),
        P(("dp", "tensor"), None),
        P("dp", None),
        P(("dp", "tensor"), None),
        P(),
        P(None, "tensor"),
        P("tensor", None),
        P(),
        P(),
        P("tensor", None, None),
        P("tensor", None, None),
    )
    out_specs = (
        P(("dp", "tensor"), None),
        P(("dp", "tensor"), None),
        P(),
        P(None, "tensor"),
        P("tensor", None),
        P(),
        P(),
        P("tensor", None, None),
        P("tensor", None, None),
    )
    return jax.shard_map(local, mesh=mesh, in_specs=in_specs, out_specs=out_specs, check_vma=False)
```
